256 devices in a mesh: rows: 64 (over x, z, core), rhs: 4 (over y).
Axes of the slice: x: 4, y: 4, z: 8, core: 2. Of those that a mesh axis runs over, the one named last changes fastest.
Arguments:
- factor: float32 [12288, 12288], P('rows', 'rhs'), may hold values from -0.1 to 0.1
- pattern: int32 [192, 192], P('rows'), may hold values 0 or 1
- owner: int32 [192], P('rows'), may hold values from 0 to 191, each once
- right_side: float32 [64, 12288], P('rhs', 'rows'), may hold values from -6 to 6
Outputs:
- solution: float32 [64, 12288], P('rhs', 'rows')
The draws below stay inside these ranges and needn't reach their ends.
All inputs are finite; a program needn't handle non-finite values. No bound on the sum of `pattern` on one device may be relied on, other than what follows from the above.
Results may differ from the reference program's by a relative error of at most 0.0001.
Values sent between devices are 32-bit elements; how exact they have to be, the bound alone decides.
No kernel may reach another device: no remote copies, remote signals or barrier semaphores. Data moves between devices by JAX's collectives and lax.ppermute only.
A program may use at most 192 MiB of HBM per device.

```python
import jax
import jax.numpy as jnp
from jax import lax

N = 12288
NB = 192
NRHS = 64


def touch_ends(drawn, stream_key, smallest, high):
    index_at = [jax.random.randint(jax.random.fold_in(stream_key, axis), (), 0, length) for axis, length in enumerate(drawn.shape)]
    main_axis = drawn.shape.index(max(drawn.shape))
    beside = index_at[:main_axis] + [(index_at[main_axis] + 1) % drawn.shape[main_axis]] + index_at[main_axis + 1:]
    return drawn.at[tuple(index_at)].set(smallest).at[tuple(beside)].set(high)


def block_levels(key, shape, shards, least, top_value):
    def one(dim, parts):
        draws = jax.random.uniform(jax.random.fold_in(jax.random.fold_in(key, 6), dim), (parts,), jnp.float32, least / len(shards), top_value / len(shards))
        return jnp.repeat(jnp.exp(draws), shape[dim] // parts).reshape((-1,) + (1,) * (len(shape) - dim - 1))

    loudness = one(*shards[0])
    for cut in shards[1:]:
        loudness = loudness * one(*cut)
    return loudness


def normal_values(key, extent, spread, most, shards=(), kind=jnp.bfloat16):
    values = spread * jax.random.normal(key, extent, jnp.float32)
    if shards:
        values = values * block_levels(key, extent, shards, -0.22, 0.18)
    return jnp.clip(values, -most, most).astype(kind)


def setup_inputs(seed: int = 0) -> dict:
    key_list = jax.random.split(jax.random.key(seed), 5)
    factor = normal_values(key_list[0], (N, N), 0.015625, 0.1, ((0, 64), (1, 4)), jnp.float32)
    pattern = touch_ends((jax.random.randint(key_list[1], (NB, NB), 0, 3) < 2).astype(jnp.int32), jax.random.fold_in(key_list[1], 1), 0, 1)
    owner = jax.random.permutation(key_list[2], NB).astype(jnp.int32)
    right_side = normal_values(key_list[3], (NRHS, N), 1.0, 6.0, ((0, 4), (1, 64)), jnp.float32)
    return dict(factor=factor, pattern=pattern, owner=owner, right_side=right_side)


def classify(ids, leaf):
    level = jnp.where(ids < 4 * leaf, 2, jnp.where(ids < 8 * leaf, 1, 0)).astype(jnp.int32)
    group = jnp.where(level == 2, ids // leaf, jnp.where(level == 1, (ids - 4 * leaf) // (2 * leaf), 0)).astype(jnp.int32)
    return level, group


def reference(factor, pattern, owner, right_side):
    total = owner.shape[0]
    width = factor.shape[1]
    block = width // total
    count = right_side.shape[0]
    leaf = total // 12
    slots = jnp.arange(total, dtype=jnp.int32)
    inverse = jnp.zeros((total,), jnp.int32).at[owner].set(slots)
    glob = factor.reshape(total, block, width)[inverse].reshape(width, width)
    patt = pattern[inverse]
    level, group = classify(slots, leaf)
    desc = ((level[:, None] == 1) & (level[None, :] == 2) & (group[None, :] // 2 == group[:, None])) | ((level[:, None] == 0) & (level[None, :] > 0))
    keep = (desc & (patt > 0)).astype(factor.dtype)
    offpart = (glob.reshape(total, block, total, block) * keep[:, None, :, None]).reshape(width, width)
    same = (level[:, None] == level[None, :]) & (group[:, None] == group[None, :])
    same_full = jnp.repeat(jnp.repeat(same, block, 0), block, 1)
    index = jnp.arange(width, dtype=jnp.int32)
    diagpart = jnp.where(same_full & (index[:, None] > index[None, :]), glob, 0.0) + jnp.eye(width, dtype=jnp.float32)
    level_cols = jnp.repeat(level, block)
    rhs = right_side.reshape(count, total, block)[:, inverse].reshape(count, width)
    high = lax.Precision.HIGHEST
    solved = jnp.zeros((count, width), jnp.float32)
    for lvl in (2, 1, 0):
        resid = rhs - lax.dot_general(solved, offpart, (((1,), (1,)), ((), ())), precision=high)
        resid = jnp.where(level_cols[None, :] == lvl, resid, 0.0)
        fresh = lax.dot_general(resid, diagpart, (((1,), (1,)), ((), ())), precision=high)
        solved = jnp.where(level_cols[None, :] == lvl, fresh, solved)
    result = jnp.zeros((count, width), jnp.float32)
    carried = jnp.zeros((count, width), jnp.float32)
    for lvl in (0, 1, 2):
        tvec = jnp.where(level_cols[None, :] == lvl, solved - carried, 0.0)
        fresh = jnp.dot(tvec, diagpart, precision=high)
        result = jnp.where(level_cols[None, :] == lvl, fresh, result)
        if lvl < 2:
            carried = carried + jnp.dot(jnp.where(level_cols[None, :] == lvl, result, 0.0), offpart, precision=high)
    return result.reshape(count, total, block)[:, owner].reshape(count, width)
```

```python
import functools

import jax
import jax.numpy as jnp
from jax import lax
from jax.experimental import pallas as pl
from jax.experimental.pallas import tpu as pltpu
from jax.sharding import Mesh, PartitionSpec as P

BLOCK = 64
RHS = 16
SLOTS = 3
ROWS = SLOTS * BLOCK
THIRD = 4096
PEERS = 32
PLACES = PEERS * SLOTS
VMEM = pl.BlockSpec(memory_space=pltpu.VMEM)
SMEM = pl.BlockSpec(memory_space=pltpu.SMEM)
PARAMS = pltpu.CompilerParams(vmem_limit_bytes=48 * 1024 * 1024)
CHIPS = ("x", "z")


def f32(*shape):
    return jax.ShapeDtypeStruct(shape, jnp.float32)


def classify(ids, leaf):
    level = jnp.where(ids < 4 * leaf, 2, jnp.where(ids < 8 * leaf, 1, 0)).astype(jnp.int32)
    group = jnp.where(
        level == 2, ids // leaf, jnp.where(level == 1, (ids - 4 * leaf) // (2 * leaf), 0)
    )
    return (level, group)


def left_half():
    return lax.broadcasted_iota(jnp.int32, (8, 128), 1) < BLOCK


def pack(rows):
    return [
        jnp.concatenate(
            [rows[:8, s * BLOCK : (s + 1) * BLOCK], rows[8:, s * BLOCK : (s + 1) * BLOCK]], axis=1
        )
        for s in range(SLOTS)
    ]


def unpack(tiles):
    upper = jnp.concatenate([t[:, :BLOCK] for t in tiles], axis=1)
    lower = jnp.concatenate([t[:, BLOCK:] for t in tiles], axis=1)
    return jnp.concatenate([upper, lower], axis=0)


def only(own_ref, level, rows):
    slot = lax.broadcasted_iota(jnp.int32, rows.shape, 1) // BLOCK
    keep = jnp.zeros(rows.shape, jnp.bool_)
    for s in range(SLOTS):
        g = own_ref[s]
        here = (g >= (2 - level) * 64) & (g < (3 - level) * 64)
        keep = keep | ((slot == s) & here)
    return jnp.where(keep, rows, 0.0)


def to_canonical(inv_ref, level, mine_ref, other_ref, x_ref):
    base = (2 - level) * 64
    half = left_half()

    def tile(place):
        far = place >= PLACES
        near_at = jnp.where(far, 0, place)
        far_at = jnp.where(far, place - PLACES, 0)
        chip, slot = near_at // SLOTS, near_at % SLOTS
        chip2, slot2 = far_at // SLOTS, far_at % SLOTS
        return jnp.where(far, other_ref[chip2, slot2], mine_ref[chip, slot])

    for t in range(32):
        a = tile(inv_ref[base + 2 * t])
        b = tile(inv_ref[base + 2 * t + 1])
        ra = pltpu.roll(a, BLOCK, 1)
        rb = pltpu.roll(b, BLOCK, 1)
        x_ref[0:8, 128 * t : 128 * (t + 1)] = jnp.where(half, a, rb)
        x_ref[8:16, 128 * t : 128 * (t + 1)] = jnp.where(half, ra, b)


def to_places(inv_ref, level, x_ref, out_ref):
    base = (2 - level) * 64
    half = left_half()
    out_ref[...] = jnp.zeros_like(out_ref)
    for t in range(32):
        top = x_ref[0:8, 128 * t : 128 * (t + 1)]
        bottom = x_ref[8:16, 128 * t : 128 * (t + 1)]
        out_ref[inv_ref[base + 2 * t]] = jnp.where(half, top, pltpu.roll(bottom, BLOCK, 1))
        out_ref[inv_ref[base + 2 * t + 1]] = jnp.where(half, pltpu.roll(top, BLOCK, 1), bottom)


def times_rows(x, m_ref):
    return lax.dot_general(
        x,
        m_ref[...],
        (((1,), (1,)), ((), ())),
        precision=lax.Precision.HIGHEST,
        preferred_element_type=jnp.float32,
    )


def times_cols(x, m_ref):
    return lax.dot_general(
        x,
        m_ref[...],
        (((1,), (0,)), ((), ())),
        precision=lax.Precision.HIGHEST,
        preferred_element_type=jnp.float32,
    )


def spread(tiles, send_ref):
    for peer in range(PEERS):
        for s in range(SLOTS):
            send_ref[peer, s] = tiles[s]


def arrived(got_ref):
    return unpack([jnp.sum(got_ref[:, s], axis=0) for s in range(SLOTS)])


def start_kernel(own_ref, b_ref, send_ref):
    tiles = pack(b_ref[...])
    lane = lax.broadcasted_iota(jnp.int32, (8, 128), 1)
    names = jnp.zeros((8, 128), jnp.float32)
    for s in range(SLOTS):
        names = jnp.where(lane == s, own_ref[s].astype(jnp.float32), names)
    spread(tiles, send_ref)
    for peer in range(PEERS):
        send_ref[peer, SLOTS] = names


def mask_kernel(own_ref, kind_ref, full_ref, out_ref):
    s = pl.program_id(0)
    col0 = pl.program_id(1) * out_ref.shape[1]
    g = own_ref[s]
    row = g * BLOCK + lax.broadcasted_iota(jnp.int32, out_ref.shape, 0)
    col = col0 + lax.broadcasted_iota(jnp.int32, out_ref.shape, 1)
    kind = kind_ref[0]
    allowed = (kind == 1) | ((kind == 2) & (row > col))
    out_ref[...] = jnp.where(allowed, full_ref[...], 0.0)


def leaves_kernel(own_ref, order_ref, b_ref, mine_ref, other_ref, m_ref, inv_ref, y_ref, send_ref, x_ref):
    def note(p, carry):
        inv_ref[order_ref[p]] = p
        return carry

    lax.fori_loop(0, 2 * PLACES, note, 0)
    to_canonical(inv_ref, 2, mine_ref, other_ref, x_ref)
    y = only(own_ref, 2, times_rows(x_ref[...], m_ref) + b_ref[...])
    y_ref[...] = y
    spread(pack(y), send_ref)


def resid_kernel(level, own_ref, inv_ref, b_ref, old_ref, mine_ref, other_ref, m_ref, upd_ref, r_ref, send_ref, x_ref):
    to_canonical(inv_ref, level + 1, mine_ref, other_ref, x_ref)
    upd = times_rows(x_ref[...], m_ref)
    if level == 0:
        upd = upd + old_ref[...]
    upd_ref[...] = upd
    r = only(own_ref, level, b_ref[...] - upd)
    r_ref[...] = r
    spread(pack(r), send_ref)


def middle_kernel(own_ref, inv_ref, r_ref, mine_ref, other_ref, m_ref, y_ref, send_ref, x_ref):
    to_canonical(inv_ref, 1, mine_ref, other_ref, x_ref)
    y = only(own_ref, 1, times_rows(x_ref[...], m_ref)) + r_ref[...]
    y_ref[...] = y
    spread(pack(y), send_ref)


def top_kernel(own_ref, inv_ref, r_ref, mine_ref, other_ref, m_ref, y_ref, part_ref, x_ref):
    to_canonical(inv_ref, 0, mine_ref, other_ref, x_ref)
    y = only(own_ref, 0, times_rows(x_ref[...], m_ref)) + r_ref[...]
    y_ref[...] = y
    x_ref[...] = times_cols(y, m_ref)
    to_places(inv_ref, 0, x_ref, part_ref)


def add_kernel(level, inv_ref, y_ref, got_ref, m_ref, x_out_ref, part_ref, x_ref):
    x = y_ref[...] + arrived(got_ref)
    x_out_ref[...] = x
    x_ref[...] = times_cols(x, m_ref)
    to_places(inv_ref, level, x_ref, part_ref)


def add_both_kernel(level, inv_ref, y_ref, other_x_ref, got_ref, m_ref, x_out_ref, part_ref, x_ref):
    x = y_ref[...] + arrived(got_ref) + other_x_ref[...]
    x_out_ref[...] = x
    x_ref[...] = times_cols(x, m_ref)
    to_places(inv_ref, level, x_ref, part_ref)


def sub_kernel(level, own_ref, inv_ref, y_ref, got_ref, m_ref, t_ref, part_ref, x_ref):
    t = only(own_ref, level, y_ref[...] - arrived(got_ref))
    t_ref[...] = t
    x_ref[...] = times_cols(t, m_ref)
    to_places(inv_ref, level, x_ref, part_ref)


def last_kernel(t_ref, x_ref, got_ref, out_ref):
    out_ref[...] = t_ref[...] + x_ref[...] + arrived(got_ref)


def swap(x):
    return lax.ppermute(x, "c", [(0, 1), (1, 0)])


def exchange(x):
    return lax.all_to_all(x, CHIPS, 0, 0)


def gather(send):
    mine = exchange(send)
    return mine, swap(mine)


def reduce(part):
    far = swap(part[PLACES:])
    return exchange((part[:PLACES] + far).reshape(PEERS, SLOTS, 8, 128))


def call(kernel, outs, specs, out_specs, scratch=True):
    return pl.pallas_call(
        kernel,
        out_shape=outs,
        in_specs=specs,
        out_specs=out_specs,
        scratch_shapes=[pltpu.VMEM((RHS, THIRD), jnp.float32)] if scratch else [],
        compiler_params=PARAMS,
    )


def shards(factor, pattern, owner, right_side):
    total = pattern.shape[1]
    leaf = total // 12
    width = total * BLOCK
    vec = f32(RHS, ROWS)
    send_shape = f32(PEERS, SLOTS, 8, 128)
    part_shape = f32(2 * PLACES, 8, 128)

    full = lax.all_gather(factor, "y", axis=1, tiled=True)

    send = call(start_kernel, f32(PEERS, SLOTS + 1, 8, 128), [SMEM, VMEM], VMEM, False)(owner, right_side)
    mine, other = gather(send)
    names = jnp.concatenate([mine[:, SLOTS, 0, :SLOTS], other[:, SLOTS, 0, :SLOTS]], axis=0)
    order = names.reshape(-1).astype(jnp.int32)

    level_own, group_own = classify(owner, leaf)
    level_col, group_col = classify(jnp.arange(total, dtype=jnp.int32), leaf)
    desc = (level_own[:, None] == 1) & (level_col[None, :] == 2) & (
        group_col[None, :] // 2 == group_own[:, None]
    ) | (level_own[:, None] == 0) & (level_col[None, :] > 0)
    same = (level_own[:, None] == level_col[None, :]) & (group_own[:, None] == group_col[None, :])
    kind = jnp.where(same, 2, jnp.where(desc & (pattern > 0), 1, 0)).astype(jnp.int32)
    kind = jnp.broadcast_to(kind[:, :, None], (SLOTS, total, BLOCK)).reshape(SLOTS, 1, width)

    def masked(k):
        tile = 2048
        per = THIRD // tile

        def kernel(own_ref, kind_ref, full_ref, out_ref):
            s = pl.program_id(0)
            col0 = k * THIRD + pl.program_id(1) * tile
            row = own_ref[s] * BLOCK + lax.broadcasted_iota(jnp.int32, out_ref.shape, 0)
            col = col0 + lax.broadcasted_iota(jnp.int32, out_ref.shape, 1)
            kinds = kind_ref[0]
            allowed = (kinds == 1) | ((kinds == 2) & (row > col))
            out_ref[...] = jnp.where(allowed, full_ref[...], 0.0)

        return pl.pallas_call(
            kernel,
            grid=(SLOTS, per),
            out_shape=f32(ROWS, THIRD),
            in_specs=[
                SMEM,
                pl.BlockSpec((1, 1, tile), lambda s, j: (s, 0, k * per + j)),
                pl.BlockSpec((BLOCK, tile), lambda s, j: (s, k * per + j)),
            ],
            out_specs=pl.BlockSpec((BLOCK, tile), lambda s, j: (s, j)),
            compiler_params=PARAMS,
        )(owner, kind, full)

    m2, m1, m0 = masked(0), masked(1), masked(2)

    inv, y2, send = call(
        leaves_kernel,
        (jax.ShapeDtypeStruct((total,), jnp.int32), vec, send_shape),
        [SMEM, SMEM, VMEM, VMEM, VMEM, VMEM],
        (SMEM, VMEM, VMEM),
    )(owner, order, right_side, mine, other, m2)
    mine, other = gather(send)
    upd, r1, send = call(
        functools.partial(resid_kernel, 1),
        (vec, vec, send_shape),
        [SMEM, SMEM] + [VMEM] * 5,
        (VMEM, VMEM, VMEM),
    )(owner, inv, right_side, right_side, mine, other, m2)
    mine, other = gather(send)
    y1, send = call(
        middle_kernel, (vec, send_shape), [SMEM, SMEM] + [VMEM] * 4, (VMEM, VMEM)
    )(owner, inv, r1, mine, other, m1)
    mine, other = gather(send)
    upd, r0, send = call(
        functools.partial(resid_kernel, 0),
        (vec, vec, send_shape),
        [SMEM, SMEM] + [VMEM] * 5,
        (VMEM, VMEM, VMEM),
    )(owner, inv, right_side, upd, mine, other, m1)
    mine, other = gather(send)
    y0, part = call(
        top_kernel, (vec, part_shape), [SMEM, SMEM] + [VMEM] * 4, (VMEM, VMEM)
    )(owner, inv, r0, mine, other, m0)

    got = reduce(part)
    x0, part = call(
        functools.partial(add_kernel, 1), (vec, part_shape), [SMEM] + [VMEM] * 3, (VMEM, VMEM)
    )(inv, y0, got, m1)
    got = reduce(part)
    t1, part = call(
        functools.partial(sub_kernel, 1), (vec, part_shape), [SMEM, SMEM] + [VMEM] * 3, (VMEM, VMEM)
    )(owner, inv, y1, got, m1)
    got = reduce(part)
    x01, part = call(
        functools.partial(add_both_kernel, 2), (vec, part_shape), [SMEM] + [VMEM] * 4, (VMEM, VMEM)
    )(inv, t1, x0, got, m2)
    got = reduce(part)
    t2, part = call(
        functools.partial(sub_kernel, 2), (vec, part_shape), [SMEM, SMEM] + [VMEM] * 3, (VMEM, VMEM)
    )(owner, inv, y2, got, m2)
    got = reduce(part)
    return call(last_kernel, vec, [VMEM] * 3, VMEM, False)(t2, x01, got)


def solution(mesh):
    fine = Mesh(mesh.devices.reshape(4, 8, 2, 4), ("x", "z", "c", "y"))
    rows = ("x", "z", "c")
    in_specs = (P(rows, "y"), P(rows, None), P(rows), P("y", rows))
    out_specs = P("y", rows)
    return jax.shard_map(shards, mesh=fine, in_specs=in_specs, out_specs=out_specs, check_vma=False)
```

```python
import functools

import jax
import jax.numpy as jnp
from jax import lax
from jax.experimental import pallas as pl
from jax.experimental.pallas import tpu as pltpu
from jax.sharding import Mesh, PartitionSpec as P

BLOCK = 64
RHS = 16
SLOTS = 3
ROWS = SLOTS * BLOCK
THIRD = 4096
PEERS = 32
PLACES = PEERS * SLOTS
PART = 1024
HALF = 512
VMEM = pl.BlockSpec(memory_space=pltpu.VMEM)
SMEM = pl.BlockSpec(memory_space=pltpu.SMEM)
ANY = pl.BlockSpec(memory_space=pl.ANY)
PARAMS = pltpu.CompilerParams(vmem_limit_bytes=48 * 1024 * 1024)
CHIPS = ("x", "z")


def f32(*shape):
    return jax.ShapeDtypeStruct(shape, jnp.float32)


def classify(ids, leaf):
    level = jnp.where(ids < 4 * leaf, 2, jnp.where(ids < 8 * leaf, 1, 0)).astype(jnp.int32)
    group = jnp.where(
        level == 2, ids // leaf, jnp.where(level == 1, (ids - 4 * leaf) // (2 * leaf), 0)
    )
    return (level, group)


def left_half():
    return lax.broadcasted_iota(jnp.int32, (8, 128), 1) < BLOCK


def pack(rows):
    return [
        jnp.concatenate(
            [rows[:8, s * BLOCK : (s + 1) * BLOCK], rows[8:, s * BLOCK : (s + 1) * BLOCK]], axis=1
        )
        for s in range(SLOTS)
    ]


def unpack(tiles):
    upper = jnp.concatenate([t[:, :BLOCK] for t in tiles], axis=1)
    lower = jnp.concatenate([t[:, BLOCK:] for t in tiles], axis=1)
    return jnp.concatenate([upper, lower], axis=0)


def only(own_ref, level, rows):
    slot = lax.broadcasted_iota(jnp.int32, rows.shape, 1) // BLOCK
    keep = jnp.zeros(rows.shape, jnp.bool_)
    for s in range(SLOTS):
        g = own_ref[s]
        here = (g >= (2 - level) * 64) & (g < (3 - level) * 64)
        keep = keep | ((slot == s) & here)
    return jnp.where(keep, rows, 0.0)


def to_canonical(inv_ref, level, mine_ref, other_ref, x_ref):
    base = (2 - level) * 64
    half = left_half()

    def tile(place):
        far = place >= PLACES
        near_at = jnp.where(far, 0, place)
        far_at = jnp.where(far, place - PLACES, 0)
        chip, slot = near_at // SLOTS, near_at % SLOTS
        chip2, slot2 = far_at // SLOTS, far_at % SLOTS
        return jnp.where(far, other_ref[chip2, slot2], mine_ref[chip, slot])

    for t in range(32):
        a = tile(inv_ref[base + 2 * t])
        b = tile(inv_ref[base + 2 * t + 1])
        ra = pltpu.roll(a, BLOCK, 1)
        rb = pltpu.roll(b, BLOCK, 1)
        x_ref[0:8, 128 * t : 128 * (t + 1)] = jnp.where(half, a, rb)
        x_ref[8:16, 128 * t : 128 * (t + 1)] = jnp.where(half, ra, b)


def to_places(inv_ref, level, x_ref, out_ref):
    base = (2 - level) * 64
    half = left_half()
    out_ref[...] = jnp.zeros_like(out_ref)
    for t in range(32):
        top = x_ref[0:8, 128 * t : 128 * (t + 1)]
        bottom = x_ref[8:16, 128 * t : 128 * (t + 1)]
        out_ref[inv_ref[base + 2 * t]] = jnp.where(half, top, pltpu.roll(bottom, BLOCK, 1))
        out_ref[inv_ref[base + 2 * t + 1]] = jnp.where(half, pltpu.roll(top, BLOCK, 1), bottom)


def times_rows(x, m):
    return lax.dot_general(
        x,
        m,
        (((1,), (1,)), ((), ())),
        precision=lax.Precision.HIGHEST,
        preferred_element_type=jnp.float32,
    )


def times_cols(x, m):
    return lax.dot_general(
        x,
        m,
        (((1,), (0,)), ((), ())),
        precision=lax.Precision.HIGHEST,
        preferred_element_type=jnp.float32,
    )


def spread(tiles, send_ref):
    for peer in range(PEERS):
        for s in range(SLOTS):
            send_ref[peer, s] = tiles[s]


def arrived(got_ref):
    return unpack([jnp.sum(got_ref[:, s], axis=0) for s in range(SLOTS)])


def start_kernel(own_ref, b_ref, send_ref):
    tiles = pack(b_ref[...])
    lane = lax.broadcasted_iota(jnp.int32, (8, 128), 1)
    names = jnp.zeros((8, 128), jnp.float32)
    for s in range(SLOTS):
        names = jnp.where(lane == s, own_ref[s].astype(jnp.float32), names)
    spread(tiles, send_ref)
    for peer in range(PEERS):
        send_ref[peer, SLOTS] = names


def turn(g, q):
    leaf = jnp.where(g // 16 == 3, 0, g // 16)
    first = jnp.where(q == 1, 1, 0)
    second = jnp.where(q == 0, 2, 0)
    return jnp.where(g < 64, leaf, jnp.where(g < 96, first, jnp.where(g < 128, second, 0)))


def part_of(e, g, q):
    return 3 * q + lax.rem(e + turn(g, q), 3)


def rows_of(s):
    return slice(s * BLOCK, (s + 1) * BLOCK)


def split_kernel(own_ref, me_ref, factor_ref, *refs):
    outs, sems = refs[:3], refs[3]
    copies = []
    for e in range(3):
        for s in range(SLOTS):
            at = lax.rem(e + turn(own_ref[s], me_ref[0]), 3) * PART
            for h in range(2):
                copies.append(
                    pltpu.make_async_copy(
                        factor_ref.at[rows_of(s), pl.ds(pl.multiple_of(at + h * HALF, HALF), HALF)],
                        outs[e].at[h, rows_of(s)],
                        sems.at[len(copies)],
                    )
                )
    for copy in copies:
        copy.start()
    for copy in copies:
        copy.wait()


def place_kernel(e, own_ref, me_ref, kind_ref, *refs):
    parts = refs[:4]
    m_ref, buf_ref, sems = refs[-3:]
    copies = []
    for d in range(4):
        q = lax.rem(me_ref[0] + d, 4)
        for s in range(SLOTS):
            g = own_ref[s]
            at = part_of(e, g, q) * PART
            row = g * BLOCK + lax.broadcasted_iota(jnp.int32, (BLOCK, HALF), 0)
            for h in range(2):
                i = len(copies)
                col0 = pl.multiple_of(at + h * HALF, HALF)
                kinds = kind_ref[s, :, pl.ds(col0, HALF)]
                col = col0 + lax.broadcasted_iota(jnp.int32, (BLOCK, HALF), 1)
                allowed = (kinds == 1) | ((kinds == 2) & (row > col))
                buf_ref[i] = jnp.where(allowed, parts[d](h, s), 0.0)
                copies.append(
                    pltpu.make_async_copy(
                        buf_ref.at[i], m_ref.at[rows_of(s), pl.ds(col0, HALF)], sems.at[i]
                    )
                )
                copies[-1].start()
    for copy in copies:
        copy.wait()


def fetch(m_ref, buf_ref, sem, col0):
    copy = pltpu.make_async_copy(m_ref.at[:, col0 : col0 + buf_ref.shape[1]], buf_ref, sem.at[0])
    copy.start()
    return copy


def fetch_own(own_ref, m_ref, buf_ref, sem, base, blocks, groups, col0):
    wide = buf_ref.shape[2]
    copies, starts = [], []
    for s in range(SLOTS):
        group = jnp.clip((own_ref[s] - base) // blocks, 0, groups - 1)
        start = pl.multiple_of(group * wide, wide)
        starts.append(start)
        copies.append(
            pltpu.make_async_copy(
                m_ref.at[rows_of(s), pl.ds(col0 + start, wide)], buf_ref.at[s], sem.at[s]
            )
        )
        copies[-1].start()
    return copies, starts


def own_products(copies, starts, x_ref, buf_ref):
    wide = buf_ref.shape[2]
    outs = []
    for s in range(SLOTS):
        copies[s].wait()
        outs.append(times_rows(x_ref[:, pl.ds(starts[s], wide)], buf_ref[s]))
    return jnp.concatenate(outs, axis=1)


def leaves_kernel(own_ref, order_ref, b_ref, mine_ref, other_ref, m_ref, inv_ref, y_ref, send_ref, x_ref, buf_ref, sem):
    copies, starts = fetch_own(own_ref, m_ref, buf_ref, sem, 0, 16, 4, 0)

    def note(p, carry):
        inv_ref[order_ref[p]] = p
        return carry

    lax.fori_loop(0, 2 * PLACES, note, 0)
    to_canonical(inv_ref, 2, mine_ref, other_ref, x_ref)
    y = only(own_ref, 2, own_products(copies, starts, x_ref, buf_ref) + b_ref[...])
    y_ref[...] = y
    spread(pack(y), send_ref)


def middle_resid_kernel(own_ref, inv_ref, b_ref, mine_ref, other_ref, m_ref, r_ref, send_ref, x_ref, buf_ref, sem):
    copies, starts = fetch_own(own_ref, m_ref, buf_ref, sem, 64, 32, 2, 0)
    to_canonical(inv_ref, 2, mine_ref, other_ref, x_ref)
    r = only(own_ref, 1, b_ref[...] - own_products(copies, starts, x_ref, buf_ref))
    r_ref[...] = r
    spread(pack(r), send_ref)


def middle_kernel(own_ref, inv_ref, r_ref, mine_ref, other_ref, m_ref, y_ref, send_ref, x_ref, buf_ref, sem):
    copies, starts = fetch_own(own_ref, m_ref, buf_ref, sem, 64, 32, 2, THIRD)
    to_canonical(inv_ref, 1, mine_ref, other_ref, x_ref)
    y = only(own_ref, 1, own_products(copies, starts, x_ref, buf_ref) + r_ref[...])
    y_ref[...] = y
    spread(pack(y), send_ref)


def top_resid_kernel(own_ref, inv_ref, b_ref, mine2_ref, other2_ref, mine_ref, other_ref, m_ref, r_ref, send_ref, x_ref, buf_ref, sem):
    copy = fetch(m_ref, buf_ref, sem, 0)
    to_canonical(inv_ref, 2, mine2_ref, other2_ref, x_ref.at[:, :THIRD])
    to_canonical(inv_ref, 1, mine_ref, other_ref, x_ref.at[:, THIRD:])
    copy.wait()
    r = only(own_ref, 0, b_ref[...] - times_rows(x_ref[...], buf_ref[...]))
    r_ref[...] = r
    spread(pack(r), send_ref)


def top_kernel(own_ref, inv_ref, r_ref, mine_ref, other_ref, m_ref, y_ref, part_ref, x_ref, buf_ref, sem):
    copy = fetch(m_ref, buf_ref, sem, 2 * THIRD)
    to_canonical(inv_ref, 0, mine_ref, other_ref, x_ref)
    copy.wait()
    y = only(own_ref, 0, times_rows(x_ref[...], buf_ref[...])) + r_ref[...]
    y_ref[...] = y
    x_ref[...] = times_cols(y, buf_ref[...])
    to_places(inv_ref, 0, x_ref, part_ref)


def add_kernel(level, inv_ref, *refs):
    terms = refs[:-7]
    got_ref, m_ref, x_out_ref, part_ref, x_ref, buf_ref, sem = refs[-7:]
    copy = fetch(m_ref, buf_ref, sem, (2 - level) * THIRD)
    x = arrived(got_ref)
    for term in terms:
        x = x + term[...]
    x_out_ref[...] = x
    copy.wait()
    x_ref[...] = times_cols(x, buf_ref[...])
    to_places(inv_ref, level, x_ref, part_ref)


def sub_kernel(level, own_ref, inv_ref, y_ref, got_ref, m_ref, t_ref, part_ref, x_ref, buf_ref, sem):
    copy = fetch(m_ref, buf_ref, sem, (2 - level) * THIRD)
    t = only(own_ref, level, y_ref[...] - arrived(got_ref))
    t_ref[...] = t
    copy.wait()
    x_ref[...] = times_cols(t, buf_ref[...])
    to_places(inv_ref, level, x_ref, part_ref)


def last_kernel(t_ref, x_ref, got_ref, out_ref):
    out_ref[...] = t_ref[...] + x_ref[...] + arrived(got_ref)


def swap(x):
    return lax.ppermute(x, "c", [(0, 1), (1, 0)])


def exchange(x):
    return lax.all_to_all(x, CHIPS, 0, 0)


def gather(send):
    mine = exchange(send)
    return mine, swap(mine)


def reduce(part):
    far = swap(part[PLACES:])
    return exchange((part[:PLACES] + far).reshape(PEERS, SLOTS, 8, 128))


def around(x, step):
    return lax.ppermute(x, "y", [(i, (i + step) % 4) for i in range(4)])


def over_planes(part):
    before, after = around(part, 1), around(part, -1)
    opposite = [around(before[0], 1), around(after[1], -1)]
    return part, after, opposite, before


def call(kernel, outs, specs, out_specs, scratch=()):
    return pl.pallas_call(
        kernel,
        out_shape=outs,
        in_specs=specs,
        out_specs=out_specs,
        scratch_shapes=list(scratch),
        compiler_params=PARAMS,
    )


def room(columns, *buffer):
    return (
        pltpu.VMEM((RHS, columns), jnp.float32),
        pltpu.VMEM(buffer, jnp.float32),
        pltpu.SemaphoreType.DMA((SLOTS,)),
    )


def shards(factor, pattern, owner, right_side):
    total = pattern.shape[1]
    leaf = total // 12
    width = total * BLOCK
    vec = f32(RHS, ROWS)
    send_shape = f32(PEERS, SLOTS, 8, 128)
    part_shape = f32(2 * PLACES, 8, 128)
    me = lax.axis_index("y").astype(jnp.int32).reshape(1)

    piece = f32(2, ROWS, HALF)
    pieces = call(
        split_kernel, (piece,) * 3, [SMEM, SMEM, ANY], (ANY,) * 3, [pltpu.SemaphoreType.DMA((18,))]
    )(owner, me, factor)

    send = call(start_kernel, f32(PEERS, SLOTS + 1, 8, 128), [SMEM, VMEM], VMEM)(owner, right_side)

    level_own, group_own = classify(owner, leaf)
    level_col, group_col = classify(jnp.arange(total, dtype=jnp.int32), leaf)
    desc = (level_own[:, None] == 1) & (level_col[None, :] == 2) & (
        group_col[None, :] // 2 == group_own[:, None]
    ) | (level_own[:, None] == 0) & (level_col[None, :] > 0)
    same = (level_own[:, None] == level_col[None, :]) & (group_own[:, None] == group_col[None, :])
    kind = jnp.where(same, 2, jnp.where(desc & (pattern > 0), 1, 0)).astype(jnp.int32)
    kind = jnp.broadcast_to(kind[:, :, None], (SLOTS, total, BLOCK)).reshape(SLOTS, 1, width)

    def place(e, parts, old=None):
        own, after, opposite, before = parts
        given = [own, after, *opposite, before]
        olds = [] if old is None else [old]

        def kernel(own_ref, me_ref, kind_ref, *refs):
            first, second, third_a, third_b, fourth = refs[:5]
            whole = [
                lambda h, s: first[h, rows_of(s)],
                lambda h, s: second[h, rows_of(s)],
                lambda h, s: (third_a, third_b)[h][rows_of(s)],
                lambda h, s: fourth[h, rows_of(s)],
            ]
            place_kernel(e, own_ref, me_ref, kind_ref, *whole, *refs[-3:])

        return pl.pallas_call(
            kernel,
            out_shape=f32(ROWS, width),
            in_specs=[SMEM, SMEM, VMEM] + [VMEM] * 5 + [ANY] * len(olds),
            out_specs=ANY,
            input_output_aliases={8: 0} if olds else {},
            scratch_shapes=[pltpu.VMEM((24, BLOCK, HALF), jnp.float32), pltpu.SemaphoreType.DMA((24,))],
            compiler_params=PARAMS,
        )(owner, me, kind, *given, *olds)

    first = over_planes(pieces[0])
    mine, other = gather(send)
    names = jnp.concatenate([mine[:, SLOTS, 0, :SLOTS], other[:, SLOTS, 0, :SLOTS]], axis=0)
    order = names.reshape(-1).astype(jnp.int32)
    m = place(0, first)
    second = over_planes(pieces[1])

    inv, y2, send = call(
        leaves_kernel,
        (jax.ShapeDtypeStruct((total,), jnp.int32), vec, send_shape),
        [SMEM, SMEM] + [VMEM] * 3 + [ANY],
        (SMEM, VMEM, VMEM),
        room(THIRD, SLOTS, BLOCK, 1024),
    )(owner, order, right_side, mine, other, m)
    m, y2 = lax.optimization_barrier((m, y2))
    mine2, other2 = gather(send)
    m = place(1, second, m)
    third = over_planes(pieces[2])
    r1, send = call(
        middle_resid_kernel,
        (vec, send_shape),
        [SMEM, SMEM] + [VMEM] * 3 + [ANY],
        (VMEM, VMEM),
        room(THIRD, SLOTS, BLOCK, 2048),
    )(owner, inv, right_side, mine2, other2, m)
    mine, other = gather(send)
    y1, send = call(
        middle_kernel,
        (vec, send_shape),
        [SMEM, SMEM] + [VMEM] * 3 + [ANY],
        (VMEM, VMEM),
        room(THIRD, SLOTS, BLOCK, 2048),
    )(owner, inv, r1, mine, other, m)
    m, y1 = lax.optimization_barrier((m, y1))
    mine, other = gather(send)
    m = place(2, third, m)
    r0, send = call(
        top_resid_kernel,
        (vec, send_shape),
        [SMEM, SMEM] + [VMEM] * 5 + [ANY],
        (VMEM, VMEM),
        room(2 * THIRD, ROWS, 2 * THIRD),
    )(owner, inv, right_side, mine2, other2, mine, other, m)
    mine, other = gather(send)
    y0, part = call(
        top_kernel,
        (vec, part_shape),
        [SMEM, SMEM] + [VMEM] * 3 + [ANY],
        (VMEM, VMEM),
        room(THIRD, ROWS, THIRD),
    )(owner, inv, r0, mine, other, m)

    def adds(level, *terms):
        return call(
            functools.partial(add_kernel, level),
            (vec, part_shape),
            [SMEM] + [VMEM] * len(terms) + [ANY],
            (VMEM, VMEM),
            room(THIRD, ROWS, THIRD),
        )(inv, *terms, m)

    def subs(level, y, got):
        return call(
            functools.partial(sub_kernel, level),
            (vec, part_shape),
            [SMEM, SMEM, VMEM, VMEM, ANY],
            (VMEM, VMEM),
            room(THIRD, ROWS, THIRD),
        )(owner, inv, y, got, m)

    x0, part = adds(1, y0, reduce(part))
    t1, part = subs(1, y1, reduce(part))
    x01, part = adds(2, t1, x0, reduce(part))
    t2, part = subs(2, y2, reduce(part))
    return call(last_kernel, vec, [VMEM] * 3, VMEM)(t2, x01, reduce(part))


def solution(mesh):
    fine = Mesh(mesh.devices.reshape(4, 8, 2, 4), ("x", "z", "c", "y"))
    rows = ("x", "z", "c")
    in_specs = (P(rows, "y"), P(rows, None), P(rows), P("y", rows))
    out_specs = P("y", rows)
    return jax.shard_map(shards, mesh=fine, in_specs=in_specs, out_specs=out_specs, check_vma=False)
```

```python
import functools

import jax
import jax.numpy as jnp
from jax import lax
from jax.experimental import pallas as pl
from jax.experimental.pallas import tpu as pltpu
from jax.sharding import Mesh, PartitionSpec as P

BLOCK = 64
RHS = 16
SLOTS = 3
ROWS = SLOTS * BLOCK
THIRD = 4096
PEERS = 32
PLACES = PEERS * SLOTS
PART = 1024
HALF = 512
VMEM = pl.BlockSpec(memory_space=pltpu.VMEM)
SMEM = pl.BlockSpec(memory_space=pltpu.SMEM)
ANY = pl.BlockSpec(memory_space=pl.ANY)
CHIPS = ("x", "z")


def f32(*shape):
    return jax.ShapeDtypeStruct(shape, jnp.float32)


def classify(ids, leaf):
    level = jnp.where(ids < 4 * leaf, 2, jnp.where(ids < 8 * leaf, 1, 0)).astype(jnp.int32)
    group = jnp.where(
        level == 2, ids // leaf, jnp.where(level == 1, (ids - 4 * leaf) // (2 * leaf), 0)
    )
    return (level, group)


def left_half():
    return lax.broadcasted_iota(jnp.int32, (8, 128), 1) < BLOCK


def pack(rows):
    return [
        jnp.concatenate(
            [rows[:8, s * BLOCK : (s + 1) * BLOCK], rows[8:, s * BLOCK : (s + 1) * BLOCK]], axis=1
        )
        for s in range(SLOTS)
    ]


def unpack(tiles):
    upper = jnp.concatenate([t[:, :BLOCK] for t in tiles], axis=1)
    lower = jnp.concatenate([t[:, BLOCK:] for t in tiles], axis=1)
    return jnp.concatenate([upper, lower], axis=0)


def only(own_ref, level, rows):
    slot = lax.broadcasted_iota(jnp.int32, rows.shape, 1) // BLOCK
    keep = jnp.zeros(rows.shape, jnp.bool_)
    for s in range(SLOTS):
        g = own_ref[s]
        here = (g >= (2 - level) * 64) & (g < (3 - level) * 64)
        keep = keep | ((slot == s) & here)
    return jnp.where(keep, rows, 0.0)


def halves(x):
    high = x.astype(jnp.bfloat16)
    return high, (x - high.astype(jnp.float32)).astype(jnp.bfloat16)


def to_canonical(inv_ref, level, mine_ref, other_ref, x_ref):
    base = (2 - level) * 64
    half = left_half()

    def tile(place):
        near = jnp.minimum(place, PLACES - 1)
        far = jnp.maximum(place, PLACES) - PLACES
        return jnp.where(place >= PLACES, other_ref[far], mine_ref[near])

    for t in range(32):
        a = tile(inv_ref[base + 2 * t])
        b = tile(inv_ref[base + 2 * t + 1])
        top = jnp.where(half, a, pltpu.roll(b, BLOCK, 1))
        bottom = jnp.where(half, pltpu.roll(a, BLOCK, 1), b)
        high, low = halves(jnp.concatenate([top, bottom], axis=0))
        x_ref[0:16, 128 * t : 128 * (t + 1)] = high
        x_ref[16:32, 128 * t : 128 * (t + 1)] = low


def to_places(inv_ref, level, x, out_ref):
    base = (2 - level) * 64
    half = left_half()
    out_ref[...] = jnp.zeros_like(out_ref)
    for t in range(32):
        top = x[0:8, 128 * t : 128 * (t + 1)]
        bottom = x[8:16, 128 * t : 128 * (t + 1)]
        out_ref[inv_ref[base + 2 * t]] = jnp.where(half, top, pltpu.roll(bottom, BLOCK, 1))
        out_ref[inv_ref[base + 2 * t + 1]] = jnp.where(half, pltpu.roll(top, BLOCK, 1), bottom)


def times_rows(x, high, low):
    dims = (((1,), (1,)), ((), ()))
    one = lax.dot_general(high, x, dims, preferred_element_type=jnp.float32)
    two = lax.dot_general(low, x[:RHS], dims, preferred_element_type=jnp.float32)
    return one[:, :RHS] + one[:, RHS:] + two


def times_cols(x, high, low):
    dims = (((1,), (0,)), ((), ()))
    x_high, x_low = halves(x)
    both = jnp.concatenate([x_high, x_low], axis=0)
    one = lax.dot_general(both, high, dims, preferred_element_type=jnp.float32)
    two = lax.dot_general(x_high, low, dims, preferred_element_type=jnp.float32)
    return one[:RHS] + one[RHS:] + two


def spread(tiles, send_ref):
    for peer in range(PEERS):
        for s in range(SLOTS):
            send_ref[peer, s] = tiles[s]


def arrived(got_ref):
    return unpack([jnp.sum(got_ref[:, s], axis=0) for s in range(SLOTS)])


def start_kernel(own_ref, b_ref, after_ref, send_ref):
    tiles = pack(b_ref[...])
    lane = lax.broadcasted_iota(jnp.int32, (8, 128), 1)
    names = jnp.zeros((8, 128), jnp.float32)
    for s in range(SLOTS):
        names = jnp.where(lane == s, own_ref[s].astype(jnp.float32), names)
    spread(tiles, send_ref)
    for peer in range(PEERS):
        send_ref[peer, SLOTS] = names


def turn(g, q):
    leaf = jnp.where(g // 16 == 3, 0, g // 16)
    first = jnp.where(q == 1, 1, 0)
    second = jnp.where(q == 0, 2, 0)
    return jnp.where(g < 64, leaf, jnp.where(g < 96, first, jnp.where(g < 128, second, 0)))


def part_of(e, g, q):
    return 3 * q + lax.rem(e + turn(g, q), 3)


def rows_of(s):
    return slice(s * BLOCK, (s + 1) * BLOCK)


def split_kernel(own_ref, me_ref, factor_ref, *refs):
    outs, sems = refs[:3], refs[3]
    copies = []
    for e in range(3):
        for s in range(SLOTS):
            at = lax.rem(e + turn(own_ref[s], me_ref[0]), 3) * PART
            for h in range(2):
                copies.append(
                    pltpu.make_async_copy(
                        factor_ref.at[rows_of(s), pl.ds(pl.multiple_of(at + h * HALF, HALF), HALF)],
                        outs[e].at[h, rows_of(s)],
                        sems.at[len(copies)],
                    )
                )
    for copy in copies:
        copy.start()
    for copy in copies:
        copy.wait()


def sources(e, own_ref, me_ref, thr_ref, refs):
    first, second, third_a, third_b, fourth = refs
    for d in range(4):
        q = lax.rem(me_ref[0] + d, 4)
        for s in range(SLOTS):
            g = own_ref[s]
            part = part_of(e, g, q)
            row = g * BLOCK + lax.broadcasted_iota(jnp.int32, (BLOCK, HALF), 0)
            for h in range(2):

                def value(d=d, s=s, h=h, part=part, row=row):
                    given = (first, second, (third_a, third_b)[h], fourth)[d]
                    block = given[rows_of(s)] if d == 2 else given[h, rows_of(s)]
                    col0 = pl.multiple_of(part * PART + h * HALF, HALF)
                    return halves(jnp.where(row > thr_ref[s, :, pl.ds(col0, HALF)], block, 0.0))

                yield s, h, g, part, value


def put(refs, s, at, pair):
    for ref, value in zip(refs, pair):
        ref[rows_of(s), pl.ds(pl.multiple_of(at, HALF), HALF)] = value


def place_leaves_kernel(own_ref, me_ref, thr_ref, *refs):
    for s, h, g, part, value in sources(0, own_ref, me_ref, thr_ref, refs[:5]):

        @pl.when((g < 64) & (part == g // 16))
        def _(s=s, h=h, value=value):
            put(refs[5:7], s, h * HALF, value())


def place_middles_kernel(own_ref, me_ref, thr_ref, *refs):
    for e in range(2):
        for s, h, g, part, value in sources(e, own_ref, me_ref, thr_ref, refs[5 * e : 5 * e + 5]):
            middle = (g >= 64) & (g < 128)
            first = 2 * ((g - 64) // 32)

            @pl.when(middle & ((part == first) | (part == first + 1)))
            def _(s=s, h=h, value=value, part=part, first=first):
                put(refs[10:12], s, (part - first) * PART + h * HALF, value())

            @pl.when(middle & ((part == first + 4) | (part == first + 5)))
            def _(s=s, h=h, value=value, part=part, first=first):
                put(refs[12:14], s, (part - first - 4) * PART + h * HALF, value())


def place_all_kernel(own_ref, me_ref, thr_ref, *refs):
    for e in range(3):
        for s, h, g, part, value in sources(e, own_ref, me_ref, thr_ref, refs[5 * e : 5 * e + 5]):
            at = lax.rem(part, 4) * PART + h * HALF
            put([ref.at[part // 4] for ref in refs[15:17]], s, at, value())


def own_products(own_ref, base, blocks, groups, x_ref, high_ref, low_ref):
    wide = high_ref.shape[1]
    outs = []
    for s in range(SLOTS):
        group = jnp.clip((own_ref[s] - base) // blocks, 0, groups - 1)
        x = x_ref[:, pl.ds(pl.multiple_of(group * wide, wide), wide)]
        outs.append(times_rows(x, high_ref[rows_of(s)], low_ref[rows_of(s)]))
    return jnp.concatenate(outs, axis=0).T


def leaves_kernel(own_ref, order_ref, b_ref, mine_ref, other_ref, high_ref, low_ref, inv_ref, y_ref, send_ref, x_ref):
    for p in range(2 * PLACES):
        inv_ref[order_ref[p]] = p
    to_canonical(inv_ref, 2, mine_ref, other_ref, x_ref)
    y = only(own_ref, 2, own_products(own_ref, 0, 16, 4, x_ref, high_ref, low_ref) + b_ref[...])
    y_ref[...] = y
    spread(pack(y), send_ref)


def middle_resid_kernel(own_ref, inv_ref, b_ref, mine_ref, other_ref, high_ref, low_ref, r_ref, send_ref, x_ref):
    to_canonical(inv_ref, 2, mine_ref, other_ref, x_ref)
    r = only(own_ref, 1, b_ref[...] - own_products(own_ref, 64, 32, 2, x_ref, high_ref, low_ref))
    r_ref[...] = r
    spread(pack(r), send_ref)


def middle_kernel(own_ref, inv_ref, r_ref, mine_ref, other_ref, high_ref, low_ref, y_ref, send_ref, x_ref):
    to_canonical(inv_ref, 1, mine_ref, other_ref, x_ref)
    y = only(own_ref, 1, own_products(own_ref, 64, 32, 2, x_ref, high_ref, low_ref) + r_ref[...])
    y_ref[...] = y
    spread(pack(y), send_ref)


def update_kernel(inv_ref, mine_ref, other_ref, high_ref, low_ref, upd_ref, x_ref):
    to_canonical(inv_ref, 2, mine_ref, other_ref, x_ref)
    upd_ref[...] = times_rows(x_ref[...], high_ref[0], low_ref[0])


def top_resid_kernel(own_ref, inv_ref, b_ref, upd_ref, mine_ref, other_ref, high_ref, low_ref, r_ref, send_ref, x_ref):
    to_canonical(inv_ref, 1, mine_ref, other_ref, x_ref)
    upd = upd_ref[...] + times_rows(x_ref[...], high_ref[1], low_ref[1])
    r = only(own_ref, 0, b_ref[...] - upd.T)
    r_ref[...] = r
    spread(pack(r), send_ref)


def top_kernel(own_ref, inv_ref, r_ref, mine_ref, other_ref, high_ref, low_ref, y_ref, part_ref, x_ref):
    to_canonical(inv_ref, 0, mine_ref, other_ref, x_ref)
    y = only(own_ref, 0, times_rows(x_ref[...], high_ref[2], low_ref[2]).T) + r_ref[...]
    y_ref[...] = y
    to_places(inv_ref, 0, times_cols(y, high_ref[2], low_ref[2]), part_ref)


def add_kernel(level, inv_ref, *refs):
    terms = refs[:-5]
    got_ref, high_ref, low_ref, x_out_ref, part_ref = refs[-5:]
    x = arrived(got_ref)
    for term in terms:
        x = x + term[...]
    x_out_ref[...] = x
    to_places(inv_ref, level, times_cols(x, high_ref[2 - level], low_ref[2 - level]), part_ref)


def sub_kernel(level, own_ref, inv_ref, y_ref, got_ref, high_ref, low_ref, t_ref, part_ref):
    t = only(own_ref, level, y_ref[...] - arrived(got_ref))
    t_ref[...] = t
    to_places(inv_ref, level, times_cols(t, high_ref[2 - level], low_ref[2 - level]), part_ref)


def last_kernel(t_ref, x_ref, got_ref, out_ref):
    out_ref[...] = t_ref[...] + x_ref[...] + arrived(got_ref)


def swap(x):
    return lax.ppermute(x, "c", [(0, 1), (1, 0)])


def exchange(x):
    return lax.all_to_all(x, CHIPS, 0, 0)


def gather(send):
    mine = exchange(send)
    other = swap(mine)
    return mine[:, :SLOTS].reshape(PLACES, 8, 128), other[:, :SLOTS].reshape(PLACES, 8, 128)


def reduce(part):
    far = swap(part[PLACES:])
    return exchange((part[:PLACES] + far).reshape(PEERS, SLOTS, 8, 128))


def around(x, step):
    return lax.ppermute(x, "y", [(i, (i + step) % 4) for i in range(4)])


def over_planes(part):
    before, after = around(part, 1), around(part, -1)
    opposite = [around(before[0], 1), around(after[1], -1)]
    return part, after, opposite, before


def call(kernel, outs, specs, out_specs, scratch=(), work=0):
    return pl.pallas_call(
        kernel,
        out_shape=outs,
        in_specs=specs,
        out_specs=out_specs,
        scratch_shapes=list(scratch),
        compiler_params=pltpu.CompilerParams(vmem_limit_bytes=28 * 1024 * 1024),
        cost_estimate=pl.CostEstimate(flops=0, bytes_accessed=work, transcendentals=0) if work else None,
    )


def shards(factor, pattern, owner, right_side):
    total = pattern.shape[1]
    leaf = total // 12
    width = total * BLOCK
    vec = f32(RHS, ROWS)
    send_shape = f32(PEERS, SLOTS, 8, 128)
    part_shape = f32(2 * PLACES, 8, 128)
    me = lax.axis_index("y").astype(jnp.int32).reshape(1)
    canonical = [pltpu.VMEM((2 * RHS, THIRD), jnp.bfloat16)]

    def pair(*shape):
        return (jax.ShapeDtypeStruct(shape, jnp.bfloat16),) * 2

    pieces = call(
        split_kernel,
        (f32(2, ROWS, HALF),) * 3,
        [SMEM, SMEM, ANY],
        (ANY,) * 3,
        [pltpu.SemaphoreType.DMA((18,))],
    )(owner, me, factor)

    first = over_planes(pieces[0])
    late = swap(pieces[0][0, :8, :128])
    send = call(
        start_kernel, f32(PEERS, SLOTS + 1, 8, 128), [SMEM, VMEM, VMEM], VMEM
    )(owner, right_side, late)

    level_own, group_own = classify(owner, leaf)
    level_col, group_col = classify(jnp.arange(total, dtype=jnp.int32), leaf)
    desc = (level_own[:, None] == 1) & (level_col[None, :] == 2) & (
        group_col[None, :] // 2 == group_own[:, None]
    ) | (level_own[:, None] == 0) & (level_col[None, :] > 0)
    same = (level_own[:, None] == level_col[None, :]) & (group_own[:, None] == group_col[None, :])
    kind = jnp.where(same, 2, jnp.where(desc & (pattern > 0), 1, 0)).astype(jnp.int32)
    kind = jnp.broadcast_to(kind[:, :, None], (SLOTS, total, BLOCK)).reshape(SLOTS, 1, width)
    cols = jnp.arange(width, dtype=jnp.int32)[None, None, :]
    thr = jnp.where(kind == 2, cols, jnp.where(kind == 1, -1, width))

    mine = exchange(send)
    other = swap(mine)
    names = jnp.concatenate([mine[:, SLOTS, 0, :SLOTS], other[:, SLOTS, 0, :SLOTS]], axis=0)
    order = names.reshape(-1).astype(jnp.int32)
    mine, other = (v[:, :SLOTS].reshape(PLACES, 8, 128) for v in (mine, other))

    def place(kernel, outs, parts, work):
        given = [v for own, after, opposite, before in parts for v in (own, after, *opposite, before)]
        return call(
            kernel, outs, [SMEM, SMEM] + [VMEM] * (1 + len(given)), (VMEM,) * len(outs), work=work
        )(owner, me, thr, *given)

    d2 = place(place_leaves_kernel, pair(ROWS, 1024), [first], 2 << 20)
    piece, _ = lax.optimization_barrier((pieces[1], first))
    second = over_planes(piece)

    inv, y2, send = call(
        leaves_kernel,
        (jax.ShapeDtypeStruct((total,), jnp.int32), vec, send_shape),
        [SMEM, SMEM] + [VMEM] * 5,
        (SMEM, VMEM, VMEM),
        canonical,
    )(owner, order, right_side, mine, other, *d2)
    mine2, other2 = gather(send)
    middles = place(place_middles_kernel, pair(ROWS, 2048) * 2, [first, second], 8 << 20)
    piece, _ = lax.optimization_barrier((pieces[2], second))
    third = over_planes(piece)
    r1, send = call(
        middle_resid_kernel, (vec, send_shape), [SMEM, SMEM] + [VMEM] * 5, (VMEM, VMEM), canonical
    )(owner, inv, right_side, mine2, other2, *middles[:2])
    mine, other = gather(send)
    y1, send = call(
        middle_kernel, (vec, send_shape), [SMEM, SMEM] + [VMEM] * 5, (VMEM, VMEM), canonical
    )(owner, inv, r1, mine, other, *middles[2:])
    mine, other = gather(send)
    m = place(place_all_kernel, pair(3, ROWS, THIRD), [first, second, third], 24 << 20)
    upd = call(
        update_kernel, f32(ROWS, RHS), [SMEM] + [VMEM] * 4, VMEM, canonical, 4 << 20
    )(inv, mine2, other2, *m)
    r0, send = call(
        top_resid_kernel, (vec, send_shape), [SMEM, SMEM] + [VMEM] * 6, (VMEM, VMEM), canonical
    )(owner, inv, right_side, upd, mine, other, *m)
    mine, other = gather(send)
    y0, part = call(
        top_kernel, (vec, part_shape), [SMEM, SMEM] + [VMEM] * 5, (VMEM, VMEM), canonical
    )(owner, inv, r0, mine, other, *m)

    def adds(level, *terms):
        return call(
            functools.partial(add_kernel, level),
            (vec, part_shape),
            [SMEM] + [VMEM] * (len(terms) + 2),
            (VMEM, VMEM),
        )(inv, *terms, *m)

    def subs(level, y, got):
        return call(
            functools.partial(sub_kernel, level),
            (vec, part_shape),
            [SMEM, SMEM] + [VMEM] * 4,
            (VMEM, VMEM),
        )(owner, inv, y, got, *m)

    x0, part = adds(1, y0, reduce(part))
    t1, part = subs(1, y1, reduce(part))
    x01, part = adds(2, t1, x0, reduce(part))
    t2, part = subs(2, y2, reduce(part))
    return call(last_kernel, vec, [VMEM] * 3, VMEM)(t2, x01, reduce(part))


def solution(mesh):
    fine = Mesh(mesh.devices.reshape(4, 8, 2, 4), ("x", "z", "c", "y"))
    rows = ("x", "z", "c")
    in_specs = (P(rows, "y"), P(rows, None), P(rows), P("y", rows))
    out_specs = P("y", rows)
    return jax.shard_map(shards, mesh=fine, in_specs=in_specs, out_specs=out_specs, check_vma=False)
```

```python
import functools

import jax
import jax.numpy as jnp
from jax import lax
from jax.experimental import pallas as pl
from jax.experimental.pallas import tpu as pltpu
from jax.sharding import Mesh, PartitionSpec as P

BLOCK = 64
RHS = 16
SLOTS = 3
ROWS = SLOTS * BLOCK
THIRD = 4096
PEERS = 32
PLACES = PEERS * SLOTS
PART = 1024
HALF = 512
VMEM = pl.BlockSpec(memory_space=pltpu.VMEM)
SMEM = pl.BlockSpec(memory_space=pltpu.SMEM)
HBM = pl.BlockSpec(memory_space=pltpu.HBM)
CHIPS = ("x", "z")


def f32(*shape):
    return jax.ShapeDtypeStruct(shape, jnp.float32)


def left_half():
    return lax.broadcasted_iota(jnp.int32, (8, 128), 1) < BLOCK


def pack(rows):
    return [
        jnp.concatenate(
            [rows[:8, s * BLOCK : (s + 1) * BLOCK], rows[8:, s * BLOCK : (s + 1) * BLOCK]], axis=1
        )
        for s in range(SLOTS)
    ]


def unpack(tiles):
    upper = jnp.concatenate([t[:, :BLOCK] for t in tiles], axis=1)
    lower = jnp.concatenate([t[:, BLOCK:] for t in tiles], axis=1)
    return jnp.concatenate([upper, lower], axis=0)


def only(own_ref, level, rows):
    slot = lax.broadcasted_iota(jnp.int32, rows.shape, 1) // BLOCK
    keep = jnp.zeros(rows.shape, jnp.bool_)
    for s in range(SLOTS):
        g = own_ref[s]
        here = (g >= (2 - level) * 64) & (g < (3 - level) * 64)
        keep = keep | ((slot == s) & here)
    return jnp.where(keep, rows, 0.0)


def halves(x):
    high = x.astype(jnp.bfloat16)
    return high, (x - high.astype(jnp.float32)).astype(jnp.bfloat16)


def to_canonical(inv_ref, level, mine_ref, other_ref, x_ref, extra=False):
    base = (2 - level) * 64
    half = left_half()

    def tile(place):
        near = jnp.minimum(place, PLACES - 1)
        far = jnp.maximum(place, PLACES) - PLACES
        if extra:
            near, far = near + near // SLOTS, far + far // SLOTS
        return jnp.where(place >= PLACES, other_ref[far], mine_ref[near])

    for t in range(32):
        a = tile(inv_ref[base + 2 * t])
        b = tile(inv_ref[base + 2 * t + 1])
        top = jnp.where(half, a, pltpu.roll(b, BLOCK, 1))
        bottom = jnp.where(half, pltpu.roll(a, BLOCK, 1), b)
        high, low = halves(jnp.concatenate([top, bottom], axis=0))
        x_ref[0:16, 128 * t : 128 * (t + 1)] = high
        x_ref[16:32, 128 * t : 128 * (t + 1)] = low


def to_places(inv_ref, level, x, out_ref):
    base = (2 - level) * 64
    half = left_half()
    out_ref[...] = jnp.zeros_like(out_ref)
    for t in range(32):
        top = x[0:8, 128 * t : 128 * (t + 1)]
        bottom = x[8:16, 128 * t : 128 * (t + 1)]
        out_ref[inv_ref[base + 2 * t]] = jnp.where(half, top, pltpu.roll(bottom, BLOCK, 1))
        out_ref[inv_ref[base + 2 * t + 1]] = jnp.where(half, pltpu.roll(top, BLOCK, 1), bottom)


def times_rows(x, high, low):
    dims = (((1,), (1,)), ((), ()))
    one = lax.dot_general(high, x, dims, preferred_element_type=jnp.float32)
    two = lax.dot_general(low, x[:RHS], dims, preferred_element_type=jnp.float32)
    return one[:, :RHS] + one[:, RHS:] + two


def times_cols(x, high, low):
    dims = (((1,), (0,)), ((), ()))
    x_high, x_low = halves(x)
    both = jnp.concatenate([x_high, x_low], axis=0)
    one = lax.dot_general(both, high, dims, preferred_element_type=jnp.float32)
    two = lax.dot_general(x_high, low, dims, preferred_element_type=jnp.float32)
    return one[:RHS] + one[RHS:] + two


def spread(tiles, send_ref):
    for peer in range(PEERS):
        for s in range(SLOTS):
            send_ref[peer, s] = tiles[s]


def arrived(got_ref):
    return unpack([jnp.sum(got_ref[:, s], axis=0) for s in range(SLOTS)])


def start_kernel(own_ref, b_ref, after_ref, send_ref):
    tiles = pack(b_ref[...])
    lane = lax.broadcasted_iota(jnp.int32, (8, 128), 1)
    names = jnp.zeros((8, 128), jnp.float32)
    for s in range(SLOTS):
        names = jnp.where(lane == s, own_ref[s].astype(jnp.float32), names)
    spread(tiles, send_ref)
    for peer in range(PEERS):
        send_ref[peer, SLOTS] = names


def turn(g, q):
    leaf = jnp.where(g // 16 == 3, 0, g // 16)
    first = jnp.where(q == 1, 1, 0)
    second = jnp.where(q == 0, 2, 0)
    return jnp.where(g < 64, leaf, jnp.where(g < 96, first, jnp.where(g < 128, second, 0)))


def part_of(e, g, q):
    return 3 * q + lax.rem(e + turn(g, q), 3)


def rows_of(s):
    return slice(s * BLOCK, (s + 1) * BLOCK)


def split_kernel(own_ref, me_ref, factor_ref, *refs):
    outs, sems = refs[:3], refs[3]
    copies = []
    for e in range(3):
        for s in range(SLOTS):
            at = lax.rem(e + turn(own_ref[s], me_ref[0]), 3) * PART
            for h in range(2):
                copies.append(
                    pltpu.make_async_copy(
                        factor_ref.at[rows_of(s), pl.ds(pl.multiple_of(at + h * HALF, HALF), HALF)],
                        outs[e].at[h, rows_of(s)],
                        sems.at[len(copies)],
                    )
                )
    for copy in copies:
        copy.start()
    for copy in copies:
        copy.wait()


def state_of(g, part):
    group = (g - 64) // 32
    leaf = jnp.where(part == g // 16, 2, 0)
    own = (part == 4 + 2 * group) | (part == 5 + 2 * group)
    below = (part == 2 * group) | (part == 2 * group + 1)
    middle = jnp.where(own, 2, jnp.where(below, 1, 0))
    return jnp.where(g < 64, leaf, jnp.where(g < 128, middle, jnp.where(part >= 8, 2, 1)))


def masked(pattern_ref, s, g, part, h, block):
    state = state_of(g, part)
    lane = lax.broadcasted_iota(jnp.int32, (1, 128), 1)
    row = g * BLOCK + lax.broadcasted_iota(jnp.int32, (BLOCK, 128), 0)
    out = []
    for t in range(HALF // 128):
        at = part * (PART // BLOCK) + h * (HALF // BLOCK) + 2 * t
        keep = [
            jnp.where((state == 1) & (pattern_ref[s, at + i] > 0), -1, 1 << 20) for i in range(2)
        ]
        col = part * PART + h * HALF + t * 128 + lane
        below = jnp.where(state == 2, col, jnp.where(lane < BLOCK, keep[0], keep[1]))
        out.append(halves(jnp.where(row > below, block[:, 128 * t : 128 * (t + 1)], 0.0)))
    return [jnp.concatenate([pair[i] for pair in out], axis=1) for i in range(2)]


def sources(e, own_ref, me_ref, refs):
    first, second, third_a, third_b, fourth = refs
    for d in range(4):
        q = lax.rem(me_ref[0] + d, 4)
        for s in range(SLOTS):
            part = part_of(e, own_ref[s], q)
            for h in range(2):
                given = (first, second, (third_a, third_b)[h], fourth)[d]
                yield s, h, own_ref[s], part, given.at[rows_of(s)] if d == 2 else given.at[h, rows_of(s)]


def put(refs, s, at, pair):
    for ref, value in zip(refs, pair):
        ref[rows_of(s), pl.ds(pl.multiple_of(at, HALF), HALF)] = value


def wanted(own_ref, me_ref, buf_ref, sems, parts, want):
    found = []
    for e, refs in enumerate(parts):
        for s, h, g, part, src in sources(e, own_ref, me_ref, refs):
            i = len(found)
            copy = pltpu.make_async_copy(src, buf_ref.at[i], sems.at[i])
            pl.when(want(g, part))(copy.start)
            found.append((s, h, g, part, copy, buf_ref.at[i]))
    return found


def place_leaves_kernel(own_ref, me_ref, pattern_ref, *refs):
    high_ref, low_ref, buf_ref, sems = refs[5:]

    def want(g, part):
        return (g < 64) & (part == g // 16)

    for s, h, g, part, copy, buf in wanted(own_ref, me_ref, buf_ref, sems, [refs[:5]], want):

        @pl.when(want(g, part))
        def _(s=s, h=h, g=g, part=part, copy=copy, buf=buf):
            copy.wait()
            put((high_ref, low_ref), s, h * HALF, masked(pattern_ref, s, g, part, h, buf[...]))


def place_middles_kernel(own_ref, me_ref, pattern_ref, *refs):
    buf_ref, sems = refs[14:]

    def want(g, part):
        return (g >= 64) & (g < 128) & (state_of(g, part) > 0)

    for s, h, g, part, copy, buf in wanted(own_ref, me_ref, buf_ref, sems, [refs[:5], refs[5:10]], want):

        @pl.when(want(g, part))
        def _(s=s, h=h, g=g, part=part, copy=copy, buf=buf):
            copy.wait()
            pair = masked(pattern_ref, s, g, part, h, buf[...])
            at = lax.rem(part, 2) * PART + h * HALF

            @pl.when(part < 4)
            def _():
                put(refs[10:12], s, at, pair)

            @pl.when(part >= 4)
            def _():
                put(refs[12:14], s, at, pair)


def place_all_kernel(own_ref, me_ref, pattern_ref, *refs):
    outs, (buf_ref, sems) = refs[15:17], refs[17:]
    parts = [refs[:5], refs[5:10], refs[10:15]]
    found = []
    for e in range(3):
        for s, h, g, part, src in sources(e, own_ref, me_ref, parts[e]):
            i = len(found)
            copy = pltpu.make_async_copy(src, buf_ref.at[i], sems.at[i])
            copy.start()
            found.append((s, h, g, part, copy, buf_ref.at[i]))
    for s, h, g, part, copy, buf in found:
        copy.wait()
        at = lax.rem(part, 4) * PART + h * HALF
        put([ref.at[part // 4] for ref in outs], s, at, masked(pattern_ref, s, g, part, h, buf[...]))


def own_products(own_ref, base, blocks, groups, x_ref, high_ref, low_ref):
    wide = high_ref.shape[1]
    outs = []
    for s in range(SLOTS):
        group = jnp.clip((own_ref[s] - base) // blocks, 0, groups - 1)
        x = x_ref[:, pl.ds(pl.multiple_of(group * wide, wide), wide)]
        outs.append(times_rows(x, high_ref[rows_of(s)], low_ref[rows_of(s)]))
    return jnp.concatenate(outs, axis=0).T


def leaves_kernel(own_ref, b_ref, mine_ref, other_ref, high_ref, low_ref, inv_ref, y_ref, send_ref, x_ref, names_ref, order_ref, sem):
    row = lax.broadcasted_iota(jnp.int32, (8, 128), 0)
    for far, ref in enumerate((mine_ref, other_ref)):
        for k in range(PEERS // 8):
            names = ref[(SLOTS + 1) * 8 * k + SLOTS]
            for r in range(1, 8):
                names = jnp.where(row == r, ref[(SLOTS + 1) * (8 * k + r) + SLOTS], names)
            at = far * PEERS + 8 * k
            names_ref[at : at + 8] = names.astype(jnp.int32)
    copy = pltpu.make_async_copy(names_ref, order_ref, sem.at[0])
    copy.start()
    copy.wait()
    for chip in range(2 * PEERS):
        for s in range(SLOTS):
            inv_ref[order_ref[chip, s]] = chip * SLOTS + s
    to_canonical(inv_ref, 2, mine_ref, other_ref, x_ref, True)
    y = only(own_ref, 2, own_products(own_ref, 0, 16, 4, x_ref, high_ref, low_ref) + b_ref[...])
    y_ref[...] = y
    spread(pack(y), send_ref)


def middle_resid_kernel(own_ref, inv_ref, b_ref, mine_ref, other_ref, high_ref, low_ref, r_ref, send_ref, x_ref):
    to_canonical(inv_ref, 2, mine_ref, other_ref, x_ref)
    r = only(own_ref, 1, b_ref[...] - own_products(own_ref, 64, 32, 2, x_ref, high_ref, low_ref))
    r_ref[...] = r
    spread(pack(r), send_ref)


def middle_kernel(own_ref, inv_ref, r_ref, mine_ref, other_ref, high_ref, low_ref, y_ref, send_ref, x_ref):
    to_canonical(inv_ref, 1, mine_ref, other_ref, x_ref)
    y = only(own_ref, 1, own_products(own_ref, 64, 32, 2, x_ref, high_ref, low_ref) + r_ref[...])
    y_ref[...] = y
    spread(pack(y), send_ref)


def update_kernel(inv_ref, mine_ref, other_ref, high_ref, low_ref, upd_ref, x_ref):
    to_canonical(inv_ref, 2, mine_ref, other_ref, x_ref)
    upd_ref[...] = times_rows(x_ref[...], high_ref[0], low_ref[0])


def top_resid_kernel(own_ref, inv_ref, b_ref, upd_ref, mine_ref, other_ref, high_ref, low_ref, r_ref, send_ref, x_ref):
    to_canonical(inv_ref, 1, mine_ref, other_ref, x_ref)
    upd = upd_ref[...] + times_rows(x_ref[...], high_ref[1], low_ref[1])
    r = only(own_ref, 0, b_ref[...] - upd.T)
    r_ref[...] = r
    spread(pack(r), send_ref)


def top_kernel(own_ref, inv_ref, r_ref, mine_ref, other_ref, high_ref, low_ref, y_ref, part_ref, x_ref):
    to_canonical(inv_ref, 0, mine_ref, other_ref, x_ref)
    y = only(own_ref, 0, times_rows(x_ref[...], high_ref[2], low_ref[2]).T) + r_ref[...]
    y_ref[...] = y
    to_places(inv_ref, 0, times_cols(y, high_ref[2], low_ref[2]), part_ref)


def add_kernel(level, inv_ref, *refs):
    terms = refs[:-5]
    got_ref, high_ref, low_ref, x_out_ref, part_ref = refs[-5:]
    x = arrived(got_ref)
    for term in terms:
        x = x + term[...]
    x_out_ref[...] = x
    to_places(inv_ref, level, times_cols(x, high_ref[2 - level], low_ref[2 - level]), part_ref)


def sub_kernel(level, own_ref, inv_ref, y_ref, got_ref, high_ref, low_ref, t_ref, part_ref):
    t = only(own_ref, level, y_ref[...] - arrived(got_ref))
    t_ref[...] = t
    to_places(inv_ref, level, times_cols(t, high_ref[2 - level], low_ref[2 - level]), part_ref)


def last_kernel(t_ref, x_ref, got_ref, out_ref):
    out_ref[...] = t_ref[...] + x_ref[...] + arrived(got_ref)


def swap(x):
    return lax.ppermute(x, "c", [(0, 1), (1, 0)])


def exchange(x):
    return lax.all_to_all(x, CHIPS, 0, 0)


def gather(send):
    mine = exchange(send)
    other = swap(mine)
    return mine.reshape(PLACES, 8, 128), other.reshape(PLACES, 8, 128)


def reduce(part):
    far = swap(part[PLACES:])
    return exchange((part[:PLACES] + far).reshape(PEERS, SLOTS, 8, 128))


def around(x, step):
    return lax.ppermute(x, "y", [(i, (i + step) % 4) for i in range(4)])


def over_planes(part):
    before, after = around(part, 1), around(part, -1)
    opposite = [around(before[0], 1), around(after[1], -1)]
    return part, after, opposite, before


def call(kernel, outs, specs, out_specs, scratch=(), work=0):
    return pl.pallas_call(
        kernel,
        out_shape=outs,
        in_specs=specs,
        out_specs=out_specs,
        scratch_shapes=list(scratch),
        compiler_params=pltpu.CompilerParams(vmem_limit_bytes=28 * 1024 * 1024),
        cost_estimate=pl.CostEstimate(flops=0, bytes_accessed=work, transcendentals=0) if work else None,
    )


def shards(factor, pattern, owner, right_side):
    total = pattern.shape[1]
    vec = f32(RHS, ROWS)
    send_shape = f32(PEERS, SLOTS, 8, 128)
    part_shape = f32(2 * PLACES, 8, 128)
    me = lax.axis_index("y").astype(jnp.int32).reshape(1)
    canonical = [pltpu.VMEM((2 * RHS, THIRD), jnp.bfloat16)]

    def pair(*shape):
        return (jax.ShapeDtypeStruct(shape, jnp.bfloat16),) * 2

    pieces = call(
        split_kernel,
        (f32(2, ROWS, HALF),) * 3,
        [SMEM, SMEM, HBM],
        (HBM,) * 3,
        [pltpu.SemaphoreType.DMA((18,))],
    )(owner, me, factor)

    first = over_planes(pieces[0])
    late = swap(pieces[0][0, :8, :128])
    send = call(
        start_kernel, f32(PEERS, SLOTS + 1, 8, 128), [SMEM, VMEM, VMEM], VMEM
    )(owner, right_side, late)

    mine = exchange(send)
    other = swap(mine)
    mine, other = (v.reshape(PEERS * (SLOTS + 1), 8, 128) for v in (mine, other))

    def place(kernel, outs, parts, blocks, work):
        given = [v for own, after, opposite, before in parts for v in (own, after, *opposite, before)]
        return call(
            kernel,
            outs,
            [SMEM] * 3 + [HBM] * len(given),
            (VMEM,) * len(outs),
            [pltpu.VMEM((blocks, BLOCK, HALF), jnp.float32), pltpu.SemaphoreType.DMA((blocks,))],
            work,
        )(owner, me, pattern, *given)

    d2 = place(place_leaves_kernel, pair(ROWS, 1024), [first], 24, 2 << 20)
    piece, _ = lax.optimization_barrier((pieces[1], (first[1], first[3])))
    second = over_planes(piece)

    inv, y2, send = call(
        leaves_kernel,
        (jax.ShapeDtypeStruct((total,), jnp.int32), vec, send_shape),
        [SMEM] + [VMEM] * 5,
        (SMEM, VMEM, VMEM),
        canonical
        + [
            pltpu.VMEM((2 * PEERS, 128), jnp.int32),
            pltpu.SMEM((2 * PEERS, 128), jnp.int32),
            pltpu.SemaphoreType.DMA((1,)),
        ],
    )(owner, right_side, mine, other, *d2)
    mine2, other2 = gather(send)
    middles = place(place_middles_kernel, pair(ROWS, 2048) * 2, [first, second], 48, 8 << 20)
    piece, _ = lax.optimization_barrier((pieces[2], (second[1], second[3])))
    third = over_planes(piece)
    r1, send = call(
        middle_resid_kernel, (vec, send_shape), [SMEM, SMEM] + [VMEM] * 5, (VMEM, VMEM), canonical
    )(owner, inv, right_side, mine2, other2, *middles[:2])
    mine, other = gather(send)
    y1, send = call(
        middle_kernel, (vec, send_shape), [SMEM, SMEM] + [VMEM] * 5, (VMEM, VMEM), canonical
    )(owner, inv, r1, mine, other, *middles[2:])
    mine, other = gather(send)
    m = place(place_all_kernel, pair(3, ROWS, THIRD), [first, second, third], 72, 24 << 20)
    upd = call(
        update_kernel, f32(ROWS, RHS), [SMEM] + [VMEM] * 4, VMEM, canonical, 4 << 20
    )(inv, mine2, other2, *m)
    r0, send = call(
        top_resid_kernel, (vec, send_shape), [SMEM, SMEM] + [VMEM] * 6, (VMEM, VMEM), canonical
    )(owner, inv, right_side, upd, mine, other, *m)
    mine, other = gather(send)
    y0, part = call(
        top_kernel, (vec, part_shape), [SMEM, SMEM] + [VMEM] * 5, (VMEM, VMEM), canonical
    )(owner, inv, r0, mine, other, *m)

    def adds(level, *terms):
        return call(
            functools.partial(add_kernel, level),
            (vec, part_shape),
            [SMEM] + [VMEM] * (len(terms) + 2),
            (VMEM, VMEM),
        )(inv, *terms, *m)

    def subs(level, y, got):
        return call(
            functools.partial(sub_kernel, level),
            (vec, part_shape),
            [SMEM, SMEM] + [VMEM] * 4,
            (VMEM, VMEM),
        )(owner, inv, y, got, *m)

    x0, part = adds(1, y0, reduce(part))
    t1, part = subs(1, y1, reduce(part))
    x01, part = adds(2, t1, x0, reduce(part))
    t2, part = subs(2, y2, reduce(part))
    return call(last_kernel, vec, [VMEM] * 3, VMEM)(t2, x01, reduce(part))


def solution(mesh):
    fine = Mesh(mesh.devices.reshape(4, 8, 2, 4), ("x", "z", "c", "y"))
    rows = ("x", "z", "c")
    in_specs = (P(rows, "y"), P(rows, None), P(rows), P("y", rows))
    out_specs = P("y", rows)
    return jax.shard_map(shards, mesh=fine, in_specs=in_specs, out_specs=out_specs, check_vma=False)
```

```python
import functools

import jax
import jax.numpy as jnp
from jax import lax
from jax.experimental import pallas as pl
from jax.experimental.pallas import tpu as pltpu
from jax.sharding import Mesh, PartitionSpec as P

BLOCK = 64
RHS = 16
SLOTS = 3
ROWS = SLOTS * BLOCK
THIRD = 4096
PEERS = 32
PLACES = PEERS * SLOTS
PART = 1024
OWN = 192
ME = OWN + SLOTS
META = 200
HALF = 512
VMEM = pl.BlockSpec(memory_space=pltpu.VMEM)
SMEM = pl.BlockSpec(memory_space=pltpu.SMEM)
ANY = pl.BlockSpec(memory_space=pl.ANY)
HBM = pl.BlockSpec(memory_space=pltpu.HBM)
CHIPS = ("x", "z")


def f32(*shape):
    return jax.ShapeDtypeStruct(shape, jnp.float32)


def left_half():
    return lax.broadcasted_iota(jnp.int32, (8, 128), 1) < BLOCK


def pack(rows):
    return [
        jnp.concatenate(
            [rows[:8, s * BLOCK : (s + 1) * BLOCK], rows[8:, s * BLOCK : (s + 1) * BLOCK]], axis=1
        )
        for s in range(SLOTS)
    ]


def unpack(tiles):
    upper = jnp.concatenate([t[:, :BLOCK] for t in tiles], axis=1)
    lower = jnp.concatenate([t[:, BLOCK:] for t in tiles], axis=1)
    return jnp.concatenate([upper, lower], axis=0)


def only(meta_ref, level, rows):
    slot = lax.broadcasted_iota(jnp.int32, rows.shape, 1) // BLOCK
    keep = jnp.zeros(rows.shape, jnp.bool_)
    for s in range(SLOTS):
        g = meta_ref[OWN + s]
        here = (g >= (2 - level) * 64) & (g < (3 - level) * 64)
        keep = keep | ((slot == s) & here)
    return jnp.where(keep, rows, 0.0)


def halves(x):
    high = x.astype(jnp.bfloat16)
    return high, (x - high.astype(jnp.float32)).astype(jnp.bfloat16)


def to_canonical(meta_ref, level, mine_ref, other_ref, x_ref, extra=False):
    base = (2 - level) * 64
    half = left_half()

    def tile(place):
        near = jnp.minimum(place, PLACES - 1)
        far = jnp.maximum(place, PLACES) - PLACES
        if extra:
            near, far = near + near // SLOTS, far + far // SLOTS
        return jnp.where(place >= PLACES, other_ref[far], mine_ref[near])

    for t in range(32):
        a = tile(meta_ref[base + 2 * t])
        b = tile(meta_ref[base + 2 * t + 1])
        top = jnp.where(half, a, pltpu.roll(b, BLOCK, 1))
        bottom = jnp.where(half, pltpu.roll(a, BLOCK, 1), b)
        high, low = halves(jnp.concatenate([top, bottom], axis=0))
        x_ref[0:16, 128 * t : 128 * (t + 1)] = high
        x_ref[16:32, 128 * t : 128 * (t + 1)] = low


def to_places(meta_ref, level, x, out_ref):
    base = (2 - level) * 64
    half = left_half()
    out_ref[...] = jnp.zeros_like(out_ref)
    for t in range(32):
        top = x[0:8, 128 * t : 128 * (t + 1)]
        bottom = x[8:16, 128 * t : 128 * (t + 1)]
        out_ref[meta_ref[base + 2 * t]] = jnp.where(half, top, pltpu.roll(bottom, BLOCK, 1))
        out_ref[meta_ref[base + 2 * t + 1]] = jnp.where(half, pltpu.roll(top, BLOCK, 1), bottom)


def times_rows(x, high, low):
    dims = (((1,), (1,)), ((), ()))
    one = lax.dot_general(high, x, dims, preferred_element_type=jnp.float32)
    two = lax.dot_general(low, x[:RHS], dims, preferred_element_type=jnp.float32)
    return one[:, :RHS] + one[:, RHS:] + two


def times_cols(x, high, low):
    dims = (((1,), (0,)), ((), ()))
    x_high, x_low = halves(x)
    both = jnp.concatenate([x_high, x_low], axis=0)
    one = lax.dot_general(both, high, dims, preferred_element_type=jnp.float32)
    two = lax.dot_general(x_high, low, dims, preferred_element_type=jnp.float32)
    return one[:RHS] + one[RHS:] + two


def spread(tiles, send_ref):
    for peer in range(PEERS):
        for s in range(SLOTS):
            send_ref[peer, s] = tiles[s]


def arrived(got_ref):
    return unpack([jnp.sum(got_ref[:, s], axis=0) for s in range(SLOTS)])


def start_kernel(own_ref, pattern_ref, b_ref, after_ref, send_ref, below_ref):
    tiles = pack(b_ref[...])
    lane = lax.broadcasted_iota(jnp.int32, (8, 128), 1)
    names = jnp.zeros((8, 128), jnp.float32)
    for s in range(SLOTS):
        names = jnp.where(lane == s, own_ref[s].astype(jnp.float32), names)
    spread(tiles, send_ref)
    for peer in range(PEERS):
        send_ref[peer, SLOTS] = names
    lane = lax.broadcasted_iota(jnp.int32, (1, 128), 1)
    for s in range(SLOTS):
        for part in range(12):
            state = state_of(own_ref[s], part)
            for t in range(PART // 128):
                at = part * (PART // BLOCK) + 2 * t
                keep = [
                    jnp.where((state == 1) & (pattern_ref[s, at + i] > 0), -1, 1 << 20)
                    for i in range(2)
                ]
                col = part * PART + t * 128 + lane
                rest = jnp.where(lane < BLOCK, keep[0], keep[1])
                below_ref[s, :, part * PART + t * 128 : part * PART + (t + 1) * 128] = jnp.where(
                    state == 2, col, rest
                )


def names_kernel(own_ref, me_ref, mine_ref, other_ref, meta_ref, names_ref, order_ref, sem):
    row = lax.broadcasted_iota(jnp.int32, (8, 128), 0)
    for far, ref in enumerate((mine_ref, other_ref)):
        for k in range(PEERS // 8):
            names = ref[(SLOTS + 1) * 8 * k + SLOTS]
            for r in range(1, 8):
                names = jnp.where(row == r, ref[(SLOTS + 1) * (8 * k + r) + SLOTS], names)
            at = far * PEERS + 8 * k
            names_ref[at : at + 8] = names.astype(jnp.int32)
    copy = pltpu.make_async_copy(names_ref, order_ref, sem.at[0])
    copy.start()
    copy.wait()
    for chip in range(2 * PEERS):
        for s in range(SLOTS):
            meta_ref[order_ref[chip, s]] = chip * SLOTS + s
    for s in range(SLOTS):
        meta_ref[OWN + s] = own_ref[s]
    meta_ref[ME] = me_ref[0]
    for i in range(ME + 1, META):
        meta_ref[i] = 0


def turn(g, q):
    leaf = jnp.where(g // 16 == 3, 0, g // 16)
    first = jnp.where(q == 1, 1, 0)
    second = jnp.where(q == 0, 2, 0)
    return jnp.where(g < 64, leaf, jnp.where(g < 96, first, jnp.where(g < 128, second, 0)))


def part_of(e, g, q):
    return 3 * q + lax.rem(e + turn(g, q), 3)


def rows_of(s):
    return slice(s * BLOCK, (s + 1) * BLOCK)


def split_kernel(own_ref, me_ref, factor_ref, *refs):
    outs, sems = refs[:3], refs[3]
    copies = []
    for e in range(3):
        for s in range(SLOTS):
            at = lax.rem(e + turn(own_ref[s], me_ref[0]), 3) * PART
            for h in range(2):
                copies.append(
                    pltpu.make_async_copy(
                        factor_ref.at[rows_of(s), pl.ds(pl.multiple_of(at + h * HALF, HALF), HALF)],
                        outs[e].at[h, rows_of(s)],
                        sems.at[len(copies)],
                    )
                )
    for copy in copies:
        copy.start()
    for copy in copies:
        copy.wait()


def state_of(g, part):
    group = (g - 64) // 32
    leaf = jnp.where(part == g // 16, 2, 0)
    own = (part == 4 + 2 * group) | (part == 5 + 2 * group)
    below = (part == 2 * group) | (part == 2 * group + 1)
    middle = jnp.where(own, 2, jnp.where(below, 1, 0))
    return jnp.where(g < 64, leaf, jnp.where(g < 128, middle, jnp.where(part >= 8, 2, 1)))


def masked(below_ref, s, g, part, h, block):
    row = g * BLOCK + lax.broadcasted_iota(jnp.int32, (BLOCK, HALF), 0)
    col0 = pl.multiple_of(part * PART + h * HALF, HALF)
    return halves(jnp.where(row > below_ref[s, :, pl.ds(col0, HALF)], block, 0.0))


def sources(e, meta_ref, refs):
    for d in range(4):
        q = d if e == 2 else lax.rem(meta_ref[ME] + d, 4)
        for s in range(SLOTS):
            g = meta_ref[OWN + s]
            part = part_of(e, g, q)
            for h in range(2):
                if e == 2:
                    src = refs[0].at[d, h, rows_of(s)]
                elif d == 2:
                    src = refs[2 + h].at[rows_of(s)]
                else:
                    src = refs[(0, 1, 0, 4)[d]].at[h, rows_of(s)]
                yield s, h, g, part, src


def put(refs, s, at, pair):
    for ref, value in zip(refs, pair):
        ref[rows_of(s), pl.ds(pl.multiple_of(at, HALF), HALF)] = value


def wanted(meta_ref, buf_ref, sems, parts, want):
    found = []
    for e, refs in enumerate(parts):
        for s, h, g, part, src in sources(e, meta_ref, refs):
            i = len(found)
            copy = pltpu.make_async_copy(src, buf_ref.at[i], sems.at[i])
            pl.when(want(g, part))(copy.start)
            found.append((s, h, g, part, copy, buf_ref.at[i]))
    return found


def place_leaves_kernel(meta_ref, below_ref, *refs):
    high_ref, low_ref, buf_ref, sems = refs[5:]

    def want(g, part):
        return (g < 64) & (part == g // 16)

    for s, h, g, part, copy, buf in wanted(meta_ref, buf_ref, sems, [refs[:5]], want):

        @pl.when(want(g, part))
        def _(s=s, h=h, g=g, part=part, copy=copy, buf=buf):
            copy.wait()
            put((high_ref, low_ref), s, h * HALF, masked(below_ref, s, g, part, h, buf[...]))


def place_middles_kernel(meta_ref, below_ref, *refs):
    buf_ref, sems = refs[14:]

    def want(g, part):
        return (g >= 64) & (g < 128) & (state_of(g, part) > 0)

    for s, h, g, part, copy, buf in wanted(meta_ref, buf_ref, sems, [refs[:5], refs[5:10]], want):

        @pl.when(want(g, part))
        def _(s=s, h=h, g=g, part=part, copy=copy, buf=buf):
            copy.wait()
            pair = masked(below_ref, s, g, part, h, buf[...])
            at = lax.rem(part, 2) * PART + h * HALF

            @pl.when(part < 4)
            def _():
                put(refs[10:12], s, at, pair)

            @pl.when(part >= 4)
            def _():
                put(refs[12:14], s, at, pair)


def place_all_kernel(meta_ref, below_ref, *refs):
    outs, (buf_ref, sems) = refs[11:13], refs[13:]
    parts = [refs[:5], refs[5:10], refs[10:11]]
    found = []
    for e in range(3):
        for s, h, g, part, src in sources(e, meta_ref, parts[e]):
            i = len(found)
            copy = pltpu.make_async_copy(src, buf_ref.at[i], sems.at[i])
            copy.start()
            found.append((s, h, g, part, copy, buf_ref.at[i]))
    for s, h, g, part, copy, buf in found:
        copy.wait()
        at = lax.rem(part, 4) * PART + h * HALF
        put([ref.at[part // 4] for ref in outs], s, at, masked(below_ref, s, g, part, h, buf[...]))


def own_products(meta_ref, base, blocks, groups, x_ref, high_ref, low_ref):
    wide = high_ref.shape[1]
    outs = []
    for s in range(SLOTS):
        group = jnp.clip((meta_ref[OWN + s] - base) // blocks, 0, groups - 1)
        x = x_ref[:, pl.ds(pl.multiple_of(group * wide, wide), wide)]
        outs.append(times_rows(x, high_ref[rows_of(s)], low_ref[rows_of(s)]))
    return jnp.concatenate(outs, axis=0).T


def leaves_kernel(meta_ref, b_ref, mine_ref, other_ref, high_ref, low_ref, y_ref, send_ref, x_ref):
    to_canonical(meta_ref, 2, mine_ref, other_ref, x_ref, True)
    y = only(meta_ref, 2, own_products(meta_ref, 0, 16, 4, x_ref, high_ref, low_ref) + b_ref[...])
    y_ref[...] = y
    spread(pack(y), send_ref)


def middle_resid_kernel(meta_ref, b_ref, mine_ref, other_ref, high_ref, low_ref, r_ref, send_ref, x_ref):
    to_canonical(meta_ref, 2, mine_ref, other_ref, x_ref)
    r = only(meta_ref, 1, b_ref[...] - own_products(meta_ref, 64, 32, 2, x_ref, high_ref, low_ref))
    r_ref[...] = r
    spread(pack(r), send_ref)


def middle_kernel(meta_ref, r_ref, mine_ref, other_ref, high_ref, low_ref, y_ref, send_ref, x_ref):
    to_canonical(meta_ref, 1, mine_ref, other_ref, x_ref)
    y = only(meta_ref, 1, own_products(meta_ref, 64, 32, 2, x_ref, high_ref, low_ref) + r_ref[...])
    y_ref[...] = y
    spread(pack(y), send_ref)


def update_kernel(meta_ref, mine_ref, other_ref, high_ref, low_ref, upd_ref, x_ref):
    to_canonical(meta_ref, 2, mine_ref, other_ref, x_ref)
    upd_ref[...] = times_rows(x_ref[...], high_ref[0], low_ref[0])


def top_resid_kernel(meta_ref, b_ref, upd_ref, mine_ref, other_ref, high_ref, low_ref, r_ref, send_ref, x_ref):
    to_canonical(meta_ref, 1, mine_ref, other_ref, x_ref)
    upd = upd_ref[...] + times_rows(x_ref[...], high_ref[1], low_ref[1])
    r = only(meta_ref, 0, b_ref[...] - upd.T)
    r_ref[...] = r
    spread(pack(r), send_ref)


def top_kernel(meta_ref, r_ref, mine_ref, other_ref, high_ref, low_ref, y_ref, part_ref, x_ref):
    to_canonical(meta_ref, 0, mine_ref, other_ref, x_ref)
    y = only(meta_ref, 0, times_rows(x_ref[...], high_ref[2], low_ref[2]).T) + r_ref[...]
    y_ref[...] = y
    to_places(meta_ref, 0, times_cols(y, high_ref[2], low_ref[2]), part_ref)


def add_kernel(level, meta_ref, *refs):
    terms = refs[:-5]
    got_ref, high_ref, low_ref, x_out_ref, part_ref = refs[-5:]
    x = arrived(got_ref)
    for term in terms:
        x = x + term[...]
    x_out_ref[...] = x
    to_places(meta_ref, level, times_cols(x, high_ref[2 - level], low_ref[2 - level]), part_ref)


def sub_kernel(level, meta_ref, y_ref, got_ref, high_ref, low_ref, t_ref, part_ref):
    t = only(meta_ref, level, y_ref[...] - arrived(got_ref))
    t_ref[...] = t
    to_places(meta_ref, level, times_cols(t, high_ref[2 - level], low_ref[2 - level]), part_ref)


def last_kernel(t_ref, x_ref, got_ref, out_ref):
    out_ref[...] = t_ref[...] + x_ref[...] + arrived(got_ref)


def swap(x):
    return lax.ppermute(x, "c", [(0, 1), (1, 0)])


def exchange(x):
    return lax.all_to_all(x, CHIPS, 0, 0)


def gather(send):
    mine = exchange(send)
    other = swap(mine)
    return mine.reshape(PLACES, 8, 128), other.reshape(PLACES, 8, 128)


def reduce(part):
    far = swap(part[PLACES:])
    return exchange((part[:PLACES] + far).reshape(PEERS, SLOTS, 8, 128))


def around(x, step):
    return lax.ppermute(x, "y", [(i, (i + step) % 4) for i in range(4)])


def over_planes(part):
    before, after = around(part, 1), around(part, -1)
    opposite = [around(before[0], 1), around(after[1], -1)]
    return part, after, opposite, before


def call(kernel, outs, specs, out_specs, scratch=(), work=0):
    return pl.pallas_call(
        kernel,
        out_shape=outs,
        in_specs=specs,
        out_specs=out_specs,
        scratch_shapes=list(scratch),
        compiler_params=pltpu.CompilerParams(vmem_limit_bytes=28 * 1024 * 1024),
        cost_estimate=pl.CostEstimate(flops=0, bytes_accessed=work, transcendentals=0) if work else None,
    )


def shards(factor, pattern, owner, right_side):
    total = pattern.shape[1]
    vec = f32(RHS, ROWS)
    send_shape = f32(PEERS, SLOTS, 8, 128)
    part_shape = f32(2 * PLACES, 8, 128)
    me = lax.axis_index("y").astype(jnp.int32).reshape(1)
    canonical = [pltpu.VMEM((2 * RHS, THIRD), jnp.bfloat16)]

    def pair(*shape):
        return (jax.ShapeDtypeStruct(shape, jnp.bfloat16),) * 2

    pieces = call(
        split_kernel,
        (f32(2, ROWS, HALF),) * 3,
        [SMEM, SMEM, HBM],
        (HBM,) * 3,
        [pltpu.SemaphoreType.DMA((18,))],
    )(owner, me, factor)

    first = over_planes(pieces[0])
    late = swap(pieces[0][0, :8, :128])
    send, below = call(
        start_kernel,
        (f32(PEERS, SLOTS + 1, 8, 128), jax.ShapeDtypeStruct((SLOTS, 1, total * BLOCK), jnp.int32)),
        [SMEM, SMEM, VMEM, VMEM],
        (VMEM, VMEM),
    )(owner, pattern, right_side, late)

    mine = exchange(send)
    other = swap(mine)
    mine, other = (v.reshape(PEERS * (SLOTS + 1), 8, 128) for v in (mine, other))
    meta = call(
        names_kernel,
        jax.ShapeDtypeStruct((META,), jnp.int32),
        [SMEM, SMEM, VMEM, VMEM],
        SMEM,
        [
            pltpu.VMEM((2 * PEERS, 128), jnp.int32),
            pltpu.SMEM((2 * PEERS, 128), jnp.int32),
            pltpu.SemaphoreType.DMA((1,)),
        ],
    )(owner, me, mine, other)

    def place(kernel, outs, parts, blocks, work):
        given = []
        for own, after, opposite, before in parts:
            given += [own, after, *opposite, before]
        if kernel is place_all_kernel:
            given.append(third)
        return call(
            kernel,
            outs,
            [SMEM, VMEM] + [ANY] * len(given),
            (VMEM,) * len(outs),
            [pltpu.VMEM((blocks, BLOCK, HALF), jnp.float32), pltpu.SemaphoreType.DMA((blocks,))],
            work,
        )(meta, below, *given)

    d2 = place(place_leaves_kernel, pair(ROWS, 1024), [first], 24, 2 << 20)
    piece, _ = lax.optimization_barrier((pieces[1], (first[2], meta)))
    second = over_planes(piece)

    y2, send = call(
        leaves_kernel, (vec, send_shape), [SMEM] + [VMEM] * 5, (VMEM, VMEM), canonical
    )(meta, right_side, mine, other, *d2)
    mine2, other2 = gather(send)
    middles = place(place_middles_kernel, pair(ROWS, 2048) * 2, [first, second], 48, 8 << 20)
    piece, _ = lax.optimization_barrier((pieces[2], (second[1], second[3])))
    third = lax.all_gather(piece, "y", axis=0, tiled=False)
    r1, send = call(
        middle_resid_kernel, (vec, send_shape), [SMEM] + [VMEM] * 5, (VMEM, VMEM), canonical
    )(meta, right_side, mine2, other2, *middles[:2])
    mine, other = gather(send)
    y1, send = call(
        middle_kernel, (vec, send_shape), [SMEM] + [VMEM] * 5, (VMEM, VMEM), canonical
    )(meta, r1, mine, other, *middles[2:])
    mine, other = gather(send)
    m = place(place_all_kernel, pair(3, ROWS, THIRD), [first, second], 72, 24 << 20)
    upd = call(
        update_kernel, f32(ROWS, RHS), [SMEM] + [VMEM] * 4, VMEM, canonical, 4 << 20
    )(meta, mine2, other2, *m)
    r0, send = call(
        top_resid_kernel, (vec, send_shape), [SMEM] + [VMEM] * 6, (VMEM, VMEM), canonical
    )(meta, right_side, upd, mine, other, *m)
    mine, other = gather(send)
    y0, part = call(
        top_kernel, (vec, part_shape), [SMEM] + [VMEM] * 5, (VMEM, VMEM), canonical
    )(meta, r0, mine, other, *m)

    def adds(level, *terms):
        return call(
            functools.partial(add_kernel, level),
            (vec, part_shape),
            [SMEM] + [VMEM] * (len(terms) + 2),
            (VMEM, VMEM),
        )(meta, *terms, *m)

    def subs(level, y, got):
        return call(
            functools.partial(sub_kernel, level),
            (vec, part_shape),
            [SMEM] + [VMEM] * 4,
            (VMEM, VMEM),
        )(meta, y, got, *m)

    x0, part = adds(1, y0, reduce(part))
    t1, part = subs(1, y1, reduce(part))
    x01, part = adds(2, t1, x0, reduce(part))
    t2, part = subs(2, y2, reduce(part))
    return call(last_kernel, vec, [VMEM] * 3, VMEM)(t2, x01, reduce(part))


def solution(mesh):
    fine = Mesh(mesh.devices.reshape(4, 8, 2, 4), ("x", "z", "c", "y"))
    rows = ("x", "z", "c")
    in_specs = (P(rows, "y"), P(rows, None), P(rows), P("y", rows))
    out_specs = P("y", rows)
    return jax.shard_map(shards, mesh=fine, in_specs=in_specs, out_specs=out_specs, check_vma=False)
```

```python
import functools

import jax
import jax.numpy as jnp
from jax import lax
from jax.experimental import pallas as pl
from jax.experimental.pallas import tpu as pltpu
from jax.sharding import Mesh, PartitionSpec as P

BLOCK = 64
RHS = 16
SLOTS = 3
ROWS = SLOTS * BLOCK
THIRD = 4096
PEERS = 32
PLACES = PEERS * SLOTS
PART = 1024
OWN = 192
ME = OWN + SLOTS
META = 200
HALF = 512
VMEM = pl.BlockSpec(memory_space=pltpu.VMEM)
SMEM = pl.BlockSpec(memory_space=pltpu.SMEM)
HBM = pl.BlockSpec(memory_space=pltpu.HBM)
CHIPS = ("x", "z")


def f32(*shape):
    return jax.ShapeDtypeStruct(shape, jnp.float32)


def left_half():
    return lax.broadcasted_iota(jnp.int32, (8, 128), 1) < BLOCK


def pack(rows):
    return [
        jnp.concatenate(
            [rows[:8, s * BLOCK : (s + 1) * BLOCK], rows[8:, s * BLOCK : (s + 1) * BLOCK]], axis=1
        )
        for s in range(SLOTS)
    ]


def unpack(tiles):
    upper = jnp.concatenate([t[:, :BLOCK] for t in tiles], axis=1)
    lower = jnp.concatenate([t[:, BLOCK:] for t in tiles], axis=1)
    return jnp.concatenate([upper, lower], axis=0)


def only(meta_ref, level, rows):
    slot = lax.broadcasted_iota(jnp.int32, rows.shape, 1) // BLOCK
    keep = jnp.zeros(rows.shape, jnp.bool_)
    for s in range(SLOTS):
        g = meta_ref[OWN + s]
        here = (g >= (2 - level) * 64) & (g < (3 - level) * 64)
        keep = keep | ((slot == s) & here)
    return jnp.where(keep, rows, 0.0)


def halves(x):
    high = x.astype(jnp.bfloat16)
    return high, (x - high.astype(jnp.float32)).astype(jnp.bfloat16)


def to_canonical(meta_ref, level, mine_ref, other_ref, x_ref, extra=False):
    base = (2 - level) * 64
    half = left_half()

    def tile(place):
        near = jnp.minimum(place, PLACES - 1)
        far = jnp.maximum(place, PLACES) - PLACES
        if extra:
            near, far = near + near // SLOTS, far + far // SLOTS
        return jnp.where(place >= PLACES, other_ref[far], mine_ref[near])

    for t in range(32):
        a = tile(meta_ref[base + 2 * t])
        b = tile(meta_ref[base + 2 * t + 1])
        top = jnp.where(half, a, pltpu.roll(b, BLOCK, 1))
        bottom = jnp.where(half, pltpu.roll(a, BLOCK, 1), b)
        high, low = halves(jnp.concatenate([top, bottom], axis=0))
        x_ref[0:16, 128 * t : 128 * (t + 1)] = high
        x_ref[16:32, 128 * t : 128 * (t + 1)] = low


def to_places(meta_ref, level, x, out_ref):
    base = (2 - level) * 64
    half = left_half()
    out_ref[...] = jnp.zeros_like(out_ref)
    for t in range(32):
        top = x[0:8, 128 * t : 128 * (t + 1)]
        bottom = x[8:16, 128 * t : 128 * (t + 1)]
        out_ref[meta_ref[base + 2 * t]] = jnp.where(half, top, pltpu.roll(bottom, BLOCK, 1))
        out_ref[meta_ref[base + 2 * t + 1]] = jnp.where(half, pltpu.roll(top, BLOCK, 1), bottom)


def times_rows(x, high, low):
    dims = (((1,), (1,)), ((), ()))
    one = lax.dot_general(high, x, dims, preferred_element_type=jnp.float32)
    two = lax.dot_general(low, x[:RHS], dims, preferred_element_type=jnp.float32)
    return one[:, :RHS] + one[:, RHS:] + two


def times_cols(x, high, low):
    dims = (((1,), (0,)), ((), ()))
    x_high, x_low = halves(x)
    both = jnp.concatenate([x_high, x_low], axis=0)
    one = lax.dot_general(both, high, dims, preferred_element_type=jnp.float32)
    two = lax.dot_general(x_high, low, dims, preferred_element_type=jnp.float32)
    return one[:RHS] + one[RHS:] + two


def spread(tiles, send_ref):
    for peer in range(PEERS):
        for s in range(SLOTS):
            send_ref[peer, s] = tiles[s]


def arrived(got_ref):
    return unpack([jnp.sum(got_ref[:, s], axis=0) for s in range(SLOTS)])


def start_kernel(own_ref, pattern_ref, b_ref, after_ref, send_ref, below_ref):
    tiles = pack(b_ref[...])
    lane = lax.broadcasted_iota(jnp.int32, (8, 128), 1)
    names = jnp.zeros((8, 128), jnp.float32)
    for s in range(SLOTS):
        names = jnp.where(lane == s, own_ref[s].astype(jnp.float32), names)
    spread(tiles, send_ref)
    for peer in range(PEERS):
        send_ref[peer, SLOTS] = names
    lane = lax.broadcasted_iota(jnp.int32, (1, 128), 1)
    for s in range(SLOTS):
        for part in range(12):
            state = state_of(own_ref[s], part)
            for t in range(PART // 128):
                at = part * (PART // BLOCK) + 2 * t
                keep = [
                    jnp.where((state == 1) & (pattern_ref[s, at + i] > 0), -1, 1 << 20)
                    for i in range(2)
                ]
                col = part * PART + t * 128 + lane
                rest = jnp.where(lane < BLOCK, keep[0], keep[1])
                below_ref[s, :, part * PART + t * 128 : part * PART + (t + 1) * 128] = jnp.where(
                    state == 2, col, rest
                )


def names_kernel(own_ref, me_ref, mine_ref, other_ref, meta_ref, names_ref, order_ref, sem):
    row = lax.broadcasted_iota(jnp.int32, (8, 128), 0)
    for far, ref in enumerate((mine_ref, other_ref)):
        for k in range(PEERS // 8):
            names = ref[(SLOTS + 1) * 8 * k + SLOTS]
            for r in range(1, 8):
                names = jnp.where(row == r, ref[(SLOTS + 1) * (8 * k + r) + SLOTS], names)
            at = far * PEERS + 8 * k
            names_ref[at : at + 8] = names.astype(jnp.int32)
    copy = pltpu.make_async_copy(names_ref, order_ref, sem.at[0])
    copy.start()
    copy.wait()
    for chip in range(2 * PEERS):
        for s in range(SLOTS):
            meta_ref[order_ref[chip, s]] = chip * SLOTS + s
    for s in range(SLOTS):
        meta_ref[OWN + s] = own_ref[s]
    meta_ref[ME] = me_ref[0]
    for i in range(ME + 1, META):
        meta_ref[i] = 0


def turn(g, q):
    leaf = jnp.where(g // 16 == 3, 0, g // 16)
    first = jnp.where(q == 1, 1, 0)
    second = jnp.where(q == 0, 2, 0)
    return jnp.where(g < 64, leaf, jnp.where(g < 96, first, jnp.where(g < 128, second, 0)))


def part_of(e, g, q):
    return 3 * q + lax.rem(e + turn(g, q), 3)


def rows_of(s):
    return slice(s * BLOCK, (s + 1) * BLOCK)


def split_kernel(own_ref, me_ref, factor_ref, *refs):
    outs, sems = refs[:3], refs[3]
    copies = []
    for e in range(3):
        for s in range(SLOTS):
            at = lax.rem(e + turn(own_ref[s], me_ref[0]), 3) * PART
            for h in range(2):
                copies.append(
                    pltpu.make_async_copy(
                        factor_ref.at[rows_of(s), pl.ds(pl.multiple_of(at + h * HALF, HALF), HALF)],
                        outs[e].at[h, rows_of(s)],
                        sems.at[len(copies)],
                    )
                )
    for copy in copies:
        copy.start()
    for copy in copies:
        copy.wait()


def state_of(g, part):
    group = (g - 64) // 32
    leaf = jnp.where(part == g // 16, 2, 0)
    own = (part == 4 + 2 * group) | (part == 5 + 2 * group)
    below = (part == 2 * group) | (part == 2 * group + 1)
    middle = jnp.where(own, 2, jnp.where(below, 1, 0))
    return jnp.where(g < 64, leaf, jnp.where(g < 128, middle, jnp.where(part >= 8, 2, 1)))


def masked(below_ref, s, g, part, h, block):
    row = g * BLOCK + lax.broadcasted_iota(jnp.int32, (BLOCK, HALF), 0)
    col0 = pl.multiple_of(part * PART + h * HALF, HALF)
    return halves(jnp.where(row > below_ref[s, :, pl.ds(col0, HALF)], block, 0.0))


def sources(e, meta_ref, refs):
    for d in range(4):
        q = lax.rem(meta_ref[ME] + d, 4)
        for s in range(SLOTS):
            g = meta_ref[OWN + s]
            for h in range(2):
                src = refs[2 + h].at[rows_of(s)] if d == 2 else refs[(0, 1, 0, 4)[d]].at[h, rows_of(s)]
                yield s, h, g, part_of(e, g, q), src


def put(refs, s, at, pair):
    for ref, value in zip(refs, pair):
        ref[rows_of(s), pl.ds(pl.multiple_of(at, HALF), HALF)] = value


def place_leaves_kernel(meta_ref, below_ref, *refs):
    for s, h, g, part, src in sources(0, meta_ref, refs[:5]):

        @pl.when((g < 64) & (part == g // 16))
        def _(s=s, h=h, g=g, part=part, src=src):
            put(refs[5:7], s, h * HALF, masked(below_ref, s, g, part, h, src[...]))


def place_middles_kernel(meta_ref, below_ref, *refs):
    for e in range(2):
        for s, h, g, part, src in sources(e, meta_ref, refs[5 * e : 5 * e + 5]):
            mine = (g >= 64) & (g < 128) & (state_of(g, part) > 0)
            at = lax.rem(part, 2) * PART + h * HALF

            @pl.when(mine & (part < 4))
            def _(s=s, h=h, g=g, part=part, src=src, at=at):
                put(refs[10:12], s, at, masked(below_ref, s, g, part, h, src[...]))

            @pl.when(mine & (part >= 4))
            def _(s=s, h=h, g=g, part=part, src=src, at=at):
                put(refs[12:14], s, at, masked(below_ref, s, g, part, h, src[...]))


def place_all_kernel(meta_ref, below_ref, *refs):
    for e in range(3):
        for s, h, g, part, src in sources(e, meta_ref, refs[5 * e : 5 * e + 5]):
            at = lax.rem(part, 4) * PART + h * HALF
            outs = [ref.at[part // 4] for ref in refs[15:17]]
            put(outs, s, at, masked(below_ref, s, g, part, h, src[...]))


def own_products(meta_ref, base, blocks, groups, x_ref, high_ref, low_ref):
    wide = high_ref.shape[1]
    outs = []
    for s in range(SLOTS):
        group = jnp.clip((meta_ref[OWN + s] - base) // blocks, 0, groups - 1)
        x = x_ref[:, pl.ds(pl.multiple_of(group * wide, wide), wide)]
        outs.append(times_rows(x, high_ref[rows_of(s)], low_ref[rows_of(s)]))
    return jnp.concatenate(outs, axis=0).T


def leaves_kernel(meta_ref, b_ref, mine_ref, other_ref, high_ref, low_ref, y_ref, send_ref, x_ref):
    to_canonical(meta_ref, 2, mine_ref, other_ref, x_ref, True)
    y = only(meta_ref, 2, own_products(meta_ref, 0, 16, 4, x_ref, high_ref, low_ref) + b_ref[...])
    y_ref[...] = y
    spread(pack(y), send_ref)


def middle_resid_kernel(meta_ref, b_ref, mine_ref, other_ref, high_ref, low_ref, r_ref, send_ref, x_ref):
    to_canonical(meta_ref, 2, mine_ref, other_ref, x_ref)
    r = only(meta_ref, 1, b_ref[...] - own_products(meta_ref, 64, 32, 2, x_ref, high_ref, low_ref))
    r_ref[...] = r
    spread(pack(r), send_ref)


def middle_kernel(meta_ref, r_ref, mine_ref, other_ref, high_ref, low_ref, y_ref, send_ref, x_ref):
    to_canonical(meta_ref, 1, mine_ref, other_ref, x_ref)
    y = only(meta_ref, 1, own_products(meta_ref, 64, 32, 2, x_ref, high_ref, low_ref) + r_ref[...])
    y_ref[...] = y
    spread(pack(y), send_ref)


def update_kernel(meta_ref, mine_ref, other_ref, high_ref, low_ref, upd_ref, x_ref):
    to_canonical(meta_ref, 2, mine_ref, other_ref, x_ref)
    upd_ref[...] = times_rows(x_ref[...], high_ref[0], low_ref[0])


def top_resid_kernel(meta_ref, b_ref, upd_ref, mine_ref, other_ref, high_ref, low_ref, r_ref, send_ref, x_ref):
    to_canonical(meta_ref, 1, mine_ref, other_ref, x_ref)
    upd = upd_ref[...] + times_rows(x_ref[...], high_ref[1], low_ref[1])
    r = only(meta_ref, 0, b_ref[...] - upd.T)
    r_ref[...] = r
    spread(pack(r), send_ref)


def top_kernel(meta_ref, r_ref, mine_ref, other_ref, high_ref, low_ref, y_ref, part_ref, x_ref):
    to_canonical(meta_ref, 0, mine_ref, other_ref, x_ref)
    y = only(meta_ref, 0, times_rows(x_ref[...], high_ref[2], low_ref[2]).T) + r_ref[...]
    y_ref[...] = y
    to_places(meta_ref, 0, times_cols(y, high_ref[2], low_ref[2]), part_ref)


def add_kernel(level, meta_ref, *refs):
    terms = refs[:-5]
    got_ref, high_ref, low_ref, x_out_ref, part_ref = refs[-5:]
    x = arrived(got_ref)
    for term in terms:
        x = x + term[...]
    x_out_ref[...] = x
    to_places(meta_ref, level, times_cols(x, high_ref[2 - level], low_ref[2 - level]), part_ref)


def sub_kernel(level, meta_ref, y_ref, got_ref, high_ref, low_ref, t_ref, part_ref):
    t = only(meta_ref, level, y_ref[...] - arrived(got_ref))
    t_ref[...] = t
    to_places(meta_ref, level, times_cols(t, high_ref[2 - level], low_ref[2 - level]), part_ref)


def last_kernel(t_ref, x_ref, got_ref, out_ref):
    out_ref[...] = t_ref[...] + x_ref[...] + arrived(got_ref)


def swap(x):
    return lax.ppermute(x, "c", [(0, 1), (1, 0)])


def exchange(x):
    return lax.all_to_all(x, CHIPS, 0, 0)


def gather(send):
    mine = exchange(send)
    other = swap(mine)
    return mine.reshape(PLACES, 8, 128), other.reshape(PLACES, 8, 128)


def reduce(part):
    far = swap(part[PLACES:])
    return exchange((part[:PLACES] + far).reshape(PEERS, SLOTS, 8, 128))


def around(x, step):
    return lax.ppermute(x, "y", [(i, (i + step) % 4) for i in range(4)])


def over_planes(part, tie=None):
    before, after = around(part, 1), around(part, -1)
    if tie is not None:
        before, after, tie = lax.optimization_barrier((before, after, tie))
    else:
        before, after = lax.optimization_barrier((before, after))
    opposite = [around(before[0], 1), around(after[1], -1)]
    return (part, after, opposite, before), tie


def call(kernel, outs, specs, out_specs, scratch=(), work=0):
    return pl.pallas_call(
        kernel,
        out_shape=outs,
        in_specs=specs,
        out_specs=out_specs,
        scratch_shapes=list(scratch),
        compiler_params=pltpu.CompilerParams(vmem_limit_bytes=28 * 1024 * 1024),
        cost_estimate=pl.CostEstimate(flops=0, bytes_accessed=work, transcendentals=0) if work else None,
    )


def shards(factor, pattern, owner, right_side):
    total = pattern.shape[1]
    vec = f32(RHS, ROWS)
    send_shape = f32(PEERS, SLOTS, 8, 128)
    part_shape = f32(2 * PLACES, 8, 128)
    me = lax.axis_index("y").astype(jnp.int32).reshape(1)
    canonical = [pltpu.VMEM((2 * RHS, THIRD), jnp.bfloat16)]

    def pair(*shape):
        return (jax.ShapeDtypeStruct(shape, jnp.bfloat16),) * 2

    pieces = call(
        split_kernel,
        (f32(2, ROWS, HALF),) * 3,
        [SMEM, SMEM, HBM],
        (HBM,) * 3,
        [pltpu.SemaphoreType.DMA((18,))],
    )(owner, me, factor)

    first, _ = over_planes(pieces[0])
    late = swap(pieces[0][0, :8, :128])
    send, below = call(
        start_kernel,
        (f32(PEERS, SLOTS + 1, 8, 128), jax.ShapeDtypeStruct((SLOTS, 1, total * BLOCK), jnp.int32)),
        [SMEM, SMEM, VMEM, VMEM],
        (VMEM, VMEM),
    )(owner, pattern, right_side, late)

    mine = exchange(send)
    other = swap(mine)
    mine, other = (v.reshape(PEERS * (SLOTS + 1), 8, 128) for v in (mine, other))
    meta = call(
        names_kernel,
        jax.ShapeDtypeStruct((META,), jnp.int32),
        [SMEM, SMEM, VMEM, VMEM],
        SMEM,
        [
            pltpu.VMEM((2 * PEERS, 128), jnp.int32),
            pltpu.SMEM((2 * PEERS, 128), jnp.int32),
            pltpu.SemaphoreType.DMA((1,)),
        ],
    )(owner, me, mine, other)

    def place(kernel, outs, parts, work):
        given = [v for own, after, opposite, before in parts for v in (own, after, *opposite, before)]
        return call(
            kernel, outs, [SMEM, VMEM] + [VMEM] * len(given), (VMEM,) * len(outs), work=work
        )(meta, below, *given)

    d2 = place(place_leaves_kernel, pair(ROWS, 1024), [first], 2 << 20)
    piece, _ = lax.optimization_barrier((pieces[1], first[2]))
    second, _ = over_planes(piece)

    y2, send = call(
        leaves_kernel, (vec, send_shape), [SMEM] + [VMEM] * 5, (VMEM, VMEM), canonical
    )(meta, right_side, mine, other, *d2)
    mine2, other2 = gather(send)
    middles = place(place_middles_kernel, pair(ROWS, 2048) * 2, [first, second], 8 << 20)
    r1, send = call(
        middle_resid_kernel, (vec, send_shape), [SMEM] + [VMEM] * 5, (VMEM, VMEM), canonical
    )(meta, right_side, mine2, other2, *middles[:2])
    piece, r1 = lax.optimization_barrier((pieces[2], r1))
    third, (mine, other) = over_planes(piece, gather(send))
    y1, send = call(
        middle_kernel, (vec, send_shape), [SMEM] + [VMEM] * 5, (VMEM, VMEM), canonical
    )(meta, r1, mine, other, *middles[2:])
    mine, other = gather(send)
    m = place(place_all_kernel, pair(3, ROWS, THIRD), [first, second, third], 24 << 20)
    upd = call(
        update_kernel, f32(ROWS, RHS), [SMEM] + [VMEM] * 4, VMEM, canonical, 4 << 20
    )(meta, mine2, other2, *m)
    r0, send = call(
        top_resid_kernel, (vec, send_shape), [SMEM] + [VMEM] * 6, (VMEM, VMEM), canonical
    )(meta, right_side, upd, mine, other, *m)
    mine, other = gather(send)
    y0, part = call(
        top_kernel, (vec, part_shape), [SMEM] + [VMEM] * 5, (VMEM, VMEM), canonical
    )(meta, r0, mine, other, *m)

    def adds(level, *terms):
        return call(
            functools.partial(add_kernel, level),
            (vec, part_shape),
            [SMEM] + [VMEM] * (len(terms) + 2),
            (VMEM, VMEM),
        )(meta, *terms, *m)

    def subs(level, y, got):
        return call(
            functools.partial(sub_kernel, level),
            (vec, part_shape),
            [SMEM] + [VMEM] * 4,
            (VMEM, VMEM),
        )(meta, y, got, *m)

    x0, part = adds(1, y0, reduce(part))
    t1, part = subs(1, y1, reduce(part))
    x01, part = adds(2, t1, x0, reduce(part))
    t2, part = subs(2, y2, reduce(part))
    return call(last_kernel, vec, [VMEM] * 3, VMEM)(t2, x01, reduce(part))


def solution(mesh):
    fine = Mesh(mesh.devices.reshape(4, 8, 2, 4), ("x", "z", "c", "y"))
    rows = ("x", "z", "c")
    in_specs = (P(rows, "y"), P(rows, None), P(rows), P("y", rows))
    out_specs = P("y", rows)
    return jax.shard_map(shards, mesh=fine, in_specs=in_specs, out_specs=out_specs, check_vma=False)
```

```python
import functools

import jax
import jax.numpy as jnp
from jax import lax
from jax.experimental import pallas as pl
from jax.experimental.pallas import tpu as pltpu
from jax.sharding import Mesh, PartitionSpec as P

BLOCK = 64
RHS = 16
SLOTS = 3
ROWS = SLOTS * BLOCK
THIRD = 4096
PEERS = 32
PLACES = PEERS * SLOTS
PART = 1024
OWN = 192
ME = OWN + SLOTS
META = 200
HALF = 512
VMEM = pl.BlockSpec(memory_space=pltpu.VMEM)
SMEM = pl.BlockSpec(memory_space=pltpu.SMEM)
HBM = pl.BlockSpec(memory_space=pltpu.HBM)
CHIPS = ("x", "z")


def f32(*shape):
    return jax.ShapeDtypeStruct(shape, jnp.float32)


def left_half():
    return lax.broadcasted_iota(jnp.int32, (8, 128), 1) < BLOCK


def pack(rows):
    return [
        jnp.concatenate(
            [rows[:8, s * BLOCK : (s + 1) * BLOCK], rows[8:, s * BLOCK : (s + 1) * BLOCK]], axis=1
        )
        for s in range(SLOTS)
    ]


def unpack(tiles):
    upper = jnp.concatenate([t[:, :BLOCK] for t in tiles], axis=1)
    lower = jnp.concatenate([t[:, BLOCK:] for t in tiles], axis=1)
    return jnp.concatenate([upper, lower], axis=0)


def only(meta_ref, level, rows):
    slot = lax.broadcasted_iota(jnp.int32, rows.shape, 1) // BLOCK
    keep = jnp.zeros(rows.shape, jnp.bool_)
    for s in range(SLOTS):
        g = meta_ref[OWN + s]
        here = (g >= (2 - level) * 64) & (g < (3 - level) * 64)
        keep = keep | ((slot == s) & here)
    return jnp.where(keep, rows, 0.0)


def halves(x):
    high = x.astype(jnp.bfloat16)
    return high, (x - high.astype(jnp.float32)).astype(jnp.bfloat16)


def to_canonical(meta_ref, level, mine_ref, other_ref, x_ref, extra=False):
    base = (2 - level) * 64
    half = left_half()

    def tile(place):
        near = jnp.minimum(place, PLACES - 1)
        far = jnp.maximum(place, PLACES) - PLACES
        if extra:
            near, far = near + near // SLOTS, far + far // SLOTS
        return jnp.where(place >= PLACES, other_ref[far], mine_ref[near])

    for t in range(32):
        a = tile(meta_ref[base + 2 * t])
        b = tile(meta_ref[base + 2 * t + 1])
        top = jnp.where(half, a, pltpu.roll(b, BLOCK, 1))
        bottom = jnp.where(half, pltpu.roll(a, BLOCK, 1), b)
        high, low = halves(jnp.concatenate([top, bottom], axis=0))
        x_ref[0:16, 128 * t : 128 * (t + 1)] = high
        x_ref[16:32, 128 * t : 128 * (t + 1)] = low


def to_places(meta_ref, level, x, out_ref):
    base = (2 - level) * 64
    half = left_half()
    out_ref[...] = jnp.zeros_like(out_ref)
    for t in range(32):
        top = x[0:8, 128 * t : 128 * (t + 1)]
        bottom = x[8:16, 128 * t : 128 * (t + 1)]
        out_ref[meta_ref[base + 2 * t]] = jnp.where(half, top, pltpu.roll(bottom, BLOCK, 1))
        out_ref[meta_ref[base + 2 * t + 1]] = jnp.where(half, pltpu.roll(top, BLOCK, 1), bottom)


def times_rows(x, high, low):
    dims = (((1,), (1,)), ((), ()))
    one = lax.dot_general(high, x, dims, preferred_element_type=jnp.float32)
    two = lax.dot_general(low, x[:RHS], dims, preferred_element_type=jnp.float32)
    return one[:, :RHS] + one[:, RHS:] + two


def times_cols(x, high, low):
    dims = (((1,), (0,)), ((), ()))
    x_high, x_low = halves(x)
    both = jnp.concatenate([x_high, x_low], axis=0)
    one = lax.dot_general(both, high, dims, preferred_element_type=jnp.float32)
    two = lax.dot_general(x_high, low, dims, preferred_element_type=jnp.float32)
    return one[:RHS] + one[RHS:] + two


def spread(tiles, send_ref):
    for peer in range(PEERS):
        for s in range(SLOTS):
            send_ref[peer, s] = tiles[s]


def arrived(got_ref):
    return unpack([jnp.sum(got_ref[:, s], axis=0) for s in range(SLOTS)])


def start_kernel(own_ref, pattern_ref, b_ref, after_ref, send_ref, below_ref):
    tiles = pack(b_ref[...])
    lane = lax.broadcasted_iota(jnp.int32, (8, 128), 1)
    names = jnp.zeros((8, 128), jnp.float32)
    for s in range(SLOTS):
        names = jnp.where(lane == s, own_ref[s].astype(jnp.float32), names)
    spread(tiles, send_ref)
    for peer in range(PEERS):
        send_ref[peer, SLOTS] = names
    lane = lax.broadcasted_iota(jnp.int32, (1, 128), 1)
    for s in range(SLOTS):
        for part in range(12):
            state = state_of(own_ref[s], part)
            for t in range(PART // 128):
                at = part * (PART // BLOCK) + 2 * t
                keep = [
                    jnp.where((state == 1) & (pattern_ref[s, at + i] > 0), -1, 1 << 20)
                    for i in range(2)
                ]
                col = part * PART + t * 128 + lane
                rest = jnp.where(lane < BLOCK, keep[0], keep[1])
                below_ref[s, :, part * PART + t * 128 : part * PART + (t + 1) * 128] = jnp.where(
                    state == 2, col, rest
                )


def names_kernel(own_ref, me_ref, mine_ref, other_ref, meta_ref, names_ref, order_ref, sem):
    row = lax.broadcasted_iota(jnp.int32, (8, 128), 0)
    for far, ref in enumerate((mine_ref, other_ref)):
        for k in range(PEERS // 8):
            names = ref[(SLOTS + 1) * 8 * k + SLOTS]
            for r in range(1, 8):
                names = jnp.where(row == r, ref[(SLOTS + 1) * (8 * k + r) + SLOTS], names)
            at = far * PEERS + 8 * k
            names_ref[at : at + 8] = names.astype(jnp.int32)
    copy = pltpu.make_async_copy(names_ref, order_ref, sem.at[0])
    copy.start()
    copy.wait()
    for chip in range(2 * PEERS):
        for s in range(SLOTS):
            meta_ref[order_ref[chip, s]] = chip * SLOTS + s
    for s in range(SLOTS):
        meta_ref[OWN + s] = own_ref[s]
    meta_ref[ME] = me_ref[0]
    for i in range(ME + 1, META):
        meta_ref[i] = 0


def turn(g, q):
    leaf = jnp.where(g // 16 == 3, 0, g // 16)
    first = jnp.where(q == 1, 1, 0)
    second = jnp.where(q == 0, 2, 0)
    return jnp.where(g < 64, leaf, jnp.where(g < 96, first, jnp.where(g < 128, second, 0)))


def part_of(e, g, q):
    return 3 * q + lax.rem(e + turn(g, q), 3)


def rows_of(s):
    return slice(s * BLOCK, (s + 1) * BLOCK)


def split_kernel(own_ref, me_ref, factor_ref, *refs):
    first, second, third_a, third_b, sems = refs
    copies = []
    for e in range(3):
        for s in range(SLOTS):
            at = lax.rem(e + turn(own_ref[s], me_ref[0]), 3) * PART
            for h in range(2):
                out = (third_a, third_b)[h] if e == 2 else (first, second)[e].at[h]
                copies.append(
                    pltpu.make_async_copy(
                        factor_ref.at[rows_of(s), pl.ds(pl.multiple_of(at + h * HALF, HALF), HALF)],
                        out.at[rows_of(s)],
                        sems.at[len(copies)],
                    )
                )
    for copy in copies:
        copy.start()
    for copy in copies:
        copy.wait()


def state_of(g, part):
    group = (g - 64) // 32
    leaf = jnp.where(part == g // 16, 2, 0)
    own = (part == 4 + 2 * group) | (part == 5 + 2 * group)
    below = (part == 2 * group) | (part == 2 * group + 1)
    middle = jnp.where(own, 2, jnp.where(below, 1, 0))
    return jnp.where(g < 64, leaf, jnp.where(g < 128, middle, jnp.where(part >= 8, 2, 1)))


def masked(below_ref, s, g, part, h, block):
    row = g * BLOCK + lax.broadcasted_iota(jnp.int32, (BLOCK, HALF), 0)
    col0 = pl.multiple_of(part * PART + h * HALF, HALF)
    return halves(jnp.where(row > below_ref[s, :, pl.ds(col0, HALF)], block, 0.0))


def sources(e, meta_ref, refs):
    for d in range(4):
        q = lax.rem(meta_ref[ME] + d, 4)
        for s in range(SLOTS):
            g = meta_ref[OWN + s]
            for h in range(2):
                if e == 2:
                    src = refs[2 * d + h].at[rows_of(s)]
                elif d == 2:
                    src = refs[2 + h].at[rows_of(s)]
                else:
                    src = refs[(0, 1, 0, 4)[d]].at[h, rows_of(s)]
                yield s, h, g, part_of(e, g, q), src


def put(refs, s, at, pair):
    for ref, value in zip(refs, pair):
        ref[rows_of(s), pl.ds(pl.multiple_of(at, HALF), HALF)] = value


def place_leaves_kernel(meta_ref, below_ref, *refs):
    for s, h, g, part, src in sources(0, meta_ref, refs[:5]):

        @pl.when((g < 64) & (part == g // 16))
        def _(s=s, h=h, g=g, part=part, src=src):
            put(refs[5:7], s, h * HALF, masked(below_ref, s, g, part, h, src[...]))


def place_middles_kernel(meta_ref, below_ref, *refs):
    for e in range(2):
        for s, h, g, part, src in sources(e, meta_ref, refs[5 * e : 5 * e + 5]):
            mine = (g >= 64) & (g < 128) & (state_of(g, part) > 0)
            at = lax.rem(part, 2) * PART + h * HALF

            @pl.when(mine & (part < 4))
            def _(s=s, h=h, g=g, part=part, src=src, at=at):
                put(refs[10:12], s, at, masked(below_ref, s, g, part, h, src[...]))

            @pl.when(mine & (part >= 4))
            def _(s=s, h=h, g=g, part=part, src=src, at=at):
                put(refs[12:14], s, at, masked(below_ref, s, g, part, h, src[...]))


def place_all_kernel(meta_ref, below_ref, *refs):
    for e in range(3):
        for s, h, g, part, src in sources(e, meta_ref, refs[5 * e : (5, 10, 18)[e]]):
            at = lax.rem(part, 4) * PART + h * HALF
            outs = [ref.at[part // 4] for ref in refs[18:20]]
            put(outs, s, at, masked(below_ref, s, g, part, h, src[...]))


def own_products(meta_ref, base, blocks, groups, x_ref, high_ref, low_ref):
    wide = high_ref.shape[1]
    outs = []
    for s in range(SLOTS):
        group = jnp.clip((meta_ref[OWN + s] - base) // blocks, 0, groups - 1)
        x = x_ref[:, pl.ds(pl.multiple_of(group * wide, wide), wide)]
        outs.append(times_rows(x, high_ref[rows_of(s)], low_ref[rows_of(s)]))
    return jnp.concatenate(outs, axis=0).T


def leaves_kernel(meta_ref, b_ref, mine_ref, other_ref, high_ref, low_ref, y_ref, send_ref, x_ref):
    to_canonical(meta_ref, 2, mine_ref, other_ref, x_ref, True)
    y = only(meta_ref, 2, own_products(meta_ref, 0, 16, 4, x_ref, high_ref, low_ref) + b_ref[...])
    y_ref[...] = y
    spread(pack(y), send_ref)


def middle_resid_kernel(meta_ref, b_ref, mine_ref, other_ref, high_ref, low_ref, r_ref, send_ref, x_ref):
    to_canonical(meta_ref, 2, mine_ref, other_ref, x_ref)
    r = only(meta_ref, 1, b_ref[...] - own_products(meta_ref, 64, 32, 2, x_ref, high_ref, low_ref))
    r_ref[...] = r
    spread(pack(r), send_ref)


def middle_kernel(meta_ref, r_ref, mine_ref, other_ref, high_ref, low_ref, y_ref, send_ref, x_ref):
    to_canonical(meta_ref, 1, mine_ref, other_ref, x_ref)
    y = only(meta_ref, 1, own_products(meta_ref, 64, 32, 2, x_ref, high_ref, low_ref) + r_ref[...])
    y_ref[...] = y
    spread(pack(y), send_ref)


def update_kernel(meta_ref, mine_ref, other_ref, high_ref, low_ref, upd_ref, x_ref):
    to_canonical(meta_ref, 2, mine_ref, other_ref, x_ref)
    upd_ref[...] = times_rows(x_ref[...], high_ref[0], low_ref[0])


def top_resid_kernel(meta_ref, b_ref, upd_ref, mine_ref, other_ref, high_ref, low_ref, r_ref, send_ref, x_ref):
    to_canonical(meta_ref, 1, mine_ref, other_ref, x_ref)
    upd = upd_ref[...] + times_rows(x_ref[...], high_ref[1], low_ref[1])
    r = only(meta_ref, 0, b_ref[...] - upd.T)
    r_ref[...] = r
    spread(pack(r), send_ref)


def top_kernel(meta_ref, r_ref, mine_ref, other_ref, high_ref, low_ref, y_ref, part_ref, x_ref):
    to_canonical(meta_ref, 0, mine_ref, other_ref, x_ref)
    y = only(meta_ref, 0, times_rows(x_ref[...], high_ref[2], low_ref[2]).T) + r_ref[...]
    y_ref[...] = y
    to_places(meta_ref, 0, times_cols(y, high_ref[2], low_ref[2]), part_ref)


def add_kernel(level, meta_ref, *refs):
    terms = refs[:-5]
    got_ref, high_ref, low_ref, x_out_ref, part_ref = refs[-5:]
    x = arrived(got_ref)
    for term in terms:
        x = x + term[...]
    x_out_ref[...] = x
    to_places(meta_ref, level, times_cols(x, high_ref[2 - level], low_ref[2 - level]), part_ref)


def sub_kernel(level, meta_ref, y_ref, got_ref, high_ref, low_ref, t_ref, part_ref):
    t = only(meta_ref, level, y_ref[...] - arrived(got_ref))
    t_ref[...] = t
    to_places(meta_ref, level, times_cols(t, high_ref[2 - level], low_ref[2 - level]), part_ref)


def last_kernel(t_ref, x_ref, got_ref, out_ref):
    out_ref[...] = t_ref[...] + x_ref[...] + arrived(got_ref)


def swap(x):
    return lax.ppermute(x, "c", [(0, 1), (1, 0)])


def exchange(x):
    return lax.all_to_all(x, CHIPS, 0, 0)


def gather(send):
    mine = exchange(send)
    other = swap(mine)
    return mine.reshape(PLACES, 8, 128), other.reshape(PLACES, 8, 128)


def reduce(part):
    far = swap(part[PLACES:])
    return exchange((part[:PLACES] + far).reshape(PEERS, SLOTS, 8, 128))


def around(x, step):
    return lax.ppermute(x, "y", [(i, (i + step) % 4) for i in range(4)])


def over_planes(part, tie=None):
    before, after = around(part, 1), around(part, -1)
    if tie is not None:
        before, after, tie = lax.optimization_barrier((before, after, tie))
    else:
        before, after = lax.optimization_barrier((before, after))
    opposite = [around(before[0], 1), around(after[1], -1)]
    return (part, after, opposite, before), tie


def call(kernel, outs, specs, out_specs, scratch=(), work=0):
    return pl.pallas_call(
        kernel,
        out_shape=outs,
        in_specs=specs,
        out_specs=out_specs,
        scratch_shapes=list(scratch),
        compiler_params=pltpu.CompilerParams(vmem_limit_bytes=28 * 1024 * 1024),
        cost_estimate=pl.CostEstimate(flops=0, bytes_accessed=work, transcendentals=0) if work else None,
    )


def shards(factor, pattern, owner, right_side):
    total = pattern.shape[1]
    vec = f32(RHS, ROWS)
    send_shape = f32(PEERS, SLOTS, 8, 128)
    part_shape = f32(2 * PLACES, 8, 128)
    me = lax.axis_index("y").astype(jnp.int32).reshape(1)
    canonical = [pltpu.VMEM((2 * RHS, THIRD), jnp.bfloat16)]

    def pair(*shape):
        return (jax.ShapeDtypeStruct(shape, jnp.bfloat16),) * 2

    pieces = call(
        split_kernel,
        (f32(2, ROWS, HALF),) * 2 + (f32(ROWS, HALF),) * 2,
        [SMEM, SMEM, HBM],
        (HBM,) * 4,
        [pltpu.SemaphoreType.DMA((18,))],
    )(owner, me, factor)

    first, _ = over_planes(pieces[0])
    late = swap(pieces[0][0, :8, :128])
    send, below = call(
        start_kernel,
        (f32(PEERS, SLOTS + 1, 8, 128), jax.ShapeDtypeStruct((SLOTS, 1, total * BLOCK), jnp.int32)),
        [SMEM, SMEM, VMEM, VMEM],
        (VMEM, VMEM),
    )(owner, pattern, right_side, late)

    mine = exchange(send)
    other = swap(mine)
    mine, other = (v.reshape(PEERS * (SLOTS + 1), 8, 128) for v in (mine, other))
    meta = call(
        names_kernel,
        jax.ShapeDtypeStruct((META,), jnp.int32),
        [SMEM, SMEM, VMEM, VMEM],
        SMEM,
        [
            pltpu.VMEM((2 * PEERS, 128), jnp.int32),
            pltpu.SMEM((2 * PEERS, 128), jnp.int32),
            pltpu.SemaphoreType.DMA((1,)),
        ],
    )(owner, me, mine, other)

    def place(kernel, outs, parts, work):
        given = [v for own, after, opposite, before in parts for v in (own, after, *opposite, before)]
        given += third if kernel is place_all_kernel else []
        return call(
            kernel, outs, [SMEM, VMEM] + [VMEM] * len(given), (VMEM,) * len(outs), work=work
        )(meta, below, *given)

    d2 = place(place_leaves_kernel, pair(ROWS, 1024), [first], 2 << 20)
    piece, _ = lax.optimization_barrier((pieces[1], first[2]))
    second, _ = over_planes(piece)

    y2, send = call(
        leaves_kernel, (vec, send_shape), [SMEM] + [VMEM] * 5, (VMEM, VMEM), canonical
    )(meta, right_side, mine, other, *d2)
    mine2, other2 = gather(send)
    middles = place(place_middles_kernel, pair(ROWS, 2048) * 2, [first, second], 8 << 20)
    r1, send = call(
        middle_resid_kernel, (vec, send_shape), [SMEM] + [VMEM] * 5, (VMEM, VMEM), canonical
    )(meta, right_side, mine2, other2, *middles[:2])
    (low, high), _ = lax.optimization_barrier((pieces[2:], (second[1], second[3])))
    before_low, after_high = around(low, 1), around(high, -1)
    before_low, after_high, send = lax.optimization_barrier((before_low, after_high, send))
    (low, high), r1 = lax.optimization_barrier((pieces[2:], r1))
    before_high, after_low = around(high, 1), around(low, -1)
    relayed = [around(before_low, 1), around(after_high, -1)]
    mine, other = gather(send)
    y1, send = call(
        middle_kernel, (vec, send_shape), [SMEM] + [VMEM] * 5, (VMEM, VMEM), canonical
    )(meta, r1, mine, other, *middles[2:])
    before_high, after_low, relayed, send = lax.optimization_barrier(
        (before_high, after_low, relayed, send)
    )
    third = [*pieces[2:], after_low, after_high, *relayed, before_low, before_high]
    mine, other = gather(send)
    m = place(place_all_kernel, pair(3, ROWS, THIRD), [first, second], 24 << 20)
    upd = call(
        update_kernel, f32(ROWS, RHS), [SMEM] + [VMEM] * 4, VMEM, canonical, 4 << 20
    )(meta, mine2, other2, *m)
    r0, send = call(
        top_resid_kernel, (vec, send_shape), [SMEM] + [VMEM] * 6, (VMEM, VMEM), canonical
    )(meta, right_side, upd, mine, other, *m)
    mine, other = gather(send)
    y0, part = call(
        top_kernel, (vec, part_shape), [SMEM] + [VMEM] * 5, (VMEM, VMEM), canonical
    )(meta, r0, mine, other, *m)

    def adds(level, *terms):
        return call(
            functools.partial(add_kernel, level),
            (vec, part_shape),
            [SMEM] + [VMEM] * (len(terms) + 2),
            (VMEM, VMEM),
        )(meta, *terms, *m)

    def subs(level, y, got):
        return call(
            functools.partial(sub_kernel, level),
            (vec, part_shape),
            [SMEM] + [VMEM] * 4,
            (VMEM, VMEM),
        )(meta, y, got, *m)

    x0, part = adds(1, y0, reduce(part))
    t1, part = subs(1, y1, reduce(part))
    x01, part = adds(2, t1, x0, reduce(part))
    t2, part = subs(2, y2, reduce(part))
    return call(last_kernel, vec, [VMEM] * 3, VMEM)(t2, x01, reduce(part))


def solution(mesh):
    fine = Mesh(mesh.devices.reshape(4, 8, 2, 4), ("x", "z", "c", "y"))
    rows = ("x", "z", "c")
    in_specs = (P(rows, "y"), P(rows, None), P(rows), P("y", rows))
    out_specs = P("y", rows)
    return jax.shard_map(shards, mesh=fine, in_specs=in_specs, out_specs=out_specs, check_vma=False)
```

```python
import functools

import jax
import jax.numpy as jnp
from jax import lax
from jax.experimental import pallas as pl
from jax.experimental.pallas import tpu as pltpu
from jax.sharding import Mesh, PartitionSpec as P

BLOCK = 64
RHS = 16
SLOTS = 3
ROWS = SLOTS * BLOCK
THIRD = 4096
PEERS = 32
PLACES = PEERS * SLOTS
PART = 1024
OWN = 192
ME = OWN + SLOTS
COLUMN = ME + 1
META = 200
HALF = 512
VMEM = pl.BlockSpec(memory_space=pltpu.VMEM)
SMEM = pl.BlockSpec(memory_space=pltpu.SMEM)
HBM = pl.BlockSpec(memory_space=pltpu.HBM)
CHIPS = ("x", "z")


def f32(*shape):
    return jax.ShapeDtypeStruct(shape, jnp.float32)


def left_half():
    return lax.broadcasted_iota(jnp.int32, (8, 128), 1) < BLOCK


def pack(rows):
    return [
        jnp.concatenate(
            [rows[:8, s * BLOCK : (s + 1) * BLOCK], rows[8:, s * BLOCK : (s + 1) * BLOCK]], axis=1
        )
        for s in range(SLOTS)
    ]


def unpack(tiles):
    upper = jnp.concatenate([t[:, :BLOCK] for t in tiles], axis=1)
    lower = jnp.concatenate([t[:, BLOCK:] for t in tiles], axis=1)
    return jnp.concatenate([upper, lower], axis=0)


def only(meta_ref, level, rows):
    slot = lax.broadcasted_iota(jnp.int32, rows.shape, 1) // BLOCK
    keep = jnp.zeros(rows.shape, jnp.bool_)
    for s in range(SLOTS):
        g = meta_ref[OWN + s]
        here = (g >= (2 - level) * 64) & (g < (3 - level) * 64)
        keep = keep | ((slot == s) & here)
    return jnp.where(keep, rows, 0.0)


def halves(x):
    high = x.astype(jnp.bfloat16)
    return high, (x - high.astype(jnp.float32)).astype(jnp.bfloat16)


def to_canonical(meta_ref, level, mine_ref, other_ref, x_ref, extra=False, relative=False):
    base = (2 - level) * 64
    half = left_half()

    def tile(place):
        near = jnp.minimum(place, PLACES - 1)
        far = jnp.maximum(place, PLACES) - PLACES
        if extra:
            near, far = near + near // SLOTS, far + far // SLOTS
        if relative:
            line = PLACES // 4

            def back(at):
                return lax.rem(meta_ref[COLUMN] + 4 - at // line, 4) * line + lax.rem(at, line)

            near, far = back(near), back(far)
        return jnp.where(place >= PLACES, other_ref[far], mine_ref[near])

    for t in range(32):
        a = tile(meta_ref[base + 2 * t])
        b = tile(meta_ref[base + 2 * t + 1])
        top = jnp.where(half, a, pltpu.roll(b, BLOCK, 1))
        bottom = jnp.where(half, pltpu.roll(a, BLOCK, 1), b)
        high, low = halves(jnp.concatenate([top, bottom], axis=0))
        x_ref[0:16, 128 * t : 128 * (t + 1)] = high
        x_ref[16:32, 128 * t : 128 * (t + 1)] = low


def to_places(meta_ref, level, x, out_ref):
    base = (2 - level) * 64
    half = left_half()
    out_ref[...] = jnp.zeros_like(out_ref)
    for t in range(32):
        top = x[0:8, 128 * t : 128 * (t + 1)]
        bottom = x[8:16, 128 * t : 128 * (t + 1)]
        out_ref[meta_ref[base + 2 * t]] = jnp.where(half, top, pltpu.roll(bottom, BLOCK, 1))
        out_ref[meta_ref[base + 2 * t + 1]] = jnp.where(half, pltpu.roll(top, BLOCK, 1), bottom)


def times_rows(x, high, low):
    dims = (((1,), (1,)), ((), ()))
    one = lax.dot_general(high, x, dims, preferred_element_type=jnp.float32)
    two = lax.dot_general(low, x[:RHS], dims, preferred_element_type=jnp.float32)
    return one[:, :RHS] + one[:, RHS:] + two


def times_cols(x, high, low):
    dims = (((1,), (0,)), ((), ()))
    x_high, x_low = halves(x)
    both = jnp.concatenate([x_high, x_low], axis=0)
    one = lax.dot_general(both, high, dims, preferred_element_type=jnp.float32)
    two = lax.dot_general(x_high, low, dims, preferred_element_type=jnp.float32)
    return one[:RHS] + one[RHS:] + two


def spread(tiles, send_ref):
    for peer in range(send_ref.shape[0]):
        for s in range(SLOTS):
            send_ref[peer, s] = tiles[s]


def arrived(got_ref):
    return unpack([jnp.sum(got_ref[:, s], axis=0) for s in range(SLOTS)])


def start_kernel(own_ref, pattern_ref, b_ref, after_ref, send_ref, below_ref):
    tiles = pack(b_ref[...])
    lane = lax.broadcasted_iota(jnp.int32, (8, 128), 1)
    names = jnp.zeros((8, 128), jnp.float32)
    for s in range(SLOTS):
        names = jnp.where(lane == s, own_ref[s].astype(jnp.float32), names)
    spread(tiles, send_ref)
    for peer in range(PEERS):
        send_ref[peer, SLOTS] = names
    lane = lax.broadcasted_iota(jnp.int32, (1, 128), 1)
    for s in range(SLOTS):
        for part in range(12):
            state = state_of(own_ref[s], part)
            for t in range(PART // 128):
                at = part * (PART // BLOCK) + 2 * t
                keep = [
                    jnp.where((state == 1) & (pattern_ref[s, at + i] > 0), -1, 1 << 20)
                    for i in range(2)
                ]
                col = part * PART + t * 128 + lane
                rest = jnp.where(lane < BLOCK, keep[0], keep[1])
                below_ref[s, :, part * PART + t * 128 : part * PART + (t + 1) * 128] = jnp.where(
                    state == 2, col, rest
                )


def names_kernel(own_ref, me_ref, mine_ref, other_ref, meta_ref, names_ref, order_ref, sem):
    row = lax.broadcasted_iota(jnp.int32, (8, 128), 0)
    for far, ref in enumerate((mine_ref, other_ref)):
        for k in range(PEERS // 8):
            names = ref[(SLOTS + 1) * 8 * k + SLOTS]
            for r in range(1, 8):
                names = jnp.where(row == r, ref[(SLOTS + 1) * (8 * k + r) + SLOTS], names)
            at = far * PEERS + 8 * k
            names_ref[at : at + 8] = names.astype(jnp.int32)
    copy = pltpu.make_async_copy(names_ref, order_ref, sem.at[0])
    copy.start()
    copy.wait()
    for chip in range(2 * PEERS):
        for s in range(SLOTS):
            meta_ref[order_ref[chip, s]] = chip * SLOTS + s
    for s in range(SLOTS):
        meta_ref[OWN + s] = own_ref[s]
    meta_ref[ME] = me_ref[0]
    meta_ref[COLUMN] = me_ref[1]
    for i in range(COLUMN + 1, META):
        meta_ref[i] = 0


def turn(g, q):
    leaf = jnp.where(g // 16 == 3, 0, g // 16)
    first = jnp.where(q == 1, 1, 0)
    second = jnp.where(q == 0, 2, 0)
    return jnp.where(g < 64, leaf, jnp.where(g < 96, first, jnp.where(g < 128, second, 0)))


def part_of(e, g, q):
    return 3 * q + lax.rem(e + turn(g, q), 3)


def rows_of(s):
    return slice(s * BLOCK, (s + 1) * BLOCK)


def split_kernel(own_ref, me_ref, factor_ref, *refs):
    first, second, third_a, third_b, sems = refs
    copies = []
    for e in range(3):
        for s in range(SLOTS):
            at = lax.rem(e + turn(own_ref[s], me_ref[0]), 3) * PART
            for h in range(2):
                out = (third_a, third_b)[h] if e == 2 else (first, second)[e].at[h]
                copies.append(
                    pltpu.make_async_copy(
                        factor_ref.at[rows_of(s), pl.ds(pl.multiple_of(at + h * HALF, HALF), HALF)],
                        out.at[rows_of(s)],
                        sems.at[len(copies)],
                    )
                )
    for copy in copies:
        copy.start()
    for copy in copies:
        copy.wait()


def state_of(g, part):
    group = (g - 64) // 32
    leaf = jnp.where(part == g // 16, 2, 0)
    own = (part == 4 + 2 * group) | (part == 5 + 2 * group)
    below = (part == 2 * group) | (part == 2 * group + 1)
    middle = jnp.where(own, 2, jnp.where(below, 1, 0))
    return jnp.where(g < 64, leaf, jnp.where(g < 128, middle, jnp.where(part >= 8, 2, 1)))


def masked(below_ref, s, g, part, h, block):
    row = g * BLOCK + lax.broadcasted_iota(jnp.int32, (BLOCK, HALF), 0)
    col0 = pl.multiple_of(part * PART + h * HALF, HALF)
    return halves(jnp.where(row > below_ref[s, :, pl.ds(col0, HALF)], block, 0.0))


def sources(e, meta_ref, refs):
    for d in range(4):
        q = lax.rem(meta_ref[ME] + d, 4)
        for s in range(SLOTS):
            g = meta_ref[OWN + s]
            for h in range(2):
                if e == 2:
                    src = refs[2 * d + h].at[rows_of(s)]
                elif d == 2:
                    src = refs[2 + h].at[rows_of(s)]
                else:
                    src = refs[(0, 1, 0, 4)[d]].at[h, rows_of(s)]
                yield s, h, g, part_of(e, g, q), src


def put(refs, s, at, pair):
    for ref, value in zip(refs, pair):
        ref[rows_of(s), pl.ds(pl.multiple_of(at, HALF), HALF)] = value


def place_leaves_kernel(meta_ref, below_ref, *refs):
    for s, h, g, part, src in sources(0, meta_ref, refs[:5]):

        @pl.when((g < 64) & (part == g // 16))
        def _(s=s, h=h, g=g, part=part, src=src):
            put(refs[5:7], s, h * HALF, masked(below_ref, s, g, part, h, src[...]))


def place_middles_kernel(meta_ref, below_ref, *refs):
    for e in range(2):
        for s, h, g, part, src in sources(e, meta_ref, refs[5 * e : 5 * e + 5]):
            mine = (g >= 64) & (g < 128) & (state_of(g, part) > 0)
            at = lax.rem(part, 2) * PART + h * HALF

            @pl.when(mine & (part < 4))
            def _(s=s, h=h, g=g, part=part, src=src, at=at):
                put(refs[10:12], s, at, masked(below_ref, s, g, part, h, src[...]))

            @pl.when(mine & (part >= 4))
            def _(s=s, h=h, g=g, part=part, src=src, at=at):
                put(refs[12:14], s, at, masked(below_ref, s, g, part, h, src[...]))


def place_all_kernel(meta_ref, below_ref, *refs):
    for e in range(3):
        for s, h, g, part, src in sources(e, meta_ref, refs[5 * e : (5, 10, 18)[e]]):
            at = lax.rem(part, 4) * PART + h * HALF
            outs = [ref.at[part // 4] for ref in refs[18:20]]
            put(outs, s, at, masked(below_ref, s, g, part, h, src[...]))


def own_products(meta_ref, base, blocks, groups, x_ref, high_ref, low_ref):
    wide = high_ref.shape[1]
    outs = []
    for s in range(SLOTS):
        group = jnp.clip((meta_ref[OWN + s] - base) // blocks, 0, groups - 1)
        x = x_ref[:, pl.ds(pl.multiple_of(group * wide, wide), wide)]
        outs.append(times_rows(x, high_ref[rows_of(s)], low_ref[rows_of(s)]))
    return jnp.concatenate(outs, axis=0).T


def leaves_kernel(meta_ref, b_ref, mine_ref, other_ref, high_ref, low_ref, y_ref, send_ref, x_ref):
    to_canonical(meta_ref, 2, mine_ref, other_ref, x_ref, True)
    y = only(meta_ref, 2, own_products(meta_ref, 0, 16, 4, x_ref, high_ref, low_ref) + b_ref[...])
    y_ref[...] = y
    spread(pack(y), send_ref)


def middle_resid_kernel(meta_ref, b_ref, mine_ref, other_ref, high_ref, low_ref, r_ref, send_ref, x_ref):
    to_canonical(meta_ref, 2, mine_ref, other_ref, x_ref)
    r = only(meta_ref, 1, b_ref[...] - own_products(meta_ref, 64, 32, 2, x_ref, high_ref, low_ref))
    r_ref[...] = r
    spread(pack(r), send_ref)


def middle_kernel(meta_ref, r_ref, mine_ref, other_ref, high_ref, low_ref, y_ref, send_ref, x_ref):
    to_canonical(meta_ref, 1, mine_ref, other_ref, x_ref, relative=True)
    y = only(meta_ref, 1, own_products(meta_ref, 64, 32, 2, x_ref, high_ref, low_ref) + r_ref[...])
    y_ref[...] = y
    spread(pack(y), send_ref)


def update_kernel(meta_ref, mine_ref, other_ref, high_ref, low_ref, upd_ref, x_ref):
    to_canonical(meta_ref, 2, mine_ref, other_ref, x_ref)
    upd_ref[...] = times_rows(x_ref[...], high_ref[0], low_ref[0])


def top_resid_kernel(meta_ref, b_ref, upd_ref, mine_ref, other_ref, high_ref, low_ref, r_ref, send_ref, x_ref):
    to_canonical(meta_ref, 1, mine_ref, other_ref, x_ref)
    upd = upd_ref[...] + times_rows(x_ref[...], high_ref[1], low_ref[1])
    r = only(meta_ref, 0, b_ref[...] - upd.T)
    r_ref[...] = r
    spread(pack(r), send_ref)


def top_kernel(meta_ref, r_ref, mine_ref, other_ref, high_ref, low_ref, y_ref, part_ref, x_ref):
    to_canonical(meta_ref, 0, mine_ref, other_ref, x_ref)
    y = only(meta_ref, 0, times_rows(x_ref[...], high_ref[2], low_ref[2]).T) + r_ref[...]
    y_ref[...] = y
    to_places(meta_ref, 0, times_cols(y, high_ref[2], low_ref[2]), part_ref)


def add_kernel(level, meta_ref, *refs):
    terms = refs[:-5]
    got_ref, high_ref, low_ref, x_out_ref, part_ref = refs[-5:]
    x = arrived(got_ref)
    for term in terms:
        x = x + term[...]
    x_out_ref[...] = x
    to_places(meta_ref, level, times_cols(x, high_ref[2 - level], low_ref[2 - level]), part_ref)


def sub_kernel(level, meta_ref, y_ref, got_ref, high_ref, low_ref, t_ref, part_ref):
    t = only(meta_ref, level, y_ref[...] - arrived(got_ref))
    t_ref[...] = t
    to_places(meta_ref, level, times_cols(t, high_ref[2 - level], low_ref[2 - level]), part_ref)


def last_kernel(t_ref, x_ref, got_ref, out_ref):
    out_ref[...] = t_ref[...] + x_ref[...] + arrived(got_ref)


def swap(x):
    return lax.ppermute(x, "c", [(0, 1), (1, 0)])


def exchange(x):
    return lax.all_to_all(x, CHIPS, 0, 0)


def gather(send):
    mine = exchange(send)
    other = swap(mine)
    return mine.reshape(PLACES, 8, 128), other.reshape(PLACES, 8, 128)


def reduce(part):
    far = swap(part[PLACES:])
    return exchange((part[:PLACES] + far).reshape(PEERS, SLOTS, 8, 128))


def around(x, step):
    return lax.ppermute(x, "y", [(i, (i + step) % 4) for i in range(4)])


def over_planes(part, tie=None):
    before, after = around(part, 1), around(part, -1)
    if tie is not None:
        before, after, tie = lax.optimization_barrier((before, after, tie))
    else:
        before, after = lax.optimization_barrier((before, after))
    opposite = [around(before[0], 1), around(after[1], -1)]
    return (part, after, opposite, before), tie


def call(kernel, outs, specs, out_specs, scratch=(), work=0):
    return pl.pallas_call(
        kernel,
        out_shape=outs,
        in_specs=specs,
        out_specs=out_specs,
        scratch_shapes=list(scratch),
        compiler_params=pltpu.CompilerParams(vmem_limit_bytes=28 * 1024 * 1024),
        cost_estimate=pl.CostEstimate(flops=0, bytes_accessed=work, transcendentals=0) if work else None,
    )


def shards(factor, pattern, owner, right_side):
    total = pattern.shape[1]
    vec = f32(RHS, ROWS)
    send_shape = f32(PEERS, SLOTS, 8, 128)
    part_shape = f32(2 * PLACES, 8, 128)
    me = jnp.stack([lax.axis_index("y"), lax.axis_index("x")]).astype(jnp.int32)
    canonical = [pltpu.VMEM((2 * RHS, THIRD), jnp.bfloat16)]

    def pair(*shape):
        return (jax.ShapeDtypeStruct(shape, jnp.bfloat16),) * 2

    pieces = call(
        split_kernel,
        (f32(2, ROWS, HALF),) * 2 + (f32(ROWS, HALF),) * 2,
        [SMEM, SMEM, HBM],
        (HBM,) * 4,
        [pltpu.SemaphoreType.DMA((18,))],
    )(owner, me, factor)

    first, _ = over_planes(pieces[0])
    late = swap(pieces[0][0, :8, :128])
    send, below = call(
        start_kernel,
        (f32(PEERS, SLOTS + 1, 8, 128), jax.ShapeDtypeStruct((SLOTS, 1, total * BLOCK), jnp.int32)),
        [SMEM, SMEM, VMEM, VMEM],
        (VMEM, VMEM),
    )(owner, pattern, right_side, late)

    mine = exchange(send)
    other = swap(mine)
    mine, other = (v.reshape(PEERS * (SLOTS + 1), 8, 128) for v in (mine, other))
    meta = call(
        names_kernel,
        jax.ShapeDtypeStruct((META,), jnp.int32),
        [SMEM, SMEM, VMEM, VMEM],
        SMEM,
        [
            pltpu.VMEM((2 * PEERS, 128), jnp.int32),
            pltpu.SMEM((2 * PEERS, 128), jnp.int32),
            pltpu.SemaphoreType.DMA((1,)),
        ],
    )(owner, me, mine, other)

    def place(kernel, outs, parts, work):
        given = [v for own, after, opposite, before in parts for v in (own, after, *opposite, before)]
        given += third if kernel is place_all_kernel else []
        return call(
            kernel, outs, [SMEM, VMEM] + [VMEM] * len(given), (VMEM,) * len(outs), work=work
        )(meta, below, *given)

    d2 = place(place_leaves_kernel, pair(ROWS, 1024), [first], 2 << 20)
    piece, _ = lax.optimization_barrier((pieces[1], first[2]))
    second, _ = over_planes(piece)

    y2, send = call(
        leaves_kernel, (vec, send_shape), [SMEM] + [VMEM] * 5, (VMEM, VMEM), canonical
    )(meta, right_side, mine, other, *d2)
    mine2, other2 = gather(send)
    middles = place(place_middles_kernel, pair(ROWS, 2048) * 2, [first, second], 8 << 20)
    r1, send = call(
        middle_resid_kernel, (vec, f32(8, SLOTS, 8, 128)), [SMEM] + [VMEM] * 5, (VMEM, VMEM), canonical
    )(meta, right_side, mine2, other2, *middles[:2])
    (low, high), _ = lax.optimization_barrier((pieces[2:], (second[1], second[3])))
    before_low, after_high = around(low, 1), around(high, -1)
    before_low, after_high, send = lax.optimization_barrier((before_low, after_high, send))
    line = lax.all_to_all(send, "z", 0, 0)
    (low, high), before_low, after_high, line = lax.optimization_barrier(
        (pieces[2:], before_low, after_high, line)
    )
    relayed = [around(before_low, 1), around(after_high, -1)]
    before_high, after_low = around(high, 1), around(low, -1)
    lines = [lax.ppermute(line, "x", [(i, (i + d) % 4) for i in range(4)]) for d in (1, 2, 3)]
    mine = jnp.concatenate([line, *lines]).reshape(PLACES, 8, 128)
    mine, relayed = lax.optimization_barrier((mine, relayed))
    other = swap(mine)
    y1, send = call(
        middle_kernel, (vec, send_shape), [SMEM] + [VMEM] * 5, (VMEM, VMEM), canonical
    )(meta, r1, mine, other, *middles[2:])
    before_high, after_low, send = lax.optimization_barrier((before_high, after_low, send))
    third = [*pieces[2:], after_low, after_high, *relayed, before_low, before_high]
    mine, other = gather(send)
    m = place(place_all_kernel, pair(3, ROWS, THIRD), [first, second], 24 << 20)
    upd = call(
        update_kernel, f32(ROWS, RHS), [SMEM] + [VMEM] * 4, VMEM, canonical, 4 << 20
    )(meta, mine2, other2, *m)
    r0, send = call(
        top_resid_kernel, (vec, send_shape), [SMEM] + [VMEM] * 6, (VMEM, VMEM), canonical
    )(meta, right_side, upd, mine, other, *m)
    mine, other = gather(send)
    y0, part = call(
        top_kernel, (vec, part_shape), [SMEM] + [VMEM] * 5, (VMEM, VMEM), canonical
    )(meta, r0, mine, other, *m)

    def adds(level, *terms):
        return call(
            functools.partial(add_kernel, level),
            (vec, part_shape),
            [SMEM] + [VMEM] * (len(terms) + 2),
            (VMEM, VMEM),
        )(meta, *terms, *m)

    def subs(level, y, got):
        return call(
            functools.partial(sub_kernel, level),
            (vec, part_shape),
            [SMEM] + [VMEM] * 4,
            (VMEM, VMEM),
        )(meta, y, got, *m)

    x0, part = adds(1, y0, reduce(part))
    t1, part = subs(1, y1, reduce(part))
    x01, part = adds(2, t1, x0, reduce(part))
    t2, part = subs(2, y2, reduce(part))
    return call(last_kernel, vec, [VMEM] * 3, VMEM)(t2, x01, reduce(part))


def solution(mesh):
    fine = Mesh(mesh.devices.reshape(4, 8, 2, 4), ("x", "z", "c", "y"))
    rows = ("x", "z", "c")
    in_specs = (P(rows, "y"), P(rows, None), P(rows), P("y", rows))
    out_specs = P("y", rows)
    return jax.shard_map(shards, mesh=fine, in_specs=in_specs, out_specs=out_specs, check_vma=False)
```

```python
import functools

import jax
import jax.numpy as jnp
from jax import lax
from jax.experimental import pallas as pl
from jax.experimental.pallas import tpu as pltpu
from jax.sharding import Mesh, PartitionSpec as P

BLOCK = 64
RHS = 16
SLOTS = 3
ROWS = SLOTS * BLOCK
THIRD = 4096
PEERS = 32
PLACES = PEERS * SLOTS
PART = 1024
OWN = 192
ME = OWN + SLOTS
COLUMN = ME + 1
META = 200
HALF = 512
VMEM = pl.BlockSpec(memory_space=pltpu.VMEM)
SMEM = pl.BlockSpec(memory_space=pltpu.SMEM)
HBM = pl.BlockSpec(memory_space=pltpu.HBM)
CHIPS = ("x", "z")


def f32(*shape):
    return jax.ShapeDtypeStruct(shape, jnp.float32)


def left_half():
    return lax.broadcasted_iota(jnp.int32, (8, 128), 1) < BLOCK


def pack(rows):
    return [
        jnp.concatenate(
            [rows[:8, s * BLOCK : (s + 1) * BLOCK], rows[8:, s * BLOCK : (s + 1) * BLOCK]], axis=1
        )
        for s in range(SLOTS)
    ]


def unpack(tiles):
    upper = jnp.concatenate([t[:, :BLOCK] for t in tiles], axis=1)
    lower = jnp.concatenate([t[:, BLOCK:] for t in tiles], axis=1)
    return jnp.concatenate([upper, lower], axis=0)


def only(meta_ref, level, rows):
    slot = lax.broadcasted_iota(jnp.int32, rows.shape, 1) // BLOCK
    keep = jnp.zeros(rows.shape, jnp.bool_)
    for s in range(SLOTS):
        g = meta_ref[OWN + s]
        here = (g >= (2 - level) * 64) & (g < (3 - level) * 64)
        keep = keep | ((slot == s) & here)
    return jnp.where(keep, rows, 0.0)


def halves(x):
    high = x.astype(jnp.bfloat16)
    return high, (x - high.astype(jnp.float32)).astype(jnp.bfloat16)


def to_canonical(meta_ref, level, mine_ref, other_ref, x_ref, extra=False, relative=False):
    base = (2 - level) * 64
    half = left_half()

    def tile(place):
        near = jnp.minimum(place, PLACES - 1)
        far = jnp.maximum(place, PLACES) - PLACES
        if extra:
            near, far = near + near // SLOTS, far + far // SLOTS
        if relative:
            line = PLACES // 4

            def back(at):
                return lax.rem(meta_ref[COLUMN] + 4 - at // line, 4) * line + lax.rem(at, line)

            near, far = back(near), back(far)
        return jnp.where(place >= PLACES, other_ref[far], mine_ref[near])

    for t in range(32):
        a = tile(meta_ref[base + 2 * t])
        b = tile(meta_ref[base + 2 * t + 1])
        top = jnp.where(half, a, pltpu.roll(b, BLOCK, 1))
        bottom = jnp.where(half, pltpu.roll(a, BLOCK, 1), b)
        high, low = halves(jnp.concatenate([top, bottom], axis=0))
        x_ref[0:16, 128 * t : 128 * (t + 1)] = high
        x_ref[16:32, 128 * t : 128 * (t + 1)] = low


def to_places(meta_ref, level, x, out_ref):
    base = (2 - level) * 64
    half = left_half()
    out_ref[...] = jnp.zeros_like(out_ref)
    for t in range(32):
        top = x[0:8, 128 * t : 128 * (t + 1)]
        bottom = x[8:16, 128 * t : 128 * (t + 1)]
        out_ref[meta_ref[base + 2 * t]] = jnp.where(half, top, pltpu.roll(bottom, BLOCK, 1))
        out_ref[meta_ref[base + 2 * t + 1]] = jnp.where(half, pltpu.roll(top, BLOCK, 1), bottom)


def times_rows(x, high, low):
    dims = (((1,), (1,)), ((), ()))
    one = lax.dot_general(high, x, dims, preferred_element_type=jnp.float32)
    two = lax.dot_general(low, x[:RHS], dims, preferred_element_type=jnp.float32)
    return one[:, :RHS] + one[:, RHS:] + two


def times_cols(x, high, low):
    dims = (((1,), (0,)), ((), ()))
    x_high, x_low = halves(x)
    both = jnp.concatenate([x_high, x_low], axis=0)
    one = lax.dot_general(both, high, dims, preferred_element_type=jnp.float32)
    two = lax.dot_general(x_high, low, dims, preferred_element_type=jnp.float32)
    return one[:RHS] + one[RHS:] + two


def spread(tiles, send_ref):
    for peer in range(send_ref.shape[0]):
        for s in range(SLOTS):
            send_ref[peer, s] = tiles[s]


def arrived(got_ref):
    return unpack([jnp.sum(got_ref[:, s], axis=0) for s in range(SLOTS)])


def start_kernel(own_ref, pattern_ref, b_ref, after_ref, send_ref, below_ref):
    tiles = pack(b_ref[...])
    lane = lax.broadcasted_iota(jnp.int32, (8, 128), 1)
    names = jnp.zeros((8, 128), jnp.float32)
    for s in range(SLOTS):
        names = jnp.where(lane == s, own_ref[s].astype(jnp.float32), names)
    spread(tiles, send_ref)
    for peer in range(PEERS):
        send_ref[peer, SLOTS] = names
    lane = lax.broadcasted_iota(jnp.int32, (1, 128), 1)
    for s in range(SLOTS):
        for part in range(12):
            state = state_of(own_ref[s], part)
            for t in range(PART // 128):
                at = part * (PART // BLOCK) + 2 * t
                keep = [
                    jnp.where((state == 1) & (pattern_ref[s, at + i] > 0), -1, 1 << 20)
                    for i in range(2)
                ]
                col = part * PART + t * 128 + lane
                rest = jnp.where(lane < BLOCK, keep[0], keep[1])
                below_ref[s, :, part * PART + t * 128 : part * PART + (t + 1) * 128] = jnp.where(
                    state == 2, col, rest
                )


def names_kernel(own_ref, me_ref, mine_ref, other_ref, meta_ref, names_ref, order_ref, sem):
    row = lax.broadcasted_iota(jnp.int32, (8, 128), 0)
    for far, ref in enumerate((mine_ref, other_ref)):
        for k in range(PEERS // 8):
            names = ref[(SLOTS + 1) * 8 * k + SLOTS]
            for r in range(1, 8):
                names = jnp.where(row == r, ref[(SLOTS + 1) * (8 * k + r) + SLOTS], names)
            at = far * PEERS + 8 * k
            names_ref[at : at + 8] = names.astype(jnp.int32)
    copy = pltpu.make_async_copy(names_ref, order_ref, sem.at[0])
    copy.start()
    copy.wait()
    for chip in range(2 * PEERS):
        for s in range(SLOTS):
            meta_ref[order_ref[chip, s]] = chip * SLOTS + s
    for s in range(SLOTS):
        meta_ref[OWN + s] = own_ref[s]
    meta_ref[ME] = me_ref[0]
    meta_ref[COLUMN] = me_ref[1]
    for i in range(COLUMN + 1, META):
        meta_ref[i] = 0


def turn(g, q):
    leaf = jnp.where(g // 16 == 3, 0, g // 16)
    first = jnp.where(q == 1, 1, 0)
    second = jnp.where(q == 0, 2, 0)
    return jnp.where(g < 64, leaf, jnp.where(g < 96, first, jnp.where(g < 128, second, 0)))


def part_of(e, g, q):
    return 3 * q + lax.rem(e + turn(g, q), 3)


def rows_of(s):
    return slice(s * BLOCK, (s + 1) * BLOCK)


def split_kernel(own_ref, me_ref, factor_ref, *refs):
    first, second, third_a, third_b, sems = refs
    copies = []
    for e in range(3):
        for s in range(SLOTS):
            at = lax.rem(e + turn(own_ref[s], me_ref[0]), 3) * PART
            for h in range(2):
                out = (third_a, third_b)[h] if e == 2 else (first, second)[e].at[h]
                copies.append(
                    pltpu.make_async_copy(
                        factor_ref.at[rows_of(s), pl.ds(pl.multiple_of(at + h * HALF, HALF), HALF)],
                        out.at[rows_of(s)],
                        sems.at[len(copies)],
                    )
                )
    for copy in copies:
        copy.start()
    for copy in copies:
        copy.wait()


def state_of(g, part):
    group = (g - 64) // 32
    leaf = jnp.where(part == g // 16, 2, 0)
    own = (part == 4 + 2 * group) | (part == 5 + 2 * group)
    below = (part == 2 * group) | (part == 2 * group + 1)
    middle = jnp.where(own, 2, jnp.where(below, 1, 0))
    return jnp.where(g < 64, leaf, jnp.where(g < 128, middle, jnp.where(part >= 8, 2, 1)))


def masked(below_ref, s, g, part, h, block):
    row = g * BLOCK + lax.broadcasted_iota(jnp.int32, (BLOCK, HALF), 0)
    col0 = pl.multiple_of(part * PART + h * HALF, HALF)
    return halves(jnp.where(row > below_ref[s, :, pl.ds(col0, HALF)], block, 0.0))


def sources(e, meta_ref, refs):
    for d in range(4):
        q = lax.rem(meta_ref[ME] + d, 4)
        for s in range(SLOTS):
            g = meta_ref[OWN + s]
            for h in range(2):
                if e == 2:
                    src = refs[2 * d + h].at[rows_of(s)]
                elif d == 2:
                    src = refs[2 + h].at[rows_of(s)]
                else:
                    src = refs[(0, 1, 0, 4)[d]].at[h, rows_of(s)]
                yield s, h, g, part_of(e, g, q), src


def put(refs, s, at, pair):
    for ref, value in zip(refs, pair):
        ref[rows_of(s), pl.ds(pl.multiple_of(at, HALF), HALF)] = value


def place_leaves_kernel(meta_ref, below_ref, *refs):
    for s, h, g, part, src in sources(0, meta_ref, refs[:5]):

        @pl.when((g < 64) & (part == g // 16))
        def _(s=s, h=h, g=g, part=part, src=src):
            put(refs[5:7], s, h * HALF, masked(below_ref, s, g, part, h, src[...]))


def place_middles_kernel(meta_ref, below_ref, *refs):
    for e in range(2):
        for s, h, g, part, src in sources(e, meta_ref, refs[5 * e : 5 * e + 5]):
            mine = (g >= 64) & (g < 128) & (state_of(g, part) > 0)
            at = lax.rem(part, 2) * PART + h * HALF

            @pl.when(mine & (part < 4))
            def _(s=s, h=h, g=g, part=part, src=src, at=at):
                put(refs[10:12], s, at, masked(below_ref, s, g, part, h, src[...]))

            @pl.when(mine & (part >= 4))
            def _(s=s, h=h, g=g, part=part, src=src, at=at):
                put(refs[12:14], s, at, masked(below_ref, s, g, part, h, src[...]))


def place_all_kernel(meta_ref, below_ref, *refs):
    for e in range(3):
        for s, h, g, part, src in sources(e, meta_ref, refs[5 * e : (5, 10, 18)[e]]):
            at = lax.rem(part, 4) * PART + h * HALF
            outs = [ref.at[part // 4] for ref in refs[18:20]]
            put(outs, s, at, masked(below_ref, s, g, part, h, src[...]))


def own_products(meta_ref, base, blocks, groups, x_ref, high_ref, low_ref):
    wide = high_ref.shape[1]
    outs = []
    for s in range(SLOTS):
        group = jnp.clip((meta_ref[OWN + s] - base) // blocks, 0, groups - 1)
        x = x_ref[:, pl.ds(pl.multiple_of(group * wide, wide), wide)]
        outs.append(times_rows(x, high_ref[rows_of(s)], low_ref[rows_of(s)]))
    return jnp.concatenate(outs, axis=0).T


def leaves_kernel(meta_ref, b_ref, mine_ref, other_ref, high_ref, low_ref, y_ref, send_ref, x_ref):
    to_canonical(meta_ref, 2, mine_ref, other_ref, x_ref, True)
    y = only(meta_ref, 2, own_products(meta_ref, 0, 16, 4, x_ref, high_ref, low_ref) + b_ref[...])
    y_ref[...] = y
    spread(pack(y), send_ref)


def middle_resid_kernel(meta_ref, b_ref, mine_ref, other_ref, high_ref, low_ref, r_ref, send_ref, x_ref):
    to_canonical(meta_ref, 2, mine_ref, other_ref, x_ref)
    r = only(meta_ref, 1, b_ref[...] - own_products(meta_ref, 64, 32, 2, x_ref, high_ref, low_ref))
    r_ref[...] = r
    spread(pack(r), send_ref)


def middle_kernel(meta_ref, r_ref, mine_ref, other_ref, high_ref, low_ref, y_ref, send_ref, x_ref):
    to_canonical(meta_ref, 1, mine_ref, other_ref, x_ref, relative=True)
    y = only(meta_ref, 1, own_products(meta_ref, 64, 32, 2, x_ref, high_ref, low_ref) + r_ref[...])
    y_ref[...] = y
    spread(pack(y), send_ref)


def top_resid_kernel(meta_ref, b_ref, mine2_ref, other2_ref, mine_ref, other_ref, high_ref, low_ref, r_ref, send_ref, x2_ref, x_ref):
    to_canonical(meta_ref, 2, mine2_ref, other2_ref, x2_ref)
    upd = times_rows(x2_ref[...], high_ref[0], low_ref[0])
    to_canonical(meta_ref, 1, mine_ref, other_ref, x_ref, relative=True)
    upd = upd + times_rows(x_ref[...], high_ref[1], low_ref[1])
    r = only(meta_ref, 0, b_ref[...] - upd.T)
    r_ref[...] = r
    spread(pack(r), send_ref)


def top_kernel(meta_ref, r_ref, mine_ref, other_ref, high_ref, low_ref, y_ref, part_ref, x_ref):
    to_canonical(meta_ref, 0, mine_ref, other_ref, x_ref)
    y = only(meta_ref, 0, times_rows(x_ref[...], high_ref[2], low_ref[2]).T) + r_ref[...]
    y_ref[...] = y
    to_places(meta_ref, 0, times_cols(y, high_ref[2], low_ref[2]), part_ref)


def add_kernel(level, meta_ref, *refs):
    terms = refs[:-5]
    got_ref, high_ref, low_ref, x_out_ref, part_ref = refs[-5:]
    x = arrived(got_ref)
    for term in terms:
        x = x + term[...]
    x_out_ref[...] = x
    to_places(meta_ref, level, times_cols(x, high_ref[2 - level], low_ref[2 - level]), part_ref)


def sub_kernel(level, meta_ref, y_ref, got_ref, high_ref, low_ref, t_ref, part_ref):
    t = only(meta_ref, level, y_ref[...] - arrived(got_ref))
    t_ref[...] = t
    to_places(meta_ref, level, times_cols(t, high_ref[2 - level], low_ref[2 - level]), part_ref)


def last_kernel(t_ref, x_ref, got_ref, out_ref):
    out_ref[...] = t_ref[...] + x_ref[...] + arrived(got_ref)


def swap(x):
    return lax.ppermute(x, "c", [(0, 1), (1, 0)])


def exchange(x):
    return lax.all_to_all(x, CHIPS, 0, 0)


def gather(send):
    mine = exchange(send)
    other = swap(mine)
    return mine.reshape(PLACES, 8, 128), other.reshape(PLACES, 8, 128)


def reduce(part):
    far = swap(part[PLACES:])
    return exchange((part[:PLACES] + far).reshape(PEERS, SLOTS, 8, 128))


def around(x, step):
    return lax.ppermute(x, "y", [(i, (i + step) % 4) for i in range(4)])


def over_planes(part, tie=None):
    before, after = around(part, 1), around(part, -1)
    if tie is not None:
        before, after, tie = lax.optimization_barrier((before, after, tie))
    else:
        before, after = lax.optimization_barrier((before, after))
    opposite = [around(before[0], 1), around(after[1], -1)]
    return (part, after, opposite, before), tie


def call(kernel, outs, specs, out_specs, scratch=(), work=0):
    return pl.pallas_call(
        kernel,
        out_shape=outs,
        in_specs=specs,
        out_specs=out_specs,
        scratch_shapes=list(scratch),
        compiler_params=pltpu.CompilerParams(vmem_limit_bytes=28 * 1024 * 1024),
        cost_estimate=pl.CostEstimate(flops=0, bytes_accessed=work, transcendentals=0) if work else None,
    )


def shards(factor, pattern, owner, right_side):
    total = pattern.shape[1]
    vec = f32(RHS, ROWS)
    send_shape = f32(PEERS, SLOTS, 8, 128)
    part_shape = f32(2 * PLACES, 8, 128)
    me = jnp.stack([lax.axis_index("y"), lax.axis_index("x")]).astype(jnp.int32)
    canonical = [pltpu.VMEM((2 * RHS, THIRD), jnp.bfloat16)]

    def pair(*shape):
        return (jax.ShapeDtypeStruct(shape, jnp.bfloat16),) * 2

    pieces = call(
        split_kernel,
        (f32(2, ROWS, HALF),) * 2 + (f32(ROWS, HALF),) * 2,
        [SMEM, SMEM, HBM],
        (HBM,) * 4,
        [pltpu.SemaphoreType.DMA((18,))],
    )(owner, me, factor)

    first, _ = over_planes(pieces[0])
    late = swap(pieces[0][0, :8, :128])
    send, below = call(
        start_kernel,
        (f32(PEERS, SLOTS + 1, 8, 128), jax.ShapeDtypeStruct((SLOTS, 1, total * BLOCK), jnp.int32)),
        [SMEM, SMEM, VMEM, VMEM],
        (VMEM, VMEM),
    )(owner, pattern, right_side, late)

    mine = exchange(send)
    other = swap(mine)
    mine, other = (v.reshape(PEERS * (SLOTS + 1), 8, 128) for v in (mine, other))
    meta = call(
        names_kernel,
        jax.ShapeDtypeStruct((META,), jnp.int32),
        [SMEM, SMEM, VMEM, VMEM],
        SMEM,
        [
            pltpu.VMEM((2 * PEERS, 128), jnp.int32),
            pltpu.SMEM((2 * PEERS, 128), jnp.int32),
            pltpu.SemaphoreType.DMA((1,)),
        ],
    )(owner, me, mine, other)

    def place(kernel, outs, parts, work):
        given = [v for own, after, opposite, before in parts for v in (own, after, *opposite, before)]
        given += third if kernel is place_all_kernel else []
        return call(
            kernel, outs, [SMEM, VMEM] + [VMEM] * len(given), (VMEM,) * len(outs), work=work
        )(meta, below, *given)

    d2 = place(place_leaves_kernel, pair(ROWS, 1024), [first], 2 << 20)
    piece, _ = lax.optimization_barrier((pieces[1], first[2]))
    second, _ = over_planes(piece)

    y2, send = call(
        leaves_kernel, (vec, send_shape), [SMEM] + [VMEM] * 5, (VMEM, VMEM), canonical
    )(meta, right_side, mine, other, *d2)
    mine2, other2 = gather(send)
    middles = place(place_middles_kernel, pair(ROWS, 2048) * 2, [first, second], 8 << 20)
    r1, send = call(
        middle_resid_kernel, (vec, f32(8, SLOTS, 8, 128)), [SMEM] + [VMEM] * 5, (VMEM, VMEM), canonical
    )(meta, right_side, mine2, other2, *middles[:2])
    (low, high), _ = lax.optimization_barrier((pieces[2:], (second[1], second[3])))
    before_low, after_high = around(low, 1), around(high, -1)
    before_low, after_high, send = lax.optimization_barrier((before_low, after_high, send))
    line = lax.all_to_all(send, "z", 0, 0)
    (low, high), before_low, after_high, line = lax.optimization_barrier(
        (pieces[2:], before_low, after_high, line)
    )
    relayed = [around(before_low, 1), around(after_high, -1)]
    before_high, after_low = around(high, 1), around(low, -1)
    lines = [lax.ppermute(line, "x", [(i, (i + d) % 4) for i in range(4)]) for d in (1, 2, 3)]
    mine = jnp.concatenate([line, *lines]).reshape(PLACES, 8, 128)
    mine, relayed = lax.optimization_barrier((mine, relayed))
    other = swap(mine)
    y1, send = call(
        middle_kernel, (vec, f32(8, SLOTS, 8, 128)), [SMEM] + [VMEM] * 5, (VMEM, VMEM), canonical
    )(meta, r1, mine, other, *middles[2:])
    line = lax.all_to_all(send, "z", 0, 0)
    lines = [lax.ppermute(line, "x", [(i, (i + d) % 4) for i in range(4)]) for d in (1, 2, 3)]
    mine = jnp.concatenate([line, *lines]).reshape(PLACES, 8, 128)
    mine, before_high, after_low = lax.optimization_barrier((mine, before_high, after_low))
    other = swap(mine)
    third = [*pieces[2:], after_low, after_high, *relayed, before_low, before_high]
    m = place(place_all_kernel, pair(3, ROWS, THIRD), [first, second], 24 << 20)
    r0, send = call(
        top_resid_kernel, (vec, send_shape), [SMEM] + [VMEM] * 7, (VMEM, VMEM), canonical * 2
    )(meta, right_side, mine2, other2, mine, other, *m)
    mine, other = gather(send)
    y0, part = call(
        top_kernel, (vec, part_shape), [SMEM] + [VMEM] * 5, (VMEM, VMEM), canonical
    )(meta, r0, mine, other, *m)

    def adds(level, *terms):
        return call(
            functools.partial(add_kernel, level),
            (vec, part_shape),
            [SMEM] + [VMEM] * (len(terms) + 2),
            (VMEM, VMEM),
        )(meta, *terms, *m)

    def subs(level, y, got):
        return call(
            functools.partial(sub_kernel, level),
            (vec, part_shape),
            [SMEM] + [VMEM] * 4,
            (VMEM, VMEM),
        )(meta, y, got, *m)

    x0, part = adds(1, y0, reduce(part))
    t1, part = subs(1, y1, reduce(part))
    x01, part = adds(2, t1, x0, reduce(part))
    t2, part = subs(2, y2, reduce(part))
    return call(last_kernel, vec, [VMEM] * 3, VMEM)(t2, x01, reduce(part))


def solution(mesh):
    fine = Mesh(mesh.devices.reshape(4, 8, 2, 4), ("x", "z", "c", "y"))
    rows = ("x", "z", "c")
    in_specs = (P(rows, "y"), P(rows, None), P(rows), P("y", rows))
    out_specs = P("y", rows)
    return jax.shard_map(shards, mesh=fine, in_specs=in_specs, out_specs=out_specs, check_vma=False)
```

```python
import functools

import jax
import jax.numpy as jnp
from jax import lax
from jax.experimental import pallas as pl
from jax.experimental.pallas import tpu as pltpu
from jax.sharding import Mesh, PartitionSpec as P

BLOCK = 64
RHS = 16
SLOTS = 3
ROWS = SLOTS * BLOCK
THIRD = 4096
PEERS = 32
PLACES = PEERS * SLOTS
PART = 1024
OWN = 192
ME = OWN + SLOTS
COLUMN = ME + 1
META = 200
HALF = 512
VMEM = pl.BlockSpec(memory_space=pltpu.VMEM)
SMEM = pl.BlockSpec(memory_space=pltpu.SMEM)
HBM = pl.BlockSpec(memory_space=pltpu.HBM)
CHIPS = ("x", "z")


def f32(*shape):
    return jax.ShapeDtypeStruct(shape, jnp.float32)


def left_half():
    return lax.broadcasted_iota(jnp.int32, (8, 128), 1) < BLOCK


def pack(rows):
    return [
        jnp.concatenate(
            [rows[:8, s * BLOCK : (s + 1) * BLOCK], rows[8:, s * BLOCK : (s + 1) * BLOCK]], axis=1
        )
        for s in range(SLOTS)
    ]


def unpack(tiles):
    upper = jnp.concatenate([t[:, :BLOCK] for t in tiles], axis=1)
    lower = jnp.concatenate([t[:, BLOCK:] for t in tiles], axis=1)
    return jnp.concatenate([upper, lower], axis=0)


def only(meta_ref, level, rows):
    slot = lax.broadcasted_iota(jnp.int32, rows.shape, 1) // BLOCK
    keep = jnp.zeros(rows.shape, jnp.bool_)
    for s in range(SLOTS):
        g = meta_ref[OWN + s]
        here = (g >= (2 - level) * 64) & (g < (3 - level) * 64)
        keep = keep | ((slot == s) & here)
    return jnp.where(keep, rows, 0.0)


def halves(x):
    high = x.astype(jnp.bfloat16)
    return high, (x - high.astype(jnp.float32)).astype(jnp.bfloat16)


def to_canonical(meta_ref, level, mine_ref, other_ref, x_ref, extra=False, relative=False):
    base = (2 - level) * 64
    half = left_half()

    def tile(place):
        near = jnp.minimum(place, PLACES - 1)
        far = jnp.maximum(place, PLACES) - PLACES
        if extra:
            near, far = near + near // SLOTS, far + far // SLOTS
        if relative:
            line = PLACES // 4

            def back(at):
                return lax.rem(meta_ref[COLUMN] + 4 - at // line, 4) * line + lax.rem(at, line)

            near, far = back(near), back(far)
        return jnp.where(place >= PLACES, other_ref[far], mine_ref[near])

    for t in range(32):
        a = tile(meta_ref[base + 2 * t])
        b = tile(meta_ref[base + 2 * t + 1])
        top = jnp.where(half, a, pltpu.roll(b, BLOCK, 1))
        bottom = jnp.where(half, pltpu.roll(a, BLOCK, 1), b)
        high, low = halves(jnp.concatenate([top, bottom], axis=0))
        x_ref[0:16, 128 * t : 128 * (t + 1)] = high
        x_ref[16:32, 128 * t : 128 * (t + 1)] = low


def to_places(meta_ref, level, x, out_ref):
    base = (2 - level) * 64
    half = left_half()
    out_ref[...] = jnp.zeros_like(out_ref)
    for t in range(32):
        top = x[0:8, 128 * t : 128 * (t + 1)]
        bottom = x[8:16, 128 * t : 128 * (t + 1)]
        out_ref[meta_ref[base + 2 * t]] = jnp.where(half, top, pltpu.roll(bottom, BLOCK, 1))
        out_ref[meta_ref[base + 2 * t + 1]] = jnp.where(half, pltpu.roll(top, BLOCK, 1), bottom)


def times_rows(x, high, low):
    dims = (((1,), (1,)), ((), ()))
    one = lax.dot_general(high, x, dims, preferred_element_type=jnp.float32)
    two = lax.dot_general(low, x[:RHS], dims, preferred_element_type=jnp.float32)
    return one[:, :RHS] + one[:, RHS:] + two


def times_cols(x, high, low):
    dims = (((1,), (0,)), ((), ()))
    x_high, x_low = halves(x)
    both = jnp.concatenate([x_high, x_low], axis=0)
    one = lax.dot_general(both, high, dims, preferred_element_type=jnp.float32)
    two = lax.dot_general(x_high, low, dims, preferred_element_type=jnp.float32)
    return one[:RHS] + one[RHS:] + two


def spread(tiles, send_ref):
    for peer in range(send_ref.shape[0]):
        for s in range(SLOTS):
            send_ref[peer, s] = tiles[s]


def arrived(got_ref):
    return unpack([jnp.sum(got_ref[:, s], axis=0) for s in range(SLOTS)])


def start_kernel(own_ref, pattern_ref, b_ref, after_ref, send_ref, below_ref):
    tiles = pack(b_ref[...])
    lane = lax.broadcasted_iota(jnp.int32, (8, 128), 1)
    names = jnp.zeros((8, 128), jnp.float32)
    for s in range(SLOTS):
        names = jnp.where(lane == s, own_ref[s].astype(jnp.float32), names)
    spread(tiles, send_ref)
    for peer in range(PEERS):
        send_ref[peer, SLOTS] = names
    lane = lax.broadcasted_iota(jnp.int32, (1, 128), 1)
    for s in range(SLOTS):
        for part in range(12):
            state = state_of(own_ref[s], part)
            for t in range(PART // 128):
                at = part * (PART // BLOCK) + 2 * t
                keep = [
                    jnp.where((state == 1) & (pattern_ref[s, at + i] > 0), -1, 1 << 20)
                    for i in range(2)
                ]
                col = part * PART + t * 128 + lane
                rest = jnp.where(lane < BLOCK, keep[0], keep[1])
                below_ref[s, :, part * PART + t * 128 : part * PART + (t + 1) * 128] = jnp.where(
                    state == 2, col, rest
                )


def names_kernel(own_ref, me_ref, mine_ref, other_ref, meta_ref, names_ref, order_ref, sem):
    row = lax.broadcasted_iota(jnp.int32, (8, 128), 0)
    for far, ref in enumerate((mine_ref, other_ref)):
        for k in range(PEERS // 8):
            names = ref[(SLOTS + 1) * 8 * k + SLOTS]
            for r in range(1, 8):
                names = jnp.where(row == r, ref[(SLOTS + 1) * (8 * k + r) + SLOTS], names)
            at = far * PEERS + 8 * k
            names_ref[at : at + 8] = names.astype(jnp.int32)
    copy = pltpu.make_async_copy(names_ref, order_ref, sem.at[0])
    copy.start()
    copy.wait()
    for chip in range(2 * PEERS):
        for s in range(SLOTS):
            meta_ref[order_ref[chip, s]] = chip * SLOTS + s
    for s in range(SLOTS):
        meta_ref[OWN + s] = own_ref[s]
    meta_ref[ME] = me_ref[0]
    meta_ref[COLUMN] = me_ref[1]
    for i in range(COLUMN + 1, META):
        meta_ref[i] = 0


def turn(g, q):
    leaf = jnp.where(g // 16 == 3, 0, g // 16)
    first = jnp.where(q == 1, 1, 0)
    second = jnp.where(q == 0, 2, 0)
    return jnp.where(g < 64, leaf, jnp.where(g < 96, first, jnp.where(g < 128, second, 0)))


def part_of(e, g, q):
    return 3 * q + lax.rem(e + turn(g, q), 3)


def rows_of(s):
    return slice(s * BLOCK, (s + 1) * BLOCK)


def split_kernel(own_ref, me_ref, factor_ref, *refs):
    first, second, third_a, third_b, sems = refs
    copies = []
    for e in range(3):
        for s in range(SLOTS):
            at = lax.rem(e + turn(own_ref[s], me_ref[0]), 3) * PART
            for h in range(2):
                out = (third_a, third_b)[h] if e == 2 else (first, second)[e].at[h]
                copies.append(
                    pltpu.make_async_copy(
                        factor_ref.at[rows_of(s), pl.ds(pl.multiple_of(at + h * HALF, HALF), HALF)],
                        out.at[rows_of(s)],
                        sems.at[len(copies)],
                    )
                )
    for copy in copies:
        copy.start()
    for copy in copies:
        copy.wait()


def state_of(g, part):
    group = (g - 64) // 32
    leaf = jnp.where(part == g // 16, 2, 0)
    own = (part == 4 + 2 * group) | (part == 5 + 2 * group)
    below = (part == 2 * group) | (part == 2 * group + 1)
    middle = jnp.where(own, 2, jnp.where(below, 1, 0))
    return jnp.where(g < 64, leaf, jnp.where(g < 128, middle, jnp.where(part >= 8, 2, 1)))


def masked(below_ref, s, g, part, h, block):
    row = g * BLOCK + lax.broadcasted_iota(jnp.int32, (BLOCK, HALF), 0)
    col0 = pl.multiple_of(part * PART + h * HALF, HALF)
    return halves(jnp.where(row > below_ref[s, :, pl.ds(col0, HALF)], block, 0.0))


def sources(e, meta_ref, refs):
    for d in range(4):
        q = lax.rem(meta_ref[ME] + d, 4)
        for s in range(SLOTS):
            g = meta_ref[OWN + s]
            for h in range(2):
                if e == 2:
                    src = refs[2 * d + h].at[rows_of(s)]
                elif d == 2:
                    src = refs[2 + h].at[rows_of(s)]
                else:
                    src = refs[(0, 1, 0, 4)[d]].at[h, rows_of(s)]
                yield s, h, g, part_of(e, g, q), src


def put(refs, s, at, pair):
    for ref, value in zip(refs, pair):
        ref[rows_of(s), pl.ds(pl.multiple_of(at, HALF), HALF)] = value


def place_leaves_kernel(meta_ref, below_ref, *refs):
    for s, h, g, part, src in sources(0, meta_ref, refs[:5]):

        @pl.when((g < 64) & (part == g // 16))
        def _(s=s, h=h, g=g, part=part, src=src):
            put(refs[5:7], s, h * HALF, masked(below_ref, s, g, part, h, src[...]))


def place_middles_kernel(meta_ref, below_ref, *refs):
    for e in range(2):
        for s, h, g, part, src in sources(e, meta_ref, refs[5 * e : 5 * e + 5]):
            mine = (g >= 64) & (g < 128) & (state_of(g, part) > 0)
            at = lax.rem(part, 2) * PART + h * HALF

            @pl.when(mine & (part < 4))
            def _(s=s, h=h, g=g, part=part, src=src, at=at):
                put(refs[10:12], s, at, masked(below_ref, s, g, part, h, src[...]))

            @pl.when(mine & (part >= 4))
            def _(s=s, h=h, g=g, part=part, src=src, at=at):
                put(refs[12:14], s, at, masked(below_ref, s, g, part, h, src[...]))


def place_all_kernel(meta_ref, below_ref, *refs):
    for e in range(3):
        for s, h, g, part, src in sources(e, meta_ref, refs[5 * e : (5, 10, 18)[e]]):
            at = lax.rem(part, 4) * PART + h * HALF
            outs = [ref.at[part // 4] for ref in refs[18:20]]
            put(outs, s, at, masked(below_ref, s, g, part, h, src[...]))


def own_products(meta_ref, base, blocks, groups, x_ref, high_ref, low_ref):
    wide = high_ref.shape[1]
    outs = []
    for s in range(SLOTS):
        group = jnp.clip((meta_ref[OWN + s] - base) // blocks, 0, groups - 1)
        x = x_ref[:, pl.ds(pl.multiple_of(group * wide, wide), wide)]
        outs.append(times_rows(x, high_ref[rows_of(s)], low_ref[rows_of(s)]))
    return jnp.concatenate(outs, axis=0).T


def leaves_kernel(meta_ref, b_ref, mine_ref, other_ref, high_ref, low_ref, y_ref, send_ref, x_ref):
    to_canonical(meta_ref, 2, mine_ref, other_ref, x_ref, True)
    y = only(meta_ref, 2, own_products(meta_ref, 0, 16, 4, x_ref, high_ref, low_ref) + b_ref[...])
    y_ref[...] = y
    spread(pack(y), send_ref)


def middle_resid_kernel(meta_ref, b_ref, mine_ref, other_ref, high_ref, low_ref, r_ref, send_ref, x_ref):
    to_canonical(meta_ref, 2, mine_ref, other_ref, x_ref)
    r = only(meta_ref, 1, b_ref[...] - own_products(meta_ref, 64, 32, 2, x_ref, high_ref, low_ref))
    r_ref[...] = r
    spread(pack(r), send_ref)


def middle_kernel(meta_ref, r_ref, mine_ref, other_ref, high_ref, low_ref, y_ref, send_ref, x_ref):
    to_canonical(meta_ref, 1, mine_ref, other_ref, x_ref, relative=True)
    y = only(meta_ref, 1, own_products(meta_ref, 64, 32, 2, x_ref, high_ref, low_ref) + r_ref[...])
    y_ref[...] = y
    spread(pack(y), send_ref)


def top_resid_kernel(meta_ref, b_ref, mine2_ref, other2_ref, mine_ref, other_ref, high_ref, low_ref, r_ref, send_ref, x2_ref, x_ref):
    to_canonical(meta_ref, 2, mine2_ref, other2_ref, x2_ref)
    upd = times_rows(x2_ref[...], high_ref[0], low_ref[0])
    to_canonical(meta_ref, 1, mine_ref, other_ref, x_ref, relative=True)
    upd = upd + times_rows(x_ref[...], high_ref[1], low_ref[1])
    r = only(meta_ref, 0, b_ref[...] - upd.T)
    r_ref[...] = r
    spread(pack(r), send_ref)


def top_kernel(meta_ref, r_ref, mine_ref, other_ref, high_ref, low_ref, y_ref, part_ref, x_ref):
    to_canonical(meta_ref, 0, mine_ref, other_ref, x_ref)
    y = only(meta_ref, 0, times_rows(x_ref[...], high_ref[2], low_ref[2]).T) + r_ref[...]
    y_ref[...] = y
    to_places(meta_ref, 0, times_cols(y, high_ref[2], low_ref[2]), part_ref)


def add_kernel(level, meta_ref, *refs):
    terms = refs[:-5]
    got_ref, high_ref, low_ref, x_out_ref, part_ref = refs[-5:]
    x = arrived(got_ref)
    for term in terms:
        x = x + term[...]
    x_out_ref[...] = x
    to_places(meta_ref, level, times_cols(x, high_ref[2 - level], low_ref[2 - level]), part_ref)


def sub_kernel(level, meta_ref, y_ref, got_ref, high_ref, low_ref, t_ref, part_ref):
    t = only(meta_ref, level, y_ref[...] - arrived(got_ref))
    t_ref[...] = t
    to_places(meta_ref, level, times_cols(t, high_ref[2 - level], low_ref[2 - level]), part_ref)


def last_kernel(t_ref, x_ref, got_ref, out_ref):
    out_ref[...] = t_ref[...] + x_ref[...] + arrived(got_ref)


def swap(x):
    return lax.ppermute(x, "c", [(0, 1), (1, 0)])


def exchange(x):
    return lax.all_to_all(x, CHIPS, 0, 0)


def gather(send):
    mine = exchange(send)
    other = swap(mine)
    return mine.reshape(PLACES, 8, 128), other.reshape(PLACES, 8, 128)


def reduce(part):
    far = swap(part[PLACES:])
    return exchange((part[:PLACES] + far).reshape(PEERS, SLOTS, 8, 128))


def around(x, step):
    return lax.ppermute(x, "y", [(i, (i + step) % 4) for i in range(4)])


def over_planes(part, tie=None):
    before, after = around(part, 1), around(part, -1)
    if tie is not None:
        before, after, tie = lax.optimization_barrier((before, after, tie))
    else:
        before, after = lax.optimization_barrier((before, after))
    opposite = [around(before[0], 1), around(after[1], -1)]
    return (part, after, opposite, before), tie


def call(kernel, outs, specs, out_specs, scratch=(), work=0):
    return pl.pallas_call(
        kernel,
        out_shape=outs,
        in_specs=specs,
        out_specs=out_specs,
        scratch_shapes=list(scratch),
        compiler_params=pltpu.CompilerParams(vmem_limit_bytes=28 * 1024 * 1024),
        cost_estimate=pl.CostEstimate(flops=0, bytes_accessed=work, transcendentals=0) if work else None,
    )


def shards(factor, pattern, owner, right_side):
    total = pattern.shape[1]
    vec = f32(RHS, ROWS)
    send_shape = f32(PEERS, SLOTS, 8, 128)
    part_shape = f32(2 * PLACES, 8, 128)
    me = jnp.stack([lax.axis_index("y"), lax.axis_index("x")]).astype(jnp.int32)
    canonical = [pltpu.VMEM((2 * RHS, THIRD), jnp.bfloat16)]

    def pair(*shape):
        return (jax.ShapeDtypeStruct(shape, jnp.bfloat16),) * 2

    pieces = call(
        split_kernel,
        (f32(2, ROWS, HALF),) * 2 + (f32(ROWS, HALF),) * 2,
        [SMEM, SMEM, HBM],
        (HBM,) * 4,
        [pltpu.SemaphoreType.DMA((18,))],
    )(owner, me, factor)

    first, _ = over_planes(pieces[0])
    late = swap(pieces[0][0, :8, :128])
    send, below = call(
        start_kernel,
        (f32(PEERS, SLOTS + 1, 8, 128), jax.ShapeDtypeStruct((SLOTS, 1, total * BLOCK), jnp.int32)),
        [SMEM, SMEM, VMEM, VMEM],
        (VMEM, VMEM),
    )(owner, pattern, right_side, late)

    mine = exchange(send)
    other = swap(mine)
    mine, other = (v.reshape(PEERS * (SLOTS + 1), 8, 128) for v in (mine, other))
    meta = call(
        names_kernel,
        jax.ShapeDtypeStruct((META,), jnp.int32),
        [SMEM, SMEM, VMEM, VMEM],
        SMEM,
        [
            pltpu.VMEM((2 * PEERS, 128), jnp.int32),
            pltpu.SMEM((2 * PEERS, 128), jnp.int32),
            pltpu.SemaphoreType.DMA((1,)),
        ],
    )(owner, me, mine, other)

    def place(kernel, outs, parts, work):
        given = [v for own, after, opposite, before in parts for v in (own, after, *opposite, before)]
        given += third if kernel is place_all_kernel else []
        return call(
            kernel, outs, [SMEM, VMEM] + [VMEM] * len(given), (VMEM,) * len(outs), work=work
        )(meta, below, *given)

    d2 = place(place_leaves_kernel, pair(ROWS, 1024), [first], 2 << 20)
    piece, _ = lax.optimization_barrier((pieces[1], first[2]))
    second, _ = over_planes(piece)

    y2, send = call(
        leaves_kernel, (vec, send_shape), [SMEM] + [VMEM] * 5, (VMEM, VMEM), canonical
    )(meta, right_side, mine, other, *d2)
    mine2, other2 = gather(send)
    middles = place(place_middles_kernel, pair(ROWS, 2048) * 2, [first, second], 8 << 20)
    r1, send = call(
        middle_resid_kernel, (vec, f32(8, SLOTS, 8, 128)), [SMEM] + [VMEM] * 5, (VMEM, VMEM), canonical
    )(meta, right_side, mine2, other2, *middles[:2])
    (low, high), _ = lax.optimization_barrier((pieces[2:], (second[1], second[3])))
    before_low, after_high = around(low, 1), around(high, -1)
    before_low, after_high, send = lax.optimization_barrier((before_low, after_high, send))
    line = lax.all_to_all(send, "z", 0, 0)
    (low, high), before_low, after_high, line = lax.optimization_barrier(
        (pieces[2:], before_low, after_high, line)
    )
    relayed = [around(before_low, 1), around(after_high, -1)]
    before_high, after_low = around(high, 1), around(low, -1)
    lines = [lax.ppermute(line, "x", [(i, (i + d) % 4) for i in range(4)]) for d in (1, 2, 3)]
    mine = jnp.concatenate([line, *lines]).reshape(PLACES, 8, 128)
    mine, relayed = lax.optimization_barrier((mine, relayed))
    other = swap(mine)
    y1, send = call(
        middle_kernel, (vec, f32(8, SLOTS, 8, 128)), [SMEM] + [VMEM] * 5, (VMEM, VMEM), canonical
    )(meta, r1, mine, other, *middles[2:])
    line = lax.all_to_all(send, "z", 0, 0)
    lines = [lax.ppermute(line, "x", [(i, (i + d) % 4) for i in range(4)]) for d in (1, 2, 3)]
    mine = jnp.concatenate([line, *lines]).reshape(PLACES, 8, 128)
    third = [*pieces[2:], after_low, after_high, *relayed, before_low, before_high]
    m = place(place_all_kernel, pair(3, ROWS, THIRD), [first, second], 24 << 20)
    mine, m = lax.optimization_barrier((mine, m))
    other = swap(mine)
    r0, send = call(
        top_resid_kernel, (vec, send_shape), [SMEM] + [VMEM] * 7, (VMEM, VMEM), canonical * 2
    )(meta, right_side, mine2, other2, mine, other, *m)
    mine, other = gather(send)
    y0, part = call(
        top_kernel, (vec, part_shape), [SMEM] + [VMEM] * 5, (VMEM, VMEM), canonical
    )(meta, r0, mine, other, *m)

    def adds(level, *terms):
        return call(
            functools.partial(add_kernel, level),
            (vec, part_shape),
            [SMEM] + [VMEM] * (len(terms) + 2),
            (VMEM, VMEM),
        )(meta, *terms, *m)

    def subs(level, y, got):
        return call(
            functools.partial(sub_kernel, level),
            (vec, part_shape),
            [SMEM] + [VMEM] * 4,
            (VMEM, VMEM),
        )(meta, y, got, *m)

    x0, part = adds(1, y0, reduce(part))
    t1, part = subs(1, y1, reduce(part))
    x01, part = adds(2, t1, x0, reduce(part))
    t2, part = subs(2, y2, reduce(part))
    return call(last_kernel, vec, [VMEM] * 3, VMEM)(t2, x01, reduce(part))


def solution(mesh):
    fine = Mesh(mesh.devices.reshape(4, 8, 2, 4), ("x", "z", "c", "y"))
    rows = ("x", "z", "c")
    in_specs = (P(rows, "y"), P(rows, None), P(rows), P("y", rows))
    out_specs = P("y", rows)
    return jax.shard_map(shards, mesh=fine, in_specs=in_specs, out_specs=out_specs, check_vma=False)
```

```python
import functools

import jax
import jax.numpy as jnp
from jax import lax
from jax.experimental import pallas as pl
from jax.experimental.pallas import tpu as pltpu
from jax.sharding import Mesh, PartitionSpec as P

BLOCK = 64
RHS = 16
SLOTS = 3
ROWS = SLOTS * BLOCK
THIRD = 4096
PEERS = 32
PLACES = PEERS * SLOTS
PART = 1024
OWN = 192
ME = OWN + SLOTS
COLUMN = ME + 1
META = 200
HALF = 512
VMEM = pl.BlockSpec(memory_space=pltpu.VMEM)
SMEM = pl.BlockSpec(memory_space=pltpu.SMEM)
HBM = pl.BlockSpec(memory_space=pltpu.HBM)
CHIPS = ("x", "z")


def f32(*shape):
    return jax.ShapeDtypeStruct(shape, jnp.float32)


def left_half():
    return lax.broadcasted_iota(jnp.int32, (8, 128), 1) < BLOCK


def pack(rows):
    return [
        jnp.concatenate(
            [rows[:8, s * BLOCK : (s + 1) * BLOCK], rows[8:, s * BLOCK : (s + 1) * BLOCK]], axis=1
        )
        for s in range(SLOTS)
    ]


def unpack(tiles):
    upper = jnp.concatenate([t[:, :BLOCK] for t in tiles], axis=1)
    lower = jnp.concatenate([t[:, BLOCK:] for t in tiles], axis=1)
    return jnp.concatenate([upper, lower], axis=0)


def only(meta_ref, level, rows):
    slot = lax.broadcasted_iota(jnp.int32, rows.shape, 1) // BLOCK
    keep = jnp.zeros(rows.shape, jnp.bool_)
    for s in range(SLOTS):
        g = meta_ref[OWN + s]
        here = (g >= (2 - level) * 64) & (g < (3 - level) * 64)
        keep = keep | ((slot == s) & here)
    return jnp.where(keep, rows, 0.0)


def halves(x):
    high = x.astype(jnp.bfloat16)
    return high, (x - high.astype(jnp.float32)).astype(jnp.bfloat16)


def to_canonical(meta_ref, level, mine_ref, other_ref, x_ref, extra=False, relative=False):
    base = (2 - level) * 64
    half = left_half()

    def tile(place):
        near = jnp.minimum(place, PLACES - 1)
        far = jnp.maximum(place, PLACES) - PLACES
        if extra:
            near, far = near + near // SLOTS, far + far // SLOTS
        if relative:
            line = PLACES // 4

            def back(at):
                return lax.rem(meta_ref[COLUMN] + 4 - at // line, 4) * line + lax.rem(at, line)

            near, far = back(near), back(far)
        return jnp.where(place >= PLACES, other_ref[far], mine_ref[near])

    for t in range(32):
        a = tile(meta_ref[base + 2 * t])
        b = tile(meta_ref[base + 2 * t + 1])
        top = jnp.where(half, a, pltpu.roll(b, BLOCK, 1))
        bottom = jnp.where(half, pltpu.roll(a, BLOCK, 1), b)
        high, low = halves(jnp.concatenate([top, bottom], axis=0))
        x_ref[0:16, 128 * t : 128 * (t + 1)] = high
        x_ref[16:32, 128 * t : 128 * (t + 1)] = low


def to_places(meta_ref, level, x, out_ref):
    base = (2 - level) * 64
    half = left_half()
    out_ref[...] = jnp.zeros_like(out_ref)
    for t in range(32):
        top = x[0:8, 128 * t : 128 * (t + 1)]
        bottom = x[8:16, 128 * t : 128 * (t + 1)]
        out_ref[meta_ref[base + 2 * t]] = jnp.where(half, top, pltpu.roll(bottom, BLOCK, 1))
        out_ref[meta_ref[base + 2 * t + 1]] = jnp.where(half, pltpu.roll(top, BLOCK, 1), bottom)


def times_rows(x, high, low):
    dims = (((1,), (1,)), ((), ()))
    one = lax.dot_general(high, x, dims, preferred_element_type=jnp.float32)
    two = lax.dot_general(low, x[:RHS], dims, preferred_element_type=jnp.float32)
    return one[:, :RHS] + one[:, RHS:] + two


def times_cols(x, high, low):
    dims = (((1,), (0,)), ((), ()))
    x_high, x_low = halves(x)
    both = jnp.concatenate([x_high, x_low], axis=0)
    one = lax.dot_general(both, high, dims, preferred_element_type=jnp.float32)
    two = lax.dot_general(x_high, low, dims, preferred_element_type=jnp.float32)
    return one[:RHS] + one[RHS:] + two


def spread(tiles, send_ref):
    for peer in range(send_ref.shape[0]):
        for s in range(SLOTS):
            send_ref[peer, s] = tiles[s]


def arrived(got_ref):
    return unpack([jnp.sum(got_ref[:, s], axis=0) for s in range(SLOTS)])


def start_kernel(own_ref, pattern_ref, b_ref, after_ref, send_ref, below_ref):
    tiles = pack(b_ref[...])
    lane = lax.broadcasted_iota(jnp.int32, (8, 128), 1)
    names = jnp.zeros((8, 128), jnp.float32)
    for s in range(SLOTS):
        names = jnp.where(lane == s, own_ref[s].astype(jnp.float32), names)
    spread(tiles, send_ref)
    for peer in range(PEERS):
        send_ref[peer, SLOTS] = names
    lane = lax.broadcasted_iota(jnp.int32, (1, 128), 1)
    for s in range(SLOTS):
        for part in range(12):
            state = state_of(own_ref[s], part)
            for t in range(PART // 128):
                at = part * (PART // BLOCK) + 2 * t
                keep = [
                    jnp.where((state == 1) & (pattern_ref[s, at + i] > 0), -1, 1 << 20)
                    for i in range(2)
                ]
                col = part * PART + t * 128 + lane
                rest = jnp.where(lane < BLOCK, keep[0], keep[1])
                below_ref[s, :, part * PART + t * 128 : part * PART + (t + 1) * 128] = jnp.where(
                    state == 2, col, rest
                )


def names_kernel(own_ref, me_ref, mine_ref, other_ref, meta_ref, names_ref, order_ref, sem):
    row = lax.broadcasted_iota(jnp.int32, (8, 128), 0)
    for far, ref in enumerate((mine_ref, other_ref)):
        for k in range(PEERS // 8):
            names = ref[(SLOTS + 1) * 8 * k + SLOTS]
            for r in range(1, 8):
                names = jnp.where(row == r, ref[(SLOTS + 1) * (8 * k + r) + SLOTS], names)
            at = far * PEERS + 8 * k
            names_ref[at : at + 8] = names.astype(jnp.int32)
    copy = pltpu.make_async_copy(names_ref, order_ref, sem.at[0])
    copy.start()
    copy.wait()
    for chip in range(2 * PEERS):
        for s in range(SLOTS):
            meta_ref[order_ref[chip, s]] = chip * SLOTS + s
    for s in range(SLOTS):
        meta_ref[OWN + s] = own_ref[s]
    meta_ref[ME] = me_ref[0]
    meta_ref[COLUMN] = me_ref[1]
    for i in range(COLUMN + 1, META):
        meta_ref[i] = 0


def turn(g, q):
    leaf = jnp.where(g // 16 == 3, 0, g // 16)
    first = jnp.where(q == 1, 1, 0)
    second = jnp.where(q == 0, 2, 0)
    return jnp.where(g < 64, leaf, jnp.where(g < 96, first, jnp.where(g < 128, second, 0)))


def part_of(e, g, q):
    return 3 * q + lax.rem(e + turn(g, q), 3)


def rows_of(s):
    return slice(s * BLOCK, (s + 1) * BLOCK)


def split_kernel(own_ref, me_ref, factor_ref, *refs):
    first, second, third_a, third_b, sems = refs
    copies = []
    for e in range(3):
        for s in range(SLOTS):
            at = lax.rem(e + turn(own_ref[s], me_ref[0]), 3) * PART
            for h in range(2):
                out = (third_a, third_b)[h] if e == 2 else (first, second)[e].at[h]
                copies.append(
                    pltpu.make_async_copy(
                        factor_ref.at[rows_of(s), pl.ds(pl.multiple_of(at + h * HALF, HALF), HALF)],
                        out.at[rows_of(s)],
                        sems.at[len(copies)],
                    )
                )
    for copy in copies:
        copy.start()
    for copy in copies:
        copy.wait()


def state_of(g, part):
    group = (g - 64) // 32
    leaf = jnp.where(part == g // 16, 2, 0)
    own = (part == 4 + 2 * group) | (part == 5 + 2 * group)
    below = (part == 2 * group) | (part == 2 * group + 1)
    middle = jnp.where(own, 2, jnp.where(below, 1, 0))
    return jnp.where(g < 64, leaf, jnp.where(g < 128, middle, jnp.where(part >= 8, 2, 1)))


def masked(below_ref, s, g, part, h, block):
    row = g * BLOCK + lax.broadcasted_iota(jnp.int32, (BLOCK, HALF), 0)
    col0 = pl.multiple_of(part * PART + h * HALF, HALF)
    return halves(jnp.where(row > below_ref[s, :, pl.ds(col0, HALF)], block, 0.0))


def sources(e, meta_ref, refs):
    for d in range(4):
        q = lax.rem(meta_ref[ME] + d, 4)
        for s in range(SLOTS):
            g = meta_ref[OWN + s]
            for h in range(2):
                if e == 2:
                    src = refs[2 * d + h].at[rows_of(s)]
                elif d == 2:
                    src = refs[2 + h].at[rows_of(s)]
                else:
                    src = refs[(0, 1, 0, 4)[d]].at[h, rows_of(s)]
                yield s, h, g, part_of(e, g, q), src


def put(refs, s, at, pair):
    for ref, value in zip(refs, pair):
        ref[rows_of(s), pl.ds(pl.multiple_of(at, HALF), HALF)] = value


def place_leaves_kernel(meta_ref, below_ref, *refs):
    for s, h, g, part, src in sources(0, meta_ref, refs[:5]):

        @pl.when((g < 64) & (part == g // 16))
        def _(s=s, h=h, g=g, part=part, src=src):
            put(refs[5:7], s, h * HALF, masked(below_ref, s, g, part, h, src[...]))


def place_middles_kernel(meta_ref, below_ref, *refs):
    for e in range(2):
        for s, h, g, part, src in sources(e, meta_ref, refs[5 * e : 5 * e + 5]):
            mine = (g >= 64) & (g < 128) & (state_of(g, part) > 0)
            at = lax.rem(part, 2) * PART + h * HALF

            @pl.when(mine & (part < 4))
            def _(s=s, h=h, g=g, part=part, src=src, at=at):
                put(refs[10:12], s, at, masked(below_ref, s, g, part, h, src[...]))

            @pl.when(mine & (part >= 4))
            def _(s=s, h=h, g=g, part=part, src=src, at=at):
                put(refs[12:14], s, at, masked(below_ref, s, g, part, h, src[...]))


def place_all_kernel(meta_ref, below_ref, *refs):
    for e in range(3):
        for s, h, g, part, src in sources(e, meta_ref, refs[5 * e : (5, 10, 18)[e]]):
            at = lax.rem(part, 4) * PART + h * HALF
            outs = [ref.at[part // 4] for ref in refs[18:20]]
            put(outs, s, at, masked(below_ref, s, g, part, h, src[...]))


def own_products(meta_ref, base, blocks, groups, x_ref, high_ref, low_ref):
    wide = high_ref.shape[1]
    outs = []
    for s in range(SLOTS):
        group = jnp.clip((meta_ref[OWN + s] - base) // blocks, 0, groups - 1)
        x = x_ref[:, pl.ds(pl.multiple_of(group * wide, wide), wide)]
        outs.append(times_rows(x, high_ref[rows_of(s)], low_ref[rows_of(s)]))
    return jnp.concatenate(outs, axis=0).T


def leaves_kernel(meta_ref, b_ref, mine_ref, other_ref, high_ref, low_ref, y_ref, send_ref, x_ref):
    to_canonical(meta_ref, 2, mine_ref, other_ref, x_ref, True)
    y = only(meta_ref, 2, own_products(meta_ref, 0, 16, 4, x_ref, high_ref, low_ref) + b_ref[...])
    y_ref[...] = y
    spread(pack(y), send_ref)


def middle_resid_kernel(meta_ref, b_ref, mine_ref, other_ref, high_ref, low_ref, r_ref, send_ref, x_ref):
    to_canonical(meta_ref, 2, mine_ref, other_ref, x_ref)
    r = only(meta_ref, 1, b_ref[...] - own_products(meta_ref, 64, 32, 2, x_ref, high_ref, low_ref))
    r_ref[...] = r
    spread(pack(r), send_ref)


def middle_kernel(meta_ref, r_ref, mine_ref, other_ref, high_ref, low_ref, y_ref, send_ref, x_ref):
    to_canonical(meta_ref, 1, mine_ref, other_ref, x_ref, relative=True)
    y = only(meta_ref, 1, own_products(meta_ref, 64, 32, 2, x_ref, high_ref, low_ref) + r_ref[...])
    y_ref[...] = y
    spread(pack(y), send_ref)


def update_kernel(meta_ref, mine_ref, other_ref, high_ref, low_ref, upd_ref, x_ref):
    to_canonical(meta_ref, 2, mine_ref, other_ref, x_ref)
    upd_ref[...] = times_rows(x_ref[...], high_ref[0], low_ref[0])


def top_resid_kernel(meta_ref, b_ref, upd_ref, mine_ref, other_ref, high_ref, low_ref, r_ref, send_ref, x_ref):
    to_canonical(meta_ref, 1, mine_ref, other_ref, x_ref, relative=True)
    upd = upd_ref[...] + times_rows(x_ref[...], high_ref[1], low_ref[1])
    r = only(meta_ref, 0, b_ref[...] - upd.T)
    r_ref[...] = r
    spread(pack(r), send_ref)


def top_kernel(meta_ref, r_ref, mine_ref, other_ref, high_ref, low_ref, y_ref, part_ref, x_ref):
    to_canonical(meta_ref, 0, mine_ref, other_ref, x_ref)
    y = only(meta_ref, 0, times_rows(x_ref[...], high_ref[2], low_ref[2]).T) + r_ref[...]
    y_ref[...] = y
    to_places(meta_ref, 0, times_cols(y, high_ref[2], low_ref[2]), part_ref)


def add_kernel(level, meta_ref, *refs):
    terms = refs[:-5]
    got_ref, high_ref, low_ref, x_out_ref, part_ref = refs[-5:]
    x = arrived(got_ref)
    for term in terms:
        x = x + term[...]
    x_out_ref[...] = x
    to_places(meta_ref, level, times_cols(x, high_ref[2 - level], low_ref[2 - level]), part_ref)


def sub_kernel(level, meta_ref, y_ref, got_ref, high_ref, low_ref, t_ref, part_ref):
    t = only(meta_ref, level, y_ref[...] - arrived(got_ref))
    t_ref[...] = t
    to_places(meta_ref, level, times_cols(t, high_ref[2 - level], low_ref[2 - level]), part_ref)


def last_kernel(t_ref, x_ref, got_ref, out_ref):
    out_ref[...] = t_ref[...] + x_ref[...] + arrived(got_ref)


def swap(x):
    return lax.ppermute(x, "c", [(0, 1), (1, 0)])


def exchange(x):
    return lax.all_to_all(x, CHIPS, 0, 0)


def gather(send):
    mine = exchange(send)
    other = swap(mine)
    return mine.reshape(PLACES, 8, 128), other.reshape(PLACES, 8, 128)


def reduce(part):
    far = swap(part[PLACES:])
    return exchange((part[:PLACES] + far).reshape(PEERS, SLOTS, 8, 128))


def around(x, step):
    return lax.ppermute(x, "y", [(i, (i + step) % 4) for i in range(4)])


def over_planes(part, tie=None):
    before, after = around(part, 1), around(part, -1)
    if tie is not None:
        before, after, tie = lax.optimization_barrier((before, after, tie))
    else:
        before, after = lax.optimization_barrier((before, after))
    opposite = [around(before[0], 1), around(after[1], -1)]
    return (part, after, opposite, before), tie


def call(kernel, outs, specs, out_specs, scratch=(), work=0):
    return pl.pallas_call(
        kernel,
        out_shape=outs,
        in_specs=specs,
        out_specs=out_specs,
        scratch_shapes=list(scratch),
        compiler_params=pltpu.CompilerParams(vmem_limit_bytes=28 * 1024 * 1024),
        cost_estimate=pl.CostEstimate(flops=0, bytes_accessed=work, transcendentals=0) if work else None,
    )


def shards(factor, pattern, owner, right_side):
    total = pattern.shape[1]
    vec = f32(RHS, ROWS)
    send_shape = f32(PEERS, SLOTS, 8, 128)
    part_shape = f32(2 * PLACES, 8, 128)
    me = jnp.stack([lax.axis_index("y"), lax.axis_index("x")]).astype(jnp.int32)
    canonical = [pltpu.VMEM((2 * RHS, THIRD), jnp.bfloat16)]

    def pair(*shape):
        return (jax.ShapeDtypeStruct(shape, jnp.bfloat16),) * 2

    pieces = call(
        split_kernel,
        (f32(2, ROWS, HALF),) * 2 + (f32(ROWS, HALF),) * 2,
        [SMEM, SMEM, HBM],
        (HBM,) * 4,
        [pltpu.SemaphoreType.DMA((18,))],
    )(owner, me, factor)

    first, _ = over_planes(pieces[0])
    late = swap(pieces[0][0, :8, :128])
    send, below = call(
        start_kernel,
        (f32(PEERS, SLOTS + 1, 8, 128), jax.ShapeDtypeStruct((SLOTS, 1, total * BLOCK), jnp.int32)),
        [SMEM, SMEM, VMEM, VMEM],
        (VMEM, VMEM),
    )(owner, pattern, right_side, late)

    mine = exchange(send)
    other = swap(mine)
    mine, other = (v.reshape(PEERS * (SLOTS + 1), 8, 128) for v in (mine, other))
    meta = call(
        names_kernel,
        jax.ShapeDtypeStruct((META,), jnp.int32),
        [SMEM, SMEM, VMEM, VMEM],
        SMEM,
        [
            pltpu.VMEM((2 * PEERS, 128), jnp.int32),
            pltpu.SMEM((2 * PEERS, 128), jnp.int32),
            pltpu.SemaphoreType.DMA((1,)),
        ],
    )(owner, me, mine, other)

    def place(kernel, outs, parts, work):
        given = [v for own, after, opposite, before in parts for v in (own, after, *opposite, before)]
        given += third if kernel is place_all_kernel else []
        return call(
            kernel, outs, [SMEM, VMEM] + [VMEM] * len(given), (VMEM,) * len(outs), work=work
        )(meta, below, *given)

    d2 = place(place_leaves_kernel, pair(ROWS, 1024), [first], 2 << 20)
    piece, _ = lax.optimization_barrier((pieces[1], first[2]))
    second, _ = over_planes(piece)

    y2, send = call(
        leaves_kernel, (vec, send_shape), [SMEM] + [VMEM] * 5, (VMEM, VMEM), canonical
    )(meta, right_side, mine, other, *d2)
    mine2, other2 = gather(send)
    middles = place(place_middles_kernel, pair(ROWS, 2048) * 2, [first, second], 8 << 20)
    r1, send = call(
        middle_resid_kernel, (vec, f32(8, SLOTS, 8, 128)), [SMEM] + [VMEM] * 5, (VMEM, VMEM), canonical
    )(meta, right_side, mine2, other2, *middles[:2])
    (low, high), _ = lax.optimization_barrier((pieces[2:], (second[1], second[3])))
    before_low, after_high = around(low, 1), around(high, -1)
    before_low, after_high, send = lax.optimization_barrier((before_low, after_high, send))
    line = lax.all_to_all(send, "z", 0, 0)
    (low, high), before_low, after_high, line = lax.optimization_barrier(
        (pieces[2:], before_low, after_high, line)
    )
    relayed = [around(before_low, 1), around(after_high, -1)]
    before_high, after_low = around(high, 1), around(low, -1)
    lines = [lax.ppermute(line, "x", [(i, (i + d) % 4) for i in range(4)]) for d in (1, 2, 3)]
    mine = jnp.concatenate([line, *lines]).reshape(PLACES, 8, 128)
    mine, relayed = lax.optimization_barrier((mine, relayed))
    other = swap(mine)
    y1, send = call(
        middle_kernel, (vec, f32(8, SLOTS, 8, 128)), [SMEM] + [VMEM] * 5, (VMEM, VMEM), canonical
    )(meta, r1, mine, other, *middles[2:])
    line = lax.all_to_all(send, "z", 0, 0)
    lines = [lax.ppermute(line, "x", [(i, (i + d) % 4) for i in range(4)]) for d in (1, 2, 3)]
    mine = jnp.concatenate([line, *lines]).reshape(PLACES, 8, 128)
    third = [*pieces[2:], after_low, after_high, *relayed, before_low, before_high]
    m = place(place_all_kernel, pair(3, ROWS, THIRD), [first, second], 24 << 20)
    mine, m = lax.optimization_barrier((mine, m))
    other = swap(mine)
    upd = call(
        update_kernel, f32(ROWS, RHS), [SMEM] + [VMEM] * 4, VMEM, canonical, 4 << 20
    )(meta, mine2, other2, *m)
    r0, send = call(
        top_resid_kernel, (vec, send_shape), [SMEM] + [VMEM] * 6, (VMEM, VMEM), canonical
    )(meta, right_side, upd, mine, other, *m)
    mine, other = gather(send)
    y0, part = call(
        top_kernel, (vec, part_shape), [SMEM] + [VMEM] * 5, (VMEM, VMEM), canonical
    )(meta, r0, mine, other, *m)

    def adds(level, *terms):
        return call(
            functools.partial(add_kernel, level),
            (vec, part_shape),
            [SMEM] + [VMEM] * (len(terms) + 2),
            (VMEM, VMEM),
        )(meta, *terms, *m)

    def subs(level, y, got):
        return call(
            functools.partial(sub_kernel, level),
            (vec, part_shape),
            [SMEM] + [VMEM] * 4,
            (VMEM, VMEM),
        )(meta, y, got, *m)

    x0, part = adds(1, y0, reduce(part))
    t1, part = subs(1, y1, reduce(part))
    x01, part = adds(2, t1, x0, reduce(part))
    t2, part = subs(2, y2, reduce(part))
    return call(last_kernel, vec, [VMEM] * 3, VMEM)(t2, x01, reduce(part))


def solution(mesh):
    fine = Mesh(mesh.devices.reshape(4, 8, 2, 4), ("x", "z", "c", "y"))
    rows = ("x", "z", "c")
    in_specs = (P(rows, "y"), P(rows, None), P(rows), P("y", rows))
    out_specs = P("y", rows)
    return jax.shard_map(shards, mesh=fine, in_specs=in_specs, out_specs=out_specs, check_vma=False)
```

```python
import functools

import jax
import jax.numpy as jnp
from jax import lax
from jax.experimental import pallas as pl
from jax.experimental.pallas import tpu as pltpu
from jax.sharding import Mesh, PartitionSpec as P

BLOCK = 64
RHS = 16
SLOTS = 3
ROWS = SLOTS * BLOCK
THIRD = 4096
PEERS = 32
PLACES = PEERS * SLOTS
PART = 1024
OWN = 192
ME = OWN + SLOTS
COLUMN = ME + 1
META = 200
HALF = 512
VMEM = pl.BlockSpec(memory_space=pltpu.VMEM)
SMEM = pl.BlockSpec(memory_space=pltpu.SMEM)
HBM = pl.BlockSpec(memory_space=pltpu.HBM)
CHIPS = ("x", "z")


def f32(*shape):
    return jax.ShapeDtypeStruct(shape, jnp.float32)


def left_half():
    return lax.broadcasted_iota(jnp.int32, (8, 128), 1) < BLOCK


def pack(rows):
    return [
        jnp.concatenate(
            [rows[:8, s * BLOCK : (s + 1) * BLOCK], rows[8:, s * BLOCK : (s + 1) * BLOCK]], axis=1
        )
        for s in range(SLOTS)
    ]


def unpack(tiles):
    upper = jnp.concatenate([t[:, :BLOCK] for t in tiles], axis=1)
    lower = jnp.concatenate([t[:, BLOCK:] for t in tiles], axis=1)
    return jnp.concatenate([upper, lower], axis=0)


def only(meta_ref, level, rows):
    slot = lax.broadcasted_iota(jnp.int32, rows.shape, 1) // BLOCK
    keep = jnp.zeros(rows.shape, jnp.bool_)
    for s in range(SLOTS):
        g = meta_ref[OWN + s]
        here = (g >= (2 - level) * 64) & (g < (3 - level) * 64)
        keep = keep | ((slot == s) & here)
    return jnp.where(keep, rows, 0.0)


def halves(x):
    high = x.astype(jnp.bfloat16)
    return high, (x - high.astype(jnp.float32)).astype(jnp.bfloat16)


def to_canonical(meta_ref, level, mine_ref, other_ref, x_ref, extra=False, relative=False):
    base = (2 - level) * 64
    half = left_half()

    def tile(place):
        near = jnp.minimum(place, PLACES - 1)
        far = jnp.maximum(place, PLACES) - PLACES
        if extra:
            near, far = near + near // SLOTS, far + far // SLOTS
        if relative:
            line = PLACES // 4

            def back(at):
                return lax.rem(meta_ref[COLUMN] + 4 - at // line, 4) * line + lax.rem(at, line)

            near, far = back(near), back(far)
        return jnp.where(place >= PLACES, other_ref[far], mine_ref[near])

    for t in range(32):
        a = tile(meta_ref[base + 2 * t])
        b = tile(meta_ref[base + 2 * t + 1])
        top = jnp.where(half, a, pltpu.roll(b, BLOCK, 1))
        bottom = jnp.where(half, pltpu.roll(a, BLOCK, 1), b)
        high, low = halves(jnp.concatenate([top, bottom], axis=0))
        x_ref[0:16, 128 * t : 128 * (t + 1)] = high
        x_ref[16:32, 128 * t : 128 * (t + 1)] = low


def to_places(meta_ref, level, x, out_ref):
    base = (2 - level) * 64
    half = left_half()
    for t in range(32):
        top = x[0:8, 128 * t : 128 * (t + 1)]
        bottom = x[8:16, 128 * t : 128 * (t + 1)]
        out_ref[meta_ref[base + 2 * t]] = jnp.where(half, top, pltpu.roll(bottom, BLOCK, 1))
        out_ref[meta_ref[base + 2 * t + 1]] = jnp.where(half, pltpu.roll(top, BLOCK, 1), bottom)


def times_rows(x, high, low):
    dims = (((1,), (1,)), ((), ()))
    one = lax.dot_general(high, x, dims, preferred_element_type=jnp.float32)
    two = lax.dot_general(low, x[:RHS], dims, preferred_element_type=jnp.float32)
    return one[:, :RHS] + one[:, RHS:] + two


def times_cols(x, high, low):
    dims = (((1,), (0,)), ((), ()))
    x_high, x_low = halves(x)
    both = jnp.concatenate([x_high, x_low], axis=0)
    one = lax.dot_general(both, high, dims, preferred_element_type=jnp.float32)
    two = lax.dot_general(x_high, low, dims, preferred_element_type=jnp.float32)
    return one[:RHS] + one[RHS:] + two


def spread(tiles, send_ref):
    for peer in range(send_ref.shape[0]):
        for s in range(SLOTS):
            send_ref[peer, s] = tiles[s]


def arrived(got_ref):
    return unpack([jnp.sum(got_ref[:, s], axis=0) for s in range(SLOTS)])


def start_kernel(own_ref, pattern_ref, b_ref, after_ref, send_ref, below_ref):
    tiles = pack(b_ref[...])
    lane = lax.broadcasted_iota(jnp.int32, (8, 128), 1)
    names = jnp.zeros((8, 128), jnp.float32)
    for s in range(SLOTS):
        names = jnp.where(lane == s, own_ref[s].astype(jnp.float32), names)
    spread(tiles, send_ref)
    for peer in range(PEERS):
        send_ref[peer, SLOTS] = names
    lane = lax.broadcasted_iota(jnp.int32, (1, 128), 1)
    for s in range(SLOTS):
        for part in range(12):
            state = state_of(own_ref[s], part)
            for t in range(PART // 128):
                at = part * (PART // BLOCK) + 2 * t
                keep = [
                    jnp.where((state == 1) & (pattern_ref[s, at + i] > 0), -1, 1 << 20)
                    for i in range(2)
                ]
                col = part * PART + t * 128 + lane
                rest = jnp.where(lane < BLOCK, keep[0], keep[1])
                below_ref[s, :, part * PART + t * 128 : part * PART + (t + 1) * 128] = jnp.where(
                    state == 2, col, rest
                )


def names_kernel(own_ref, me_ref, mine_ref, other_ref, meta_ref, names_ref, order_ref, sem):
    row = lax.broadcasted_iota(jnp.int32, (8, 128), 0)
    for far, ref in enumerate((mine_ref, other_ref)):
        for k in range(PEERS // 8):
            names = ref[(SLOTS + 1) * 8 * k + SLOTS]
            for r in range(1, 8):
                names = jnp.where(row == r, ref[(SLOTS + 1) * (8 * k + r) + SLOTS], names)
            at = far * PEERS + 8 * k
            names_ref[at : at + 8] = names.astype(jnp.int32)
    copy = pltpu.make_async_copy(names_ref, order_ref, sem.at[0])
    copy.start()
    copy.wait()
    for chip in range(2 * PEERS):
        for s in range(SLOTS):
            meta_ref[order_ref[chip, s]] = chip * SLOTS + s
    for s in range(SLOTS):
        meta_ref[OWN + s] = own_ref[s]
    meta_ref[ME] = me_ref[0]
    meta_ref[COLUMN] = me_ref[1]
    for i in range(COLUMN + 1, META):
        meta_ref[i] = 0


def turn(g, q):
    leaf = jnp.where(g // 16 == 3, 0, g // 16)
    first = jnp.where(q == 1, 1, 0)
    second = jnp.where(q == 0, 2, 0)
    return jnp.where(g < 64, leaf, jnp.where(g < 96, first, jnp.where(g < 128, second, 0)))


def part_of(e, g, q):
    return 3 * q + lax.rem(e + turn(g, q), 3)


def rows_of(s):
    return slice(s * BLOCK, (s + 1) * BLOCK)


def split_kernel(own_ref, me_ref, factor_ref, *refs):
    first, second, third_a, third_b, sems = refs
    copies = []
    for e in range(3):
        for s in range(SLOTS):
            at = lax.rem(e + turn(own_ref[s], me_ref[0]), 3) * PART
            for h in range(2):
                out = (third_a, third_b)[h] if e == 2 else (first, second)[e].at[h]
                copies.append(
                    pltpu.make_async_copy(
                        factor_ref.at[rows_of(s), pl.ds(pl.multiple_of(at + h * HALF, HALF), HALF)],
                        out.at[rows_of(s)],
                        sems.at[len(copies)],
                    )
                )
    for copy in copies:
        copy.start()
    for copy in copies:
        copy.wait()


def state_of(g, part):
    group = (g - 64) // 32
    leaf = jnp.where(part == g // 16, 2, 0)
    own = (part == 4 + 2 * group) | (part == 5 + 2 * group)
    below = (part == 2 * group) | (part == 2 * group + 1)
    middle = jnp.where(own, 2, jnp.where(below, 1, 0))
    return jnp.where(g < 64, leaf, jnp.where(g < 128, middle, jnp.where(part >= 8, 2, 1)))


def masked(below_ref, s, g, part, h, block):
    row = g * BLOCK + lax.broadcasted_iota(jnp.int32, (BLOCK, HALF), 0)
    col0 = pl.multiple_of(part * PART + h * HALF, HALF)
    return halves(jnp.where(row > below_ref[s, :, pl.ds(col0, HALF)], block, 0.0))


def sources(e, meta_ref, refs):
    for d in range(4):
        q = lax.rem(meta_ref[ME] + d, 4)
        for s in range(SLOTS):
            g = meta_ref[OWN + s]
            for h in range(2):
                if e == 2:
                    src = refs[2 * d + h].at[rows_of(s)]
                elif d == 2:
                    src = refs[2 + h].at[rows_of(s)]
                else:
                    src = refs[(0, 1, 0, 4)[d]].at[h, rows_of(s)]
                yield s, h, g, part_of(e, g, q), src


def put(refs, s, at, pair):
    for ref, value in zip(refs, pair):
        ref[rows_of(s), pl.ds(pl.multiple_of(at, HALF), HALF)] = value


def place_leaves_kernel(meta_ref, below_ref, *refs):
    for s, h, g, part, src in sources(0, meta_ref, refs[:5]):

        @pl.when((g < 64) & (part == g // 16))
        def _(s=s, h=h, g=g, part=part, src=src):
            put(refs[5:7], s, h * HALF, masked(below_ref, s, g, part, h, src[...]))


def place_middles_kernel(meta_ref, below_ref, *refs):
    for e in range(2):
        for s, h, g, part, src in sources(e, meta_ref, refs[5 * e : 5 * e + 5]):
            mine = (g >= 64) & (g < 128) & (state_of(g, part) > 0)
            at = lax.rem(part, 2) * PART + h * HALF

            @pl.when(mine & (part < 4))
            def _(s=s, h=h, g=g, part=part, src=src, at=at):
                put(refs[10:12], s, at, masked(below_ref, s, g, part, h, src[...]))

            @pl.when(mine & (part >= 4))
            def _(s=s, h=h, g=g, part=part, src=src, at=at):
                put(refs[12:14], s, at, masked(below_ref, s, g, part, h, src[...]))


def place_all_kernel(meta_ref, below_ref, *refs):
    for e in range(3):
        for s, h, g, part, src in sources(e, meta_ref, refs[5 * e : (5, 10, 18)[e]]):
            at = lax.rem(part, 4) * PART + h * HALF
            outs = [ref.at[part // 4] for ref in refs[18:20]]
            put(outs, s, at, masked(below_ref, s, g, part, h, src[...]))


def own_products(meta_ref, base, blocks, groups, x_ref, high_ref, low_ref):
    wide = high_ref.shape[1]
    outs = []
    for s in range(SLOTS):
        group = jnp.clip((meta_ref[OWN + s] - base) // blocks, 0, groups - 1)
        x = x_ref[:, pl.ds(pl.multiple_of(group * wide, wide), wide)]
        outs.append(times_rows(x, high_ref[rows_of(s)], low_ref[rows_of(s)]))
    return jnp.concatenate(outs, axis=0).T


def leaves_kernel(meta_ref, b_ref, mine_ref, other_ref, high_ref, low_ref, y_ref, send_ref, x_ref):
    to_canonical(meta_ref, 2, mine_ref, other_ref, x_ref, True)
    y = only(meta_ref, 2, own_products(meta_ref, 0, 16, 4, x_ref, high_ref, low_ref) + b_ref[...])
    y_ref[...] = y
    spread(pack(y), send_ref)


def middle_resid_kernel(meta_ref, b_ref, mine_ref, other_ref, high_ref, low_ref, r_ref, send_ref, x_ref):
    to_canonical(meta_ref, 2, mine_ref, other_ref, x_ref)
    r = only(meta_ref, 1, b_ref[...] - own_products(meta_ref, 64, 32, 2, x_ref, high_ref, low_ref))
    r_ref[...] = r
    spread(pack(r), send_ref)


def middle_kernel(meta_ref, r_ref, mine_ref, other_ref, high_ref, low_ref, y_ref, send_ref, x_ref):
    to_canonical(meta_ref, 1, mine_ref, other_ref, x_ref, relative=True)
    y = only(meta_ref, 1, own_products(meta_ref, 64, 32, 2, x_ref, high_ref, low_ref) + r_ref[...])
    y_ref[...] = y
    spread(pack(y), send_ref)


def update_kernel(meta_ref, mine_ref, other_ref, high_ref, low_ref, upd_ref, x_ref):
    to_canonical(meta_ref, 2, mine_ref, other_ref, x_ref)
    upd_ref[...] = times_rows(x_ref[...], high_ref[0], low_ref[0])


def top_resid_kernel(meta_ref, b_ref, upd_ref, mine_ref, other_ref, high_ref, low_ref, r_ref, send_ref, x_ref):
    to_canonical(meta_ref, 1, mine_ref, other_ref, x_ref, relative=True)
    upd = upd_ref[...] + times_rows(x_ref[...], high_ref[1], low_ref[1])
    r = only(meta_ref, 0, b_ref[...] - upd.T)
    r_ref[...] = r
    spread(pack(r), send_ref)


def top_kernel(meta_ref, r_ref, mine_ref, other_ref, high_ref, low_ref, y_ref, part_ref, x_ref):
    to_canonical(meta_ref, 0, mine_ref, other_ref, x_ref)
    y = only(meta_ref, 0, times_rows(x_ref[...], high_ref[2], low_ref[2]).T) + r_ref[...]
    y_ref[...] = y
    to_places(meta_ref, 0, times_cols(y, high_ref[2], low_ref[2]), part_ref)


def add_kernel(level, meta_ref, *refs):
    terms = refs[:-5]
    got_ref, high_ref, low_ref, x_out_ref, part_ref = refs[-5:]
    x = only(meta_ref, level - 1, arrived(got_ref))
    for term in terms:
        x = x + term[...]
    x_out_ref[...] = x
    to_places(meta_ref, level, times_cols(x, high_ref[2 - level], low_ref[2 - level]), part_ref)


def sub_kernel(level, meta_ref, y_ref, got_ref, high_ref, low_ref, t_ref, part_ref):
    t = only(meta_ref, level, y_ref[...] - arrived(got_ref))
    t_ref[...] = t
    to_places(meta_ref, level, times_cols(t, high_ref[2 - level], low_ref[2 - level]), part_ref)


def last_kernel(meta_ref, t_ref, x_ref, got_ref, out_ref):
    out_ref[...] = t_ref[...] + x_ref[...] + only(meta_ref, 2, arrived(got_ref))


def swap(x):
    return lax.ppermute(x, "c", [(0, 1), (1, 0)])


def exchange(x):
    return lax.all_to_all(x, CHIPS, 0, 0)


def gather(send):
    mine = exchange(send)
    other = swap(mine)
    return mine.reshape(PLACES, 8, 128), other.reshape(PLACES, 8, 128)


def reduce(part):
    far = swap(part[PLACES:])
    return exchange((part[:PLACES] + far).reshape(PEERS, SLOTS, 8, 128))


def around(x, step):
    return lax.ppermute(x, "y", [(i, (i + step) % 4) for i in range(4)])


def over_planes(part, tie=None):
    before, after = around(part, 1), around(part, -1)
    if tie is not None:
        before, after, tie = lax.optimization_barrier((before, after, tie))
    else:
        before, after = lax.optimization_barrier((before, after))
    opposite = [around(before[0], 1), around(after[1], -1)]
    return (part, after, opposite, before), tie


def call(kernel, outs, specs, out_specs, scratch=(), work=0):
    return pl.pallas_call(
        kernel,
        out_shape=outs,
        in_specs=specs,
        out_specs=out_specs,
        scratch_shapes=list(scratch),
        compiler_params=pltpu.CompilerParams(vmem_limit_bytes=28 * 1024 * 1024),
        cost_estimate=pl.CostEstimate(flops=0, bytes_accessed=work, transcendentals=0) if work else None,
    )


def shards(factor, pattern, owner, right_side):
    total = pattern.shape[1]
    vec = f32(RHS, ROWS)
    send_shape = f32(PEERS, SLOTS, 8, 128)
    part_shape = f32(2 * PLACES, 8, 128)
    me = jnp.stack([lax.axis_index("y"), lax.axis_index("x")]).astype(jnp.int32)
    canonical = [pltpu.VMEM((2 * RHS, THIRD), jnp.bfloat16)]

    def pair(*shape):
        return (jax.ShapeDtypeStruct(shape, jnp.bfloat16),) * 2

    pieces = call(
        split_kernel,
        (f32(2, ROWS, HALF),) * 2 + (f32(ROWS, HALF),) * 2,
        [SMEM, SMEM, HBM],
        (HBM,) * 4,
        [pltpu.SemaphoreType.DMA((18,))],
    )(owner, me, factor)

    first, _ = over_planes(pieces[0])
    late = swap(pieces[0][0, :8, :128])
    send, below = call(
        start_kernel,
        (f32(PEERS, SLOTS + 1, 8, 128), jax.ShapeDtypeStruct((SLOTS, 1, total * BLOCK), jnp.int32)),
        [SMEM, SMEM, VMEM, VMEM],
        (VMEM, VMEM),
    )(owner, pattern, right_side, late)

    mine = exchange(send)
    other = swap(mine)
    mine, other = (v.reshape(PEERS * (SLOTS + 1), 8, 128) for v in (mine, other))
    meta = call(
        names_kernel,
        jax.ShapeDtypeStruct((META,), jnp.int32),
        [SMEM, SMEM, VMEM, VMEM],
        SMEM,
        [
            pltpu.VMEM((2 * PEERS, 128), jnp.int32),
            pltpu.SMEM((2 * PEERS, 128), jnp.int32),
            pltpu.SemaphoreType.DMA((1,)),
        ],
    )(owner, me, mine, other)

    def place(kernel, outs, parts, work):
        given = [v for own, after, opposite, before in parts for v in (own, after, *opposite, before)]
        given += third if kernel is place_all_kernel else []
        return call(
            kernel, outs, [SMEM, VMEM] + [VMEM] * len(given), (VMEM,) * len(outs), work=work
        )(meta, below, *given)

    d2 = place(place_leaves_kernel, pair(ROWS, 1024), [first], 2 << 20)
    piece, _ = lax.optimization_barrier((pieces[1], first[2]))
    second, _ = over_planes(piece)

    y2, send = call(
        leaves_kernel, (vec, send_shape), [SMEM] + [VMEM] * 5, (VMEM, VMEM), canonical
    )(meta, right_side, mine, other, *d2)
    mine2, other2 = gather(send)
    middles = place(place_middles_kernel, pair(ROWS, 2048) * 2, [first, second], 8 << 20)
    r1, send = call(
        middle_resid_kernel, (vec, f32(8, SLOTS, 8, 128)), [SMEM] + [VMEM] * 5, (VMEM, VMEM), canonical
    )(meta, right_side, mine2, other2, *middles[:2])
    (low, high), _ = lax.optimization_barrier((pieces[2:], (second[1], second[3])))
    before_low, after_high = around(low, 1), around(high, -1)
    before_low, after_high, send = lax.optimization_barrier((before_low, after_high, send))
    line = lax.all_to_all(send, "z", 0, 0)
    (low, high), before_low, after_high, line = lax.optimization_barrier(
        (pieces[2:], before_low, after_high, line)
    )
    relayed = [around(before_low, 1), around(after_high, -1)]
    before_high, after_low = around(high, 1), around(low, -1)
    lines = [lax.ppermute(line, "x", [(i, (i + d) % 4) for i in range(4)]) for d in (1, 2, 3)]
    mine = jnp.concatenate([line, *lines]).reshape(PLACES, 8, 128)
    mine, relayed = lax.optimization_barrier((mine, relayed))
    other = swap(mine)
    y1, send = call(
        middle_kernel, (vec, f32(8, SLOTS, 8, 128)), [SMEM] + [VMEM] * 5, (VMEM, VMEM), canonical
    )(meta, r1, mine, other, *middles[2:])
    line = lax.all_to_all(send, "z", 0, 0)
    lines = [lax.ppermute(line, "x", [(i, (i + d) % 4) for i in range(4)]) for d in (1, 2, 3)]
    mine = jnp.concatenate([line, *lines]).reshape(PLACES, 8, 128)
    third = [*pieces[2:], after_low, after_high, *relayed, before_low, before_high]
    m = place(place_all_kernel, pair(3, ROWS, THIRD), [first, second], 24 << 20)
    mine, m = lax.optimization_barrier((mine, m))
    other = swap(mine)
    upd = call(
        update_kernel, f32(ROWS, RHS), [SMEM] + [VMEM] * 4, VMEM, canonical, 4 << 20
    )(meta, mine2, other2, *m)
    r0, send = call(
        top_resid_kernel, (vec, send_shape), [SMEM] + [VMEM] * 6, (VMEM, VMEM), canonical
    )(meta, right_side, upd, mine, other, *m)
    mine, other = gather(send)
    y0, part = call(
        top_kernel, (vec, part_shape), [SMEM] + [VMEM] * 5, (VMEM, VMEM), canonical
    )(meta, r0, mine, other, *m)

    def adds(level, *terms):
        return call(
            functools.partial(add_kernel, level),
            (vec, part_shape),
            [SMEM] + [VMEM] * (len(terms) + 2),
            (VMEM, VMEM),
        )(meta, *terms, *m)

    def subs(level, y, got):
        return call(
            functools.partial(sub_kernel, level),
            (vec, part_shape),
            [SMEM] + [VMEM] * 4,
            (VMEM, VMEM),
        )(meta, y, got, *m)

    x0, part = adds(1, y0, reduce(part))
    t1, part = subs(1, y1, reduce(part))
    x01, part = adds(2, t1, x0, reduce(part))
    t2, part = subs(2, y2, reduce(part))
    return call(last_kernel, vec, [SMEM] + [VMEM] * 3, VMEM)(meta, t2, x01, reduce(part))


def solution(mesh):
    fine = Mesh(mesh.devices.reshape(4, 8, 2, 4), ("x", "z", "c", "y"))
    rows = ("x", "z", "c")
    in_specs = (P(rows, "y"), P(rows, None), P(rows), P("y", rows))
    out_specs = P("y", rows)
    return jax.shard_map(shards, mesh=fine, in_specs=in_specs, out_specs=out_specs, check_vma=False)
```
